32 devices in a mesh: dp: 8 (over z, core), mp: 4 (over y, x).
Axes of the slice: x: 2, y: 2, z: 4, core: 2. Of those that a mesh axis runs over, the one named last changes fastest.
Arguments:
- activations: bfloat16 [8, 1024, 4096], P('dp'), may hold values from -6 to 6
- out_grads: bfloat16 [8, 1024, 8192], P('dp', None, 'mp'), may hold values from -0.1875 to 0.1875
- error_fb: bfloat16 [8, 4096, 8192], P('dp', None, 'mp'), may hold values from -6 to 6
- q_prev: float32 [8192, 128], P('mp'), may hold values from -0.0625 to 0.0625
Outputs:
- new_error: bfloat16 [8, 4096, 8192], P('dp', None, 'mp')
- q_new: float32 [8192, 128], P('mp')
The draws below stay inside these ranges and needn't reach their ends.
All inputs are finite; a program needn't handle non-finite values.
Results may differ from the reference program's by a relative error of at most 0.001.
Values sent between devices are 32-bit elements; how exact they have to be, the bound alone decides.
No kernel may reach another device: no remote copies, remote signals or barrier semaphores. Data moves between devices by JAX's collectives and lax.ppermute only.
A program may use at most 128 MiB of HBM per device.

```python
import jax
import jax.numpy as jnp
from jax import lax

D = 8192
ROWS = 4096
RANK = 128
TOK_DEV = 1024
REPLICAS = 8


def block_scale(rng, dims, shards, smallest, top_value):
    level, own = 1.0, jax.random.fold_in(rng, 6)
    for position, parts in shards:
        draws = jnp.exp(jax.random.uniform(jax.random.fold_in(own, position), (parts,), jnp.float32, smallest / len(shards), top_value / len(shards)))
        level = level * jnp.repeat(draws, dims[position] // parts).reshape([-1 if axis == position else 1 for axis in range(len(dims))])
    return level


def centred(own_key, shape, width, bound, shards=(), held_as=jnp.bfloat16):
    entries = width * jax.random.normal(own_key, shape, jnp.float32)
    if shards:
        entries = entries * block_scale(own_key, shape, shards, -0.22, 0.18)
    return jnp.clip(entries, -bound, bound).astype(held_as)


def setup_inputs(seed: int = 0) -> dict:
    splits = jax.random.split(jax.random.key(seed), 5)
    return {
        "activations": centred(splits[0], (REPLICAS, TOK_DEV, ROWS), 1.0, 6.0, ((0, 8),)),
        "out_grads": centred(splits[1], (REPLICAS, TOK_DEV, D), TOK_DEV ** -0.5, 0.1875, ((0, 8), (2, 4))),
        "error_fb": centred(splits[2], (REPLICAS, ROWS, D), 1.0, 6.0, ((0, 8), (2, 4))),
        "q_prev": centred(splits[3], (D, RANK), D ** -0.5, 0.0625, ((0, 4),), jnp.float32),
    }


def merge_one(act_r, grad_r, err_r):
    grad_full = lax.dot_general(act_r.astype(jnp.float32), grad_r.astype(jnp.float32), (((0,), (0,)), ((), ())), preferred_element_type=jnp.float32)
    return grad_full + err_r.astype(jnp.float32)

def reference(activations, out_grads, error_fb, q_prev):

    def step_fn(carry, items):
        merged = merge_one(items[0], items[1], items[2])
        term = jnp.dot(merged, q_prev, precision=lax.Precision.HIGHEST)
        return (carry + term, merged)
    p_init = jnp.zeros((ROWS, RANK), jnp.float32)
    p_sum, merged_all = lax.scan(step_fn, p_init, (activations, out_grads, error_fb))
    gram = jnp.dot(p_sum.T, p_sum, precision=lax.Precision.HIGHEST)
    chol = jnp.linalg.cholesky(gram)
    p_hat = lax.linalg.triangular_solve(chol, p_sum, left_side=False, lower=True, transpose_a=True)

    def q_fn(carry, merged):
        term = lax.dot_general(merged, p_hat, (((0,), (0,)), ((), ())), precision=lax.Precision.HIGHEST)
        return (carry + term, None)
    q_sum, unused = lax.scan(q_fn, jnp.zeros((D, RANK), jnp.float32), merged_all)
    q_new = q_sum / REPLICAS
    approx = jnp.dot(p_hat, q_new.T, precision=lax.Precision.HIGHEST)
    new_error = (merged_all - approx[None]).astype(jnp.bfloat16)
    return (new_error, q_new)
```

```python
import functools

import jax
import jax.numpy as jnp
from jax import lax
from jax.experimental import pallas as pl
from jax.experimental.pallas import tpu as pltpu
from jax.sharding import PartitionSpec as P

F32 = jnp.float32
BF16 = jnp.bfloat16
HIGHEST = lax.Precision.HIGHEST
RANK = 128
VMEM_LIMIT = 50 * 1024 * 1024


def params(limit=VMEM_LIMIT):
    return pltpu.CompilerParams(vmem_limit_bytes=limit)


def cost(flops, nbytes):
    return pl.CostEstimate(flops=flops, bytes_accessed=nbytes, transcendentals=0)


def split(x):
    hi = x.astype(BF16)
    lo = (x - hi.astype(F32)).astype(BF16)
    return jnp.concatenate([hi, lo], axis=1)


def split_rows(x):
    hi = x.astype(BF16)
    lo = (x - hi.astype(F32)).astype(BF16)
    return jnp.concatenate([hi, lo], axis=0)


def halves(y):
    return y[:, :RANK] + y[:, RANK:]


def dot(a, b, contract=((1,), (0,))):
    return lax.dot_general(a, b, (contract, ((), ())), preferred_element_type=F32)


def u_kernel(g_ref, q_ref, ucat_ref, qcat_ref):
    @pl.when(pl.program_id(0) == 0)
    def _():
        qcat_ref[...] = split(q_ref[...])

    ucat_ref[...] = split(halves(dot(g_ref[...], qcat_ref[...])))


def grads_by_q(g, q):
    tok, cols = g.shape
    tile = tok // 4
    return pl.pallas_call(
        u_kernel,
        grid=(tok // tile,),
        in_specs=[
            pl.BlockSpec((tile, cols), lambda i: (i, 0)),
            pl.BlockSpec((cols, RANK), lambda i: (0, 0)),
        ],
        out_specs=[
            pl.BlockSpec((tile, 2 * RANK), lambda i: (i, 0)),
            pl.BlockSpec((cols, 2 * RANK), lambda i: (0, 0)),
        ],
        out_shape=[
            jax.ShapeDtypeStruct((tok, 2 * RANK), BF16),
            jax.ShapeDtypeStruct((cols, 2 * RANK), BF16),
        ],
        compiler_params=params(),
        cost_estimate=cost(4 * tok * cols * RANK, tok * cols * 2 + cols * RANK * 8),
        name="grads_by_q",
    )(g, q)


def p_kernel(nz, ids_ref, a_ref, e_ref, ucat_ref, qcat_ref, p_ref, acc_ref):
    acc = dot(e_ref[...], qcat_ref[...])
    acc += dot(a_ref[...], ucat_ref[...], ((0,), (0,)))
    acc_ref[...] = halves(acc)
    rows = p_ref.shape[2]
    for k in range(nz):
        start = pl.multiple_of((ids_ref[2] ^ k) * rows, rows)
        p_ref[0, k] = acc_ref[pl.ds(start, rows), :]


def left_terms(ids, a, e, ucat, qcat, kc, nm, nz):
    tok, rows = a.shape
    cols = e.shape[1]
    tile = rows // (2 * nm)

    def block(j, ids_ref):
        return (ids_ref[0] ^ kc) * nm + (ids_ref[1] ^ j)

    return pl.pallas_call(
        functools.partial(p_kernel, nz),
        grid_spec=pltpu.PrefetchScalarGridSpec(
            num_scalar_prefetch=1,
            grid=(nm,),
            in_specs=[
                pl.BlockSpec((tok, tile), lambda j, ids_ref: (0, block(j, ids_ref))),
                pl.BlockSpec((tile, cols), lambda j, ids_ref: (block(j, ids_ref), 0)),
                pl.BlockSpec((tok, 2 * RANK), lambda j, ids_ref: (0, 0)),
                pl.BlockSpec((cols, 2 * RANK), lambda j, ids_ref: (0, 0)),
            ],
            out_specs=pl.BlockSpec((1, nz, tile // nz, RANK), lambda j, ids_ref: (j, 0, 0, 0)),
            scratch_shapes=[pltpu.VMEM((tile, RANK), F32)],
        ),
        out_shape=jax.ShapeDtypeStruct((nm, nz, tile // nz, RANK), F32),
        compiler_params=params(),
        cost_estimate=cost(2 * rows * RANK * (tok + cols), rows * (tok + cols)),
        name="left_terms",
    )(ids, a, e, ucat, qcat)


def merged_kernel(first, *refs):
    a_ref, e_ref, g_ref, out_ref = refs if first else refs[1:]
    out_ref[...] = dot(a_ref[...], g_ref[...], ((0,), (0,))) + e_ref[...].astype(F32)


def merged_part(buf, a, e, g, part, parts):
    tok, rows = a.shape
    cols = e.shape[1]
    tile = rows // 8
    steps = rows // tile // parts
    first = buf is None
    specs = [
        pl.BlockSpec((tok, tile), lambda i: (0, part * steps + i)),
        pl.BlockSpec((tile, cols), lambda i: (part * steps + i, 0)),
        pl.BlockSpec((tok, cols), lambda i: (0, 0)),
    ]
    args = [a, e, g]
    if not first:
        specs = [pl.BlockSpec(memory_space=pl.ANY)] + specs
        args = [buf] + args
    return pl.pallas_call(
        functools.partial(merged_kernel, first),
        grid=(steps,),
        in_specs=specs,
        out_specs=pl.BlockSpec((tile, cols), lambda i: (part * steps + i, 0)),
        out_shape=jax.ShapeDtypeStruct((rows, cols), F32),
        input_output_aliases={} if first else {0: 0},
        compiler_params=params(),
        cost_estimate=cost(
            2 * tok * cols * rows // parts, (rows * cols * 6 + rows * tok * 2) // parts + tok * cols * 2
        ),
        name="merged",
    )(*args)


def q_kernel(nm, nz, last, ids_ref, *refs):
    pieces, refs = refs[:nm], refs[nm:]
    if last:
        v_in, q_in, a_ref, e_ref, g_ref, q_ref, pcat, pt, v_acc, q_acc = refs
    else:
        a_ref, e_ref, v_ref, q_ref, pcat, pt, v_acc, q_acc = refs
    j = pl.program_id(0)
    rows = pieces[0].shape[1]

    @pl.when(j == 0)
    def _():
        if last:
            v_acc[...] = v_in[...]
            q_acc[...] = q_in[...]
        else:
            v_acc[...] = jnp.zeros_like(v_acc)
            q_acc[...] = jnp.zeros_like(q_acc)

    for m in range(nm):

        @pl.when(j == m)
        def _():
            for k in range(nz):
                start = pl.multiple_of((ids_ref[2] ^ k) * rows, rows)
                pcat[pl.ds(start, rows), :] = split(pieces[m][k])

    v_acc[...] += halves(dot(a_ref[...], pcat[...]))
    both = dot(pcat[...], e_ref[...], ((0,), (0,)))
    q_acc[...] += both[:RANK] + both[RANK:]

    @pl.when(j == nm - 1)
    def _():
        if last:
            more = dot(split(v_acc[...]), g_ref[...], ((0,), (0,)))
            q_ref[...] = q_acc[...] + (more[:RANK] + more[RANK:])
        else:
            v_ref[...] = v_acc[...]
            q_ref[...] = q_acc[...]


def right_terms(ids, pieces, a, e, g, kc, before=None):
    tok, rows = a.shape
    cols = e.shape[1]
    nm = len(pieces)
    nz, small = pieces[0].shape[:2]
    tile = rows // (2 * nm)
    last = before is not None

    def block(j, ids_ref):
        return (ids_ref[0] ^ kc) * nm + (ids_ref[1] ^ j)

    whole = lambda *shape: pl.BlockSpec(shape, lambda j, ids_ref: (0,) * len(shape))
    specs = [whole(nz, small, RANK)] * nm
    args = list(pieces)
    if last:
        specs += [whole(tok, RANK), whole(RANK, cols)]
        args += list(before)
    specs += [
        pl.BlockSpec((tok, tile), lambda j, ids_ref: (0, block(j, ids_ref))),
        pl.BlockSpec((tile, cols), lambda j, ids_ref: (block(j, ids_ref), 0)),
    ]
    args += [a, e]
    if last:
        specs += [whole(tok, cols)]
        args += [g]
        out_specs = whole(RANK, cols)
        out_shape = jax.ShapeDtypeStruct((RANK, cols), F32)
    else:
        out_specs = [whole(tok, RANK), whole(RANK, cols)]
        out_shape = [jax.ShapeDtypeStruct((tok, RANK), F32), jax.ShapeDtypeStruct((RANK, cols), F32)]
    return pl.pallas_call(
        functools.partial(q_kernel, nm, nz, last),
        grid_spec=pltpu.PrefetchScalarGridSpec(
            num_scalar_prefetch=1,
            grid=(nm,),
            in_specs=specs,
            out_specs=out_specs,
            scratch_shapes=[
                pltpu.VMEM((tile, 2 * RANK), BF16),
                pltpu.VMEM((8, RANK), F32),
                pltpu.VMEM((tok, RANK), F32),
                pltpu.VMEM((RANK, cols), F32),
            ],
        ),
        out_shape=out_shape,
        compiler_params=params(),
        cost_estimate=cost(2 * rows * RANK * (tok + cols), rows * (tok + cols)),
        name="right_terms",
    )(ids, *args)


def p_hat_kernel(nm, nz, ids_ref, *refs):
    pieces, (linv_ref, out_ref) = refs[: 2 * nm], refs[2 * nm :]
    small = pieces[0].shape[1]
    for h in range(2):
        for m in range(nm):
            for k in range(nz):
                block = ((ids_ref[0] ^ h) * nm + (ids_ref[1] ^ m)) * nz + (ids_ref[2] ^ k)
                tile = lax.dot_general(
                    pieces[h * nm + m][k], linv_ref[...], (((1,), (1,)), ((), ())), precision=HIGHEST,
                    preferred_element_type=F32,
                )
                out_ref[pl.ds(pl.multiple_of(block * small, small), small), :] = split(tile)


def left_factor(ids, pieces, linv):
    nm = len(pieces) // 2
    nz, small = pieces[0].shape[:2]
    rows = 2 * nm * nz * small
    return pl.pallas_call(
        functools.partial(p_hat_kernel, nm, nz),
        grid_spec=pltpu.PrefetchScalarGridSpec(
            num_scalar_prefetch=1,
            grid=(),
            in_specs=[pl.BlockSpec(memory_space=pltpu.VMEM)] * (2 * nm + 1),
            out_specs=pl.BlockSpec(memory_space=pltpu.VMEM),
        ),
        out_shape=jax.ShapeDtypeStruct((rows, 2 * RANK), BF16),
        compiler_params=params(),
        cost_estimate=cost(12 * rows * RANK * RANK, rows * RANK * 8),
        name="left_factor",
    )(ids, *pieces, linv)


def final_kernel(nz, scale, ids_ref, *refs):
    pieces, (linv_ref, phat_ref, merged_ref, err_ref, qnew_ref, q_sum, q_hi, q_lo) = (
        refs[: 2 * nz],
        refs[2 * nz :],
    )
    small = pieces[0].shape[0]

    @pl.when(pl.program_id(0) == 0)
    def _():
        for h in range(2):
            for k in range(nz):
                block = (ids_ref[0] ^ h) * nz + (ids_ref[2] ^ k)
                q_sum[pl.ds(pl.multiple_of(block * small, small), small), :] = pieces[h * nz + k][...]
        q_t = lax.dot_general(
            linv_ref[...], q_sum[...], (((1,), (0,)), ((), ())), precision=HIGHEST, preferred_element_type=F32
        ) * scale
        qnew_ref[...] = q_t.T
        hi = q_t.astype(BF16)
        lo = (q_t - hi.astype(F32)).astype(BF16)
        q_hi[...] = jnp.concatenate([hi, hi], axis=0)
        q_lo[...] = jnp.concatenate([lo, lo], axis=0)

    approx = dot(phat_ref[...], q_hi[...]) + dot(phat_ref[...], q_lo[...])
    err_ref[0] = (merged_ref[...] - approx).astype(BF16)


def finish(ids, pieces, linv, phat, merged, replicas):
    nz = len(pieces) // 2
    rows, cols = merged.shape
    tile = rows // 8
    whole = lambda *shape: pl.BlockSpec(shape, lambda j, ids_ref: (0,) * len(shape))
    return pl.pallas_call(
        functools.partial(final_kernel, nz, 1.0 / replicas),
        grid_spec=pltpu.PrefetchScalarGridSpec(
            num_scalar_prefetch=1,
            grid=(rows // tile,),
            in_specs=[whole(*pieces[0].shape)] * (2 * nz)
            + [
                whole(RANK, RANK),
                pl.BlockSpec((tile, 2 * RANK), lambda j, ids_ref: (j, 0)),
                pl.BlockSpec((tile, cols), lambda j, ids_ref: (j, 0)),
            ],
            out_specs=[
                pl.BlockSpec((1, tile, cols), lambda j, ids_ref: (0, j, 0)),
                whole(cols, RANK),
            ],
            scratch_shapes=[
                pltpu.VMEM((RANK, cols), F32),
                pltpu.VMEM((2 * RANK, cols), BF16),
                pltpu.VMEM((2 * RANK, cols), BF16),
            ],
        ),
        out_shape=[jax.ShapeDtypeStruct((1, rows, cols), BF16), jax.ShapeDtypeStruct((cols, RANK), F32)],
        compiler_params=params(),
        cost_estimate=cost(8 * rows * cols * RANK, rows * cols * 6),
        name="new_error",
    )(ids, *pieces, linv, phat, merged)


def per_device(n_dp, n_mp, activations, out_grads, error_fb, q_prev):
    a, g, e = activations[0], out_grads[0], error_fb[0]
    nz = n_dp // 2
    dp, mp = lax.axis_index("dp"), lax.axis_index("mp")
    ids = jnp.stack([dp % 2, mp, dp // 2]).astype(jnp.int32)

    def to_core(x):
        return lax.ppermute(x, "dp", [(i, i ^ 1) for i in range(n_dp)])

    def to_z(x, k):
        return lax.ppermute(x, "dp", [(i, i ^ (2 * k)) for i in range(n_dp)])

    def to_mp(x, k):
        return lax.ppermute(x, "mp", [(i, i ^ k) for i in range(n_mp)])

    ucat, qcat = grads_by_q(g, q_prev)
    p_far = left_terms(ids, a, e, ucat, qcat, 1, n_mp, nz)
    p_arrived = to_core(p_far)
    p_near = left_terms(ids, a, e, ucat, qcat, 0, n_mp, nz)
    p1 = p_near + p_arrived
    p2 = p1[0] + sum(to_mp(p1[k], k) for k in range(1, n_mp))
    p3 = p2[0] + sum(to_z(p2[k], k) for k in range(1, nz))
    p4 = jnp.stack([p3] + [to_z(p3, k) for k in range(1, nz)])
    near = [p4] + [to_mp(p4, k) for k in range(1, n_mp)]
    far = [to_core(x) for x in near]

    merged = None
    for part in range(4):
        merged = merged_part(merged, a, e, g, part, 4)

    half = right_terms(ids, near, a, e, g, 0)
    q_local = right_terms(ids, far, a, e, g, 1, half)

    small = RANK // (2 * nz)
    c = dp % 2
    z = dp // 2
    q_blocks = q_local.reshape(2, nz, small, q_local.shape[1])
    q_mine = lax.dynamic_index_in_dim(q_blocks, c, 0, keepdims=False)
    q_far = lax.dynamic_index_in_dim(q_blocks, c ^ 1, 0, keepdims=False)
    q1 = q_mine + to_core(q_far)
    take = lambda k: lax.dynamic_index_in_dim(q1, z ^ k, 0, keepdims=False)
    q3 = take(0) + sum(to_z(take(k), k) for k in range(1, nz))
    q_near = [q3] + [to_z(q3, k) for k in range(1, nz)]
    q_pieces = q_near + [to_core(x) for x in q_near]

    p_all = jnp.concatenate([x.reshape(-1, RANK) for x in near + far])
    gram = lax.dot_general(p_all, p_all, (((0,), (0,)), ((), ())), precision=HIGHEST)
    chol = jnp.linalg.cholesky(gram)
    linv = lax.linalg.triangular_solve(chol, jnp.eye(RANK, dtype=F32), left_side=True, lower=True)
    phat = left_factor(ids, near + far, linv)
    new_error, q_new = finish(ids, q_pieces, linv, phat, merged, n_dp)
    return new_error, q_new


def solution(mesh):
    placed = (P("dp", None, None), P("dp", None, "mp"), P("dp", None, "mp"), P("mp", None))
    return jax.shard_map(
        functools.partial(per_device, mesh.shape["dp"], mesh.shape["mp"]),
        mesh=mesh,
        in_specs=placed,
        out_specs=(P("dp", None, "mp"), P("mp", None)),
        check_vma=False,
    )
```

```python
import functools

import jax
import jax.numpy as jnp
from jax import lax
from jax.experimental import pallas as pl
from jax.experimental.pallas import tpu as pltpu
from jax.sharding import PartitionSpec as P

F32 = jnp.float32
BF16 = jnp.bfloat16
HIGHEST = lax.Precision.HIGHEST
RANK = 128
VMEM_LIMIT = 50 * 1024 * 1024
SMALL_LIMIT = 6 * 1024 * 1024
MERGED_LIMIT = 8 * 1024 * 1024
RIGHT_LIMIT = 11 * 1024 * 1024
FINAL_LIMIT = 9 * 1024 * 1024


def params(limit=VMEM_LIMIT):
    return pltpu.CompilerParams(vmem_limit_bytes=limit)


def cost(flops, nbytes):
    return pl.CostEstimate(flops=flops, bytes_accessed=nbytes, transcendentals=0)


def split_rows(x):
    hi = x.astype(BF16)
    lo = (x - hi.astype(F32)).astype(BF16)
    return jnp.concatenate([hi, lo], axis=0)


def fold(y):
    return y[:RANK] + y[RANK:]


def dot(a, b, contract=((1,), (0,))):
    return lax.dot_general(a, b, (contract, ((), ())), preferred_element_type=F32)


ROWS_BY_ROWS = ((1,), (1,))


def skipping(count, body, *refs):
    body(*refs[count:])


def in_vmem(body, outs, args, name, limit=SMALL_LIMIT, work=None, after=()):
    args = [*after, *args]
    return pl.pallas_call(
        functools.partial(skipping, len(after), body),
        in_specs=[pl.BlockSpec(memory_space=pl.ANY)] * len(after)
        + [pl.BlockSpec(memory_space=pltpu.VMEM)] * (len(args) - len(after)),
        out_specs=[pl.BlockSpec(memory_space=pltpu.VMEM)] * len(outs),
        out_shape=[jax.ShapeDtypeStruct(*out) for out in outs],
        compiler_params=params(limit),
        cost_estimate=work,
        name=name,
    )(*args)


def u_kernel(g_ref, q_ref, ucat_ref, qcat_ref):
    @pl.when(pl.program_id(0) == 0)
    def _():
        qcat_ref[...] = split_rows(q_ref[...].T)

    ucat_ref[...] = split_rows(fold(dot(qcat_ref[...], g_ref[...], ROWS_BY_ROWS)))


def grads_by_q(g, q):
    tok, cols = g.shape
    tile = tok // 2
    return pl.pallas_call(
        u_kernel,
        grid=(tok // tile,),
        in_specs=[
            pl.BlockSpec((tile, cols), lambda i: (i, 0)),
            pl.BlockSpec((cols, RANK), lambda i: (0, 0)),
        ],
        out_specs=[
            pl.BlockSpec((2 * RANK, tile), lambda i: (0, i)),
            pl.BlockSpec((2 * RANK, cols), lambda i: (0, 0)),
        ],
        out_shape=[
            jax.ShapeDtypeStruct((2 * RANK, tok), BF16),
            jax.ShapeDtypeStruct((2 * RANK, cols), BF16),
        ],
        compiler_params=params(),
        cost_estimate=cost(4 * tok * cols * RANK, tok * cols * 2 + cols * RANK * 8),
        name="grads_by_q",
    )(g, q)


def p_kernel(nz, ids_ref, a_ref, e_ref, ucat_ref, qcat_ref, p_ref, acc_ref):
    acc = dot(qcat_ref[...], e_ref[...], ROWS_BY_ROWS) + dot(ucat_ref[...], a_ref[...])
    acc_ref[...] = fold(acc).T
    rows = p_ref.shape[2]
    for k in range(nz):
        start = pl.multiple_of((ids_ref[2] ^ k) * rows, rows)
        p_ref[0, k] = acc_ref[pl.ds(start, rows), :]


def left_terms(ids, a, e, ucat, qcat, kc, nm, nz):
    tok, rows = a.shape
    cols = e.shape[1]
    tile = rows // (2 * nm)

    def block(j, ids_ref):
        return (ids_ref[0] ^ kc) * nm + (ids_ref[1] ^ j)

    return pl.pallas_call(
        functools.partial(p_kernel, nz),
        grid_spec=pltpu.PrefetchScalarGridSpec(
            num_scalar_prefetch=1,
            grid=(nm,),
            in_specs=[
                pl.BlockSpec((tok, tile), lambda j, ids_ref: (0, block(j, ids_ref))),
                pl.BlockSpec((tile, cols), lambda j, ids_ref: (block(j, ids_ref), 0)),
                pl.BlockSpec((2 * RANK, tok), lambda j, ids_ref: (0, 0)),
                pl.BlockSpec((2 * RANK, cols), lambda j, ids_ref: (0, 0)),
            ],
            out_specs=pl.BlockSpec((1, nz, tile // nz, RANK), lambda j, ids_ref: (j, 0, 0, 0)),
            scratch_shapes=[pltpu.VMEM((tile, RANK), F32)],
        ),
        out_shape=jax.ShapeDtypeStruct((nm, nz, tile // nz, RANK), F32),
        compiler_params=params(),
        cost_estimate=cost(2 * rows * RANK * (tok + cols), rows * (tok + cols)),
        name="left_terms",
    )(ids, a, e, ucat, qcat)


def first_sum_kernel(keeps, sends, near_ref, far_ref, *outs):
    rows = near_ref.shape[2] // 2
    for half in range(2):
        for out, members in ((outs[2 * half], sends[half]), (outs[2 * half + 1], keeps[half])):
            for i, km in enumerate(members):
                at = (km, slice(None), pl.ds(half * rows, rows))
                out[i] = near_ref[at] + far_ref[at]


def next_sum_kernel(keeps, sends, *refs):
    ins, outs = refs[:4], refs[4:]
    for half in range(2):
        kept, came = ins[2 * half : 2 * half + 2]
        for out, places in ((outs[2 * half], sends[half]), (outs[2 * half + 1], keeps[half])):
            for i, at in enumerate(places):
                out[i] = kept[at] + came[at]


def last_sum_kernel(nz, *refs):
    ins, outs = refs[:4], refs[4:]
    rows = ins[0].shape[2]
    for k in range(nz):
        for half in range(2):
            outs[k][pl.ds(half * rows, rows), :] = ins[2 * half][0, k] + ins[2 * half + 1][0, k]


def scatter_over_mp(near, far, to_mp, orders, beside):
    nm, nz, block, _ = near.shape
    rows = block // 2
    members = [list(range(nm))] * 2
    values, done = None, ()
    for step in range(len(orders[0])):
        bits = [1 << order[step] for order in orders]
        keep_lists = [[km for km in members[h] if not km & bits[h]] for h in range(2)]
        send_lists = [[km | bits[h] for km in keep_lists[h]] for h in range(2)]
        count = len(keep_lists[0])
        outs = [((count, nz, rows, RANK), F32)] * 4
        if values is None:
            parts = in_vmem(functools.partial(first_sum_kernel, keep_lists, send_lists), outs, [near, far], "first_sum")
        else:
            keep_at = [[members[h].index(km) for km in keep_lists[h]] for h in range(2)]
            send_at = [[members[h].index(km) for km in send_lists[h]] for h in range(2)]
            parts = in_vmem(functools.partial(next_sum_kernel, keep_at, send_at), outs, values, "next_sum", after=done)
            done = ()
        members = keep_lists
        came = [to_mp(parts[0], bits[0]), to_mp(parts[2], bits[1])]
        if step == 0:
            done = [beside(parts[1])]
        values = [parts[1], came[0], parts[3], came[1]]
    return in_vmem(functools.partial(last_sum_kernel, nz), [((block, RANK), F32)] * nz, values, "last_sum", after=done)


def own_sum_kernel(*refs):
    ins, out = refs[:-1], refs[-1]
    total = ins[0][...]
    for came in ins[1:]:
        total = total + came[...]
    out[...] = total


def own_kernel(nz, *refs):
    ins, outs = refs[:nz], refs[nz:]
    rows = outs[0].shape[2]
    for k in range(nz):
        for half in range(2):
            outs[half][0, k] = ins[k][pl.ds(half * rows, rows), :]


def grow_kernel(*refs):
    ins, outs = refs[:4], refs[4:]
    count = ins[0].shape[0]
    for half in range(2):
        outs[half][pl.ds(0, count)] = ins[2 * half][...]
        outs[half][pl.ds(count, count)] = ins[2 * half + 1][...]


def gather_over_mp(pieces, to_mp, orders, done):
    nz = len(pieces)
    rows = pieces[0].shape[0] // 2
    held = in_vmem(functools.partial(own_kernel, nz), [((1, nz, rows, RANK), F32)] * 2, pieces, "own_rows", after=done)
    members = [[0], [0]]
    last = len(orders[0]) - 1
    for step in range(last, -1, -1):
        bits = [1 << order[step] for order in orders]
        came = [to_mp(held[h], bits[h]) for h in range(2)]
        came_members = [[km ^ bits[h] for km in members[h]] for h in range(2)]
        if step == 0:
            return [held[0], held[1], came[0], came[1]], [
                (0, members[0]), (1, members[1]), (0, came_members[0]), (1, came_members[1])
            ]
        count = len(members[0])
        held = in_vmem(
            grow_kernel, [((2 * count, nz, rows, RANK), F32)] * 2, [held[0], came[0], held[1], came[1]], "grow"
        )
        members = [members[h] + came_members[h] for h in range(2)]


def merged_kernel(part, after_ref, a_ref, e_ref, g_ref, out_ref):
    tok, cols = g_ref.shape
    rows = out_ref.shape[0]
    tile = rows // 4

    def body(a_tile, e_tile):
        start = pl.multiple_of(pl.program_id(0) * tile, tile)
        out_ref[pl.ds(start, tile), :] = dot(a_tile[...], g_ref[...], ((0,), (0,))) + e_tile[...].astype(F32)

    pltpu.emit_pipeline(
        body,
        grid=(4,),
        in_specs=[
            pl.BlockSpec((tok, tile), lambda i: (0, part * 4 + i)),
            pl.BlockSpec((tile, cols), lambda i: (part * 4 + i, 0)),
        ],
    )(a_ref, e_ref)


def merged_part(a, e, g, part, parts, after):
    tok, rows = a.shape
    cols = e.shape[1]
    return pl.pallas_call(
        functools.partial(merged_kernel, part),
        in_specs=[pl.BlockSpec(memory_space=pl.ANY)]
        + [pl.BlockSpec(memory_space=pltpu.HBM)] * 2
        + [pl.BlockSpec(memory_space=pltpu.VMEM)],
        out_specs=pl.BlockSpec(memory_space=pltpu.VMEM),
        out_shape=pltpu.VMEM((rows // parts, cols), F32),
        compiler_params=params(MERGED_LIMIT),
        cost_estimate=cost(2 * tok * cols * rows // parts, (rows * cols * 2 + rows * tok * 2) // parts),
        name="merged",
    )(after, a, e, g)


def q_kernel(owners, kc, nm, nz, last, ids_ref, *refs):
    pieces, refs = refs[:4], refs[4:]
    if last:
        v_in, q_in, gram_in, a_ref, e_ref, g_ref, send_ref, keep_ref, gram_ref, p_half, v_acc, q_acc, gram_acc = refs
        v_acc[...], q_acc[...], gram_acc[...] = v_in[...], q_in[...], gram_in[...]
    else:
        a_ref, e_ref, v_acc, q_acc, gram_acc, p_half = refs
        for acc in (v_acc, q_acc, gram_acc):
            acc[...] = jnp.zeros_like(acc)
    rows = pieces[0].shape[2]
    tok, cols = a_ref.shape[0], e_ref.shape[1]
    tile = p_half.shape[0] // nm
    for piece, (half, members) in zip(pieces, owners):
        for i, km in enumerate(members):
            for k in range(nz):
                start = ((ids_ref[1] ^ km) * nz + (ids_ref[2] ^ k)) * (2 * rows) + half * rows
                p_half[pl.ds(pl.multiple_of(start, rows), rows), :] = piece[i, k]
    first = (ids_ref[0] ^ kc) * nm

    def body(a_tile, e_tile):
        start = pl.multiple_of(pl.program_id(0) * tile, tile)
        pcat = split_rows(p_half[pl.ds(start, tile), :].T)
        v_acc[...] += fold(dot(pcat, a_tile[...], ROWS_BY_ROWS))
        q_acc[...] += fold(dot(pcat, e_tile[...]))
        gram_acc[...] += dot(pcat, pcat, ROWS_BY_ROWS)

    pltpu.emit_pipeline(
        body,
        grid=(nm,),
        in_specs=[
            pl.BlockSpec((tok, tile), lambda j: (0, first + j)),
            pl.BlockSpec((tile, cols), lambda j: (first + j, 0)),
        ],
    )(a_ref, e_ref)

    if last:
        q_acc[...] += fold(dot(split_rows(v_acc[...]), g_ref[...]))
        whole = fold(gram_acc[...])
        gram_ref[...] = whole[:, :RANK] + whole[:, RANK:]
        small = send_ref.shape[1]
        for out, flip in ((send_ref, 1), (keep_ref, 0)):
            for k in range(nz):
                start = ((ids_ref[0] ^ flip) * nz + (ids_ref[2] ^ k)) * small
                out[k] = q_acc[pl.ds(pl.multiple_of(start, small), small), :]


def right_terms(ids, pieces, owners, a, e, g, kc, nm, before=None):
    tok, rows = a.shape
    cols = e.shape[1]
    nz = pieces[0].shape[1]
    last = before is not None
    vmem = pl.BlockSpec(memory_space=pltpu.VMEM)
    hbm = pl.BlockSpec(memory_space=pltpu.HBM)
    sums = [(RANK, tok), (RANK, cols), (2 * RANK, 2 * RANK)]
    scratch = [pltpu.VMEM((rows // 2, RANK), F32)]
    if last:
        specs = [vmem] * 7 + [hbm] * 2 + [vmem]
        args = [*pieces, *before, a, e, g]
        outs = [(nz, RANK // (2 * nz), cols)] * 2 + [(RANK, RANK)]
        scratch += [pltpu.VMEM(shape, F32) for shape in sums]
    else:
        specs = [vmem] * 4 + [hbm] * 2
        args = [*pieces, a, e]
        outs = sums
    return pl.pallas_call(
        functools.partial(q_kernel, owners, kc, nm, nz, last),
        grid_spec=pltpu.PrefetchScalarGridSpec(
            num_scalar_prefetch=1,
            grid=(),
            in_specs=specs,
            out_specs=[vmem] * 3,
            scratch_shapes=scratch,
        ),
        out_shape=[jax.ShapeDtypeStruct(shape, F32) for shape in outs],
        compiler_params=params(RIGHT_LIMIT),
        cost_estimate=cost(2 * rows * RANK * (tok + cols), rows * (tok + cols)),
        name="right_terms",
    )(ids, *args)


def chol_inverse_kernel(gram_ref, out_ref):
    left = gram_ref[...]
    row = lax.broadcasted_iota(jnp.int32, (RANK, RANK), 0)
    right = (row == lax.broadcasted_iota(jnp.int32, (RANK, RANK), 1)).astype(F32)
    for j in range(RANK):
        at = j % 8
        if j and at == 0:
            left, right = left[8:], right[8:]
        pivot_row, own = left[at : at + 1], right[at : at + 1]
        pivot = pivot_row[:, j : j + 1]
        out_ref[j : j + 1, :] = own * (1.0 / jnp.sqrt(pivot))
        inverse = 1.0 / pivot
        below = row[: left.shape[0], :1] > at
        factor = jnp.where(below, left[:, j : j + 1], 0.0)
        left = left - factor * (pivot_row * inverse)
        right = right - factor * (own * inverse)


def p_hat_kernel(owners, nm, nz, ids_ref, after_ref, *refs):
    pieces, (inv_ref, out_ref, p_all) = refs[:8], refs[8:]
    rows = pieces[0].shape[2]
    for h in range(2):
        for piece, (half, members) in zip(pieces[4 * h : 4 * h + 4], owners):
            for i, km in enumerate(members):
                for k in range(nz):
                    block = ((ids_ref[0] ^ h) * nm + (ids_ref[1] ^ km)) * nz + (ids_ref[2] ^ k)
                    start = block * (2 * rows) + half * rows
                    p_all[pl.ds(pl.multiple_of(start, rows), rows), :] = piece[i, k]
    inv_hi = inv_ref[...].T.astype(BF16)
    inv_lo = (inv_ref[...].T - inv_hi.astype(F32)).astype(BF16)
    inv = jnp.concatenate([inv_hi, inv_hi, inv_lo, inv_lo], axis=0)
    tile = p_all.shape[0] // 8

    @pl.loop(0, 8)
    def _(i):
        at = pl.ds(pl.multiple_of(i * tile, tile), tile)
        x = p_all[at, :]
        hi = x.astype(BF16)
        lo = (x - hi.astype(F32)).astype(BF16)
        y = dot(jnp.concatenate([hi, lo, hi, lo], axis=1), inv)
        y_hi = y.astype(BF16)
        y_lo = (y - y_hi.astype(F32)).astype(BF16)
        out_ref[at, :] = jnp.concatenate([y_hi, y_lo], axis=1)


def left_factor(ids, pieces, owners, inv, rows, nm, nz, after):
    return pl.pallas_call(
        functools.partial(p_hat_kernel, owners, nm, nz),
        grid_spec=pltpu.PrefetchScalarGridSpec(
            num_scalar_prefetch=1,
            grid=(),
            in_specs=[pl.BlockSpec(memory_space=pl.ANY)] + [pl.BlockSpec(memory_space=pltpu.VMEM)] * 9,
            out_specs=pl.BlockSpec(memory_space=pltpu.VMEM),
            scratch_shapes=[pltpu.VMEM((rows, RANK), F32)],
        ),
        out_shape=jax.ShapeDtypeStruct((rows, 2 * RANK), BF16),
        compiler_params=params(SMALL_LIMIT),
        cost_estimate=cost(8 * rows * RANK * RANK, rows * RANK * 8),
        name="left_factor",
    )(ids, after, *pieces, inv)


def final_kernel(nz, scale, tile, ids_ref, *refs):
    pieces, refs = refs[: 2 * nz], refs[2 * nz :]
    inv_ref, phat_ref, parts, (err_ref, qnew_ref, q_sum, q_cat) = refs[0], refs[1], refs[2:6], refs[6:]
    small = pieces[0].shape[0]
    for h in range(2):
        for k in range(nz):
            block = (ids_ref[0] ^ h) * nz + (ids_ref[2] ^ k)
            q_sum[pl.ds(pl.multiple_of(block * small, small), small), :] = pieces[h * nz + k][...]
    q_t = scale * lax.dot_general(
        inv_ref[...], q_sum[...], (((1,), (0,)), ((), ())), precision=HIGHEST, preferred_element_type=F32
    )
    qnew_ref[...] = q_t.T
    hi = q_t.astype(BF16)
    lo = (q_t - hi.astype(F32)).astype(BF16)
    q_cat[...] = jnp.concatenate([hi, hi, lo, lo], axis=0)
    part_rows, cols = parts[0].shape
    steps = part_rows // tile
    for number, merged in enumerate(parts):

        def body(out_tile):
            start = pl.multiple_of(pl.program_id(0) * tile, tile)
            x = phat_ref[pl.ds(pl.multiple_of(number * part_rows + start, tile), tile), :]
            approx = dot(jnp.concatenate([x, x], axis=1), q_cat[...])
            out_tile[0] = (merged[pl.ds(start, tile), :] - approx).astype(BF16)

        pltpu.emit_pipeline(
            body,
            grid=(steps,),
            in_specs=[],
            out_specs=[pl.BlockSpec((1, tile, cols), lambda i, number=number: (0, number * steps + i, 0))],
        )(err_ref)


def finish(ids, pieces, inv, phat, parts, replicas):
    nz = len(pieces) // 2
    part_rows, cols = parts[0].shape
    rows = part_rows * len(parts)
    vmem = pl.BlockSpec(memory_space=pltpu.VMEM)
    hbm = pl.BlockSpec(memory_space=pltpu.HBM)
    return pl.pallas_call(
        functools.partial(final_kernel, nz, 1.0 / replicas, rows // 16),
        grid_spec=pltpu.PrefetchScalarGridSpec(
            num_scalar_prefetch=1,
            grid=(),
            in_specs=[vmem] * (2 * nz + 1) + [vmem] + [vmem] * len(parts),
            out_specs=[hbm, vmem],
            scratch_shapes=[pltpu.VMEM((RANK, cols), F32), pltpu.VMEM((4 * RANK, cols), BF16)],
        ),
        out_shape=[jax.ShapeDtypeStruct((1, rows, cols), BF16), jax.ShapeDtypeStruct((cols, RANK), F32)],
        compiler_params=params(FINAL_LIMIT),
        cost_estimate=cost(8 * rows * cols * RANK, rows * cols * 6),
        name="new_error",
    )(ids, *pieces, inv, phat, *parts)


def q_sum_kernel(nz, *refs):
    keep, came, outs = refs[0], refs[1], refs[2:]
    for k in range(nz):
        outs[k][...] = keep[k] + came[k]


def per_device(n_dp, n_mp, activations, out_grads, error_fb, q_prev):
    a, g, e = activations[0], out_grads[0], error_fb[0]
    a_hbm = pltpu.with_memory_space_constraint(a, pltpu.HBM)
    e_hbm = pltpu.with_memory_space_constraint(e, pltpu.HBM)
    rows = a.shape[1]
    nz = n_dp // 2
    dp, mp = lax.axis_index("dp"), lax.axis_index("mp")
    ids = jnp.stack([dp % 2, mp, dp // 2]).astype(jnp.int32)
    bits = list(range(n_mp.bit_length() - 1))
    orders = [bits, bits[::-1]]

    def to_core(x):
        return lax.ppermute(x, "dp", [(i, i ^ 1) for i in range(n_dp)])

    def to_z(x, k):
        return lax.ppermute(x, "dp", [(i, i ^ (2 * k)) for i in range(n_dp)])

    def to_mp(x, k):
        return lax.ppermute(x, "mp", [(i, i ^ k) for i in range(n_mp)])

    ucat, qcat = grads_by_q(g, q_prev)
    p_far = left_terms(ids, a, e, ucat, qcat, 1, n_mp, nz)
    p_arrived = to_core(p_far)
    p_near = left_terms(ids, a, e, ucat, qcat, 0, n_mp, nz)
    parts = []

    def beside(sent):
        parts.append(merged_part(a_hbm, e_hbm, g, len(parts), 4, sent))
        return parts[-1]

    by_z = scatter_over_mp(p_near, p_arrived, to_mp, orders, beside)
    done = [beside(by_z[0])]
    came = [to_z(by_z[k], k) for k in range(1, nz)]
    [p_own] = in_vmem(own_sum_kernel, [(by_z[0].shape, F32)], [by_z[0], *came], "p_own", after=done)
    done = [beside(p_own)]
    p_pieces = [p_own] + [to_z(p_own, k) for k in range(1, nz)]
    near, owners = gather_over_mp(p_pieces, to_mp, orders, done)
    beside(near[0])
    far = [to_core(x) for x in near]

    half = right_terms(ids, near, owners, a_hbm, e_hbm, g, 0, n_mp)
    q_send, q_keep, gram = right_terms(ids, far, owners, a_hbm, e_hbm, g, 1, n_mp, half)

    piece = (q_keep.shape[1:], F32)
    q_by_z = in_vmem(functools.partial(q_sum_kernel, nz), [piece] * nz, [q_keep, to_core(q_send)], "q_sum")
    q_own = q_by_z[0] + sum(to_z(q_by_z[k], k) for k in range(1, nz))
    q_near = [q_own] + [to_z(q_own, k) for k in range(1, nz)]
    q_pieces = q_near + [to_core(x) for x in q_near]

    square = ((RANK, RANK), F32)
    [inv] = in_vmem(chol_inverse_kernel, [square], [gram], "chol_inverse", work=cost(2 * 10**10, 10**5))
    phat = left_factor(ids, near + far, owners, inv, rows, n_mp, nz, q_own)
    new_error, q_new = finish(ids, q_pieces, inv, phat, parts, n_dp)
    return new_error, q_new


def solution(mesh):
    placed = (P("dp", None, None), P("dp", None, "mp"), P("dp", None, "mp"), P("mp", None))
    return jax.shard_map(
        functools.partial(per_device, mesh.shape["dp"], mesh.shape["mp"]),
        mesh=mesh,
        in_specs=placed,
        out_specs=(P("dp", None, "mp"), P("mp", None)),
        check_vma=False,
    )
```

```python
import functools

import jax
import jax.numpy as jnp
from jax import lax
from jax.experimental import pallas as pl
from jax.experimental.pallas import tpu as pltpu
from jax.sharding import PartitionSpec as P

F32 = jnp.float32
BF16 = jnp.bfloat16
HIGHEST = lax.Precision.HIGHEST
RANK = 128
VMEM_LIMIT = 50 * 1024 * 1024
LEFT_LIMIT = 14 * 1024 * 1024
SMALL_LIMIT = 6 * 1024 * 1024
MERGED_LIMIT = 8 * 1024 * 1024
RIGHT_LIMIT = 11 * 1024 * 1024
FINAL_LIMIT = 9 * 1024 * 1024


def params(limit=VMEM_LIMIT):
    return pltpu.CompilerParams(vmem_limit_bytes=limit)


def cost(flops, nbytes):
    return pl.CostEstimate(flops=flops, bytes_accessed=nbytes, transcendentals=0)


def split_rows(x):
    hi = x.astype(BF16)
    lo = (x - hi.astype(F32)).astype(BF16)
    return jnp.concatenate([hi, lo], axis=0)


def fold(y):
    return y[:RANK] + y[RANK:]


def dot(a, b, contract=((1,), (0,))):
    return lax.dot_general(a, b, (contract, ((), ())), preferred_element_type=F32)


ROWS_BY_ROWS = ((1,), (1,))


def skipping(count, body, *refs):
    body(*refs[count:])


def in_vmem(body, outs, args, name, limit=SMALL_LIMIT, work=None, after=()):
    args = [*after, *args]
    return pl.pallas_call(
        functools.partial(skipping, len(after), body),
        in_specs=[pl.BlockSpec(memory_space=pltpu.VMEM)] * len(args),
        out_specs=[pl.BlockSpec(memory_space=pltpu.VMEM)] * len(outs),
        out_shape=[jax.ShapeDtypeStruct(*out) for out in outs],
        compiler_params=params(limit),
        cost_estimate=work,
        name=name,
    )(*args)


STEPS = 8


def copies_of_half(a_hbm, e_hbm, a_ref, e_ref, sems, half):
    rows = e_ref.shape[0]
    tile = rows // STEPS
    copies = []
    for i in range(STEPS):
        here = pl.ds(i * tile, tile)
        there = pl.ds(pl.multiple_of(half * rows + i * tile, tile), tile)
        copies.append(
            (
                pltpu.make_async_copy(e_hbm.at[there, :], e_ref.at[here, :], sems.at[2 * i]),
                pltpu.make_async_copy(a_hbm.at[:, there], a_ref.at[:, here], sems.at[2 * i + 1]),
            )
        )
    return copies


def p_of_half(ids_ref, copies, a_ref, e_ref, ucat_ref, qcat_ref, p_ref):
    nz, small = p_ref.shape[1:3]
    tile = e_ref.shape[0] // STEPS
    for i, (e_copy, a_copy) in enumerate(copies):
        here = pl.ds(i * tile, tile)
        e_copy.wait()
        acc = dot(qcat_ref[...], e_ref[here, :], ROWS_BY_ROWS)
        a_copy.wait()
        acc += dot(ucat_ref[...], a_ref[:, here])
        p_tile = fold(acc).T
        for k in range(tile // small):
            block = i * (tile // small) + k
            p_ref[(block // nz) ^ ids_ref[1], (block % nz) ^ ids_ref[2]] = p_tile[k * small : (k + 1) * small]


def far_kernel(
    ids_ref, q_hbm, g_hbm, a_hbm, e_hbm, p_ref, a_ref, e_ref, g_ref, ucat_ref, qcat_ref, q_ref, sems, first_sems
):
    tok = g_ref.shape[0]
    q_copy = pltpu.make_async_copy(q_hbm, q_ref, first_sems.at[0])
    q_copy.start()
    g_copies = []
    for i in range(2):
        at = pl.ds(i * (tok // 2), tok // 2)
        g_copies.append(pltpu.make_async_copy(g_hbm.at[at, :], g_ref.at[at, :], first_sems.at[1 + i]))
        g_copies[-1].start()
    copies = copies_of_half(a_hbm, e_hbm, a_ref, e_ref, sems, ids_ref[0] ^ 1)
    for pair in copies:
        for copy in pair:
            copy.start()
    q_copy.wait()
    qcat_ref[...] = split_rows(q_ref[...].T)
    for i in range(2):
        at = pl.ds(i * (tok // 2), tok // 2)
        g_copies[i].wait()
        ucat_ref[:, at] = split_rows(fold(dot(qcat_ref[...], g_ref[at, :], ROWS_BY_ROWS)))
    p_of_half(ids_ref, copies, a_ref, e_ref, ucat_ref, qcat_ref, p_ref)


def near_kernel(ids_ref, ucat_ref, qcat_ref, a_hbm, e_hbm, p_ref, a_ref, e_ref, sems):
    copies = copies_of_half(a_hbm, e_hbm, a_ref, e_ref, sems, ids_ref[0])
    for pair in copies:
        for copy in pair:
            copy.start()
    p_of_half(ids_ref, copies, a_ref, e_ref, ucat_ref, qcat_ref, p_ref)


def left_terms(ids, q, g, a, e, nm, nz, before=None):
    tok, rows = a.shape
    cols = e.shape[1]
    vmem = pl.BlockSpec(memory_space=pltpu.VMEM)
    hbm = pl.BlockSpec(memory_space=pltpu.HBM)
    outs = [
        pltpu.VMEM((nm, nz, rows // (2 * nm * nz), RANK), F32),
        pltpu.VMEM((tok, rows // 2), BF16),
        pltpu.VMEM((rows // 2, cols), BF16),
    ]
    scratch = [pltpu.SemaphoreType.DMA((2 * STEPS,))]
    if before is None:
        body, specs, args = far_kernel, [hbm] * 4, (q, g, a, e)
        outs += [
            pltpu.VMEM((tok, cols), BF16),
            pltpu.VMEM((2 * RANK, tok), BF16),
            pltpu.VMEM((2 * RANK, cols), BF16),
        ]
        scratch = [pltpu.VMEM((cols, RANK), F32)] + scratch + [pltpu.SemaphoreType.DMA((3,))]
    else:
        body, specs, args = near_kernel, [vmem] * 2 + [hbm] * 2, (*before, a, e)
    return pl.pallas_call(
        body,
        grid_spec=pltpu.PrefetchScalarGridSpec(
            num_scalar_prefetch=1,
            grid=(),
            in_specs=specs,
            out_specs=[vmem] * len(outs),
            scratch_shapes=scratch,
        ),
        out_shape=outs,
        compiler_params=params(LEFT_LIMIT),
        cost_estimate=cost(2 * rows * RANK * (tok + cols), rows * (tok + cols)),
        name="left_terms",
    )(ids, *args)


def first_sum_kernel(keeps, sends, near_ref, far_ref, *outs):
    rows = near_ref.shape[2] // 2
    for half in range(2):
        for out, members in ((outs[2 * half], sends[half]), (outs[2 * half + 1], keeps[half])):
            for i, km in enumerate(members):
                at = (km, slice(None), pl.ds(half * rows, rows))
                out[i] = near_ref[at] + far_ref[at]


def next_sum_kernel(keeps, sends, *refs):
    ins, outs = refs[:4], refs[4:]
    for half in range(2):
        kept, came = ins[2 * half : 2 * half + 2]
        for out, places in ((outs[2 * half], sends[half]), (outs[2 * half + 1], keeps[half])):
            for i, at in enumerate(places):
                out[i] = kept[at] + came[at]


def last_sum_kernel(nz, *refs):
    ins, outs = refs[:4], refs[4:]
    rows = ins[0].shape[2]
    for k in range(nz):
        for half in range(2):
            outs[k][pl.ds(half * rows, rows), :] = ins[2 * half][0, k] + ins[2 * half + 1][0, k]


def scatter_over_mp(near, far, to_mp, orders, beside):
    nm, nz, block, _ = near.shape
    rows = block // 2
    members = [list(range(nm))] * 2
    values, done = None, ()
    for step in range(len(orders[0])):
        bits = [1 << order[step] for order in orders]
        keep_lists = [[km for km in members[h] if not km & bits[h]] for h in range(2)]
        send_lists = [[km | bits[h] for km in keep_lists[h]] for h in range(2)]
        count = len(keep_lists[0])
        outs = [((count, nz, rows, RANK), F32)] * 4
        if values is None:
            parts = in_vmem(functools.partial(first_sum_kernel, keep_lists, send_lists), outs, [near, far], "first_sum")
        else:
            keep_at = [[members[h].index(km) for km in keep_lists[h]] for h in range(2)]
            send_at = [[members[h].index(km) for km in send_lists[h]] for h in range(2)]
            parts = in_vmem(functools.partial(next_sum_kernel, keep_at, send_at), outs, values, "next_sum", after=done)
            done = ()
        members = keep_lists
        came = [to_mp(parts[0], bits[0]), to_mp(parts[2], bits[1])]
        if step == 0:
            done = [beside(parts[1])]
        values = [parts[1], came[0], parts[3], came[1]]
    return in_vmem(functools.partial(last_sum_kernel, nz), [((block, RANK), F32)] * nz, values, "last_sum", after=done)


def own_sum_kernel(*refs):
    ins, out = refs[:-1], refs[-1]
    total = ins[0][...]
    for came in ins[1:]:
        total = total + came[...]
    out[...] = total


def own_kernel(nz, *refs):
    ins, outs = refs[:nz], refs[nz:]
    rows = outs[0].shape[2]
    for k in range(nz):
        for half in range(2):
            outs[half][0, k] = ins[k][pl.ds(half * rows, rows), :]


def grow_kernel(*refs):
    ins, outs = refs[:4], refs[4:]
    count = ins[0].shape[0]
    for half in range(2):
        outs[half][pl.ds(0, count)] = ins[2 * half][...]
        outs[half][pl.ds(count, count)] = ins[2 * half + 1][...]


def gather_over_mp(pieces, to_mp, orders, done):
    nz = len(pieces)
    rows = pieces[0].shape[0] // 2
    held = in_vmem(functools.partial(own_kernel, nz), [((1, nz, rows, RANK), F32)] * 2, pieces, "own_rows", after=done)
    members = [[0], [0]]
    last = len(orders[0]) - 1
    for step in range(last, -1, -1):
        bits = [1 << order[step] for order in orders]
        came = [to_mp(held[h], bits[h]) for h in range(2)]
        came_members = [[km ^ bits[h] for km in members[h]] for h in range(2)]
        if step == 0:
            return [held[0], held[1], came[0], came[1]], [
                (0, members[0]), (1, members[1]), (0, came_members[0]), (1, came_members[1])
            ]
        count = len(members[0])
        held = in_vmem(
            grow_kernel, [((2 * count, nz, rows, RANK), F32)] * 2, [held[0], came[0], held[1], came[1]], "grow"
        )
        members = [members[h] + came_members[h] for h in range(2)]


def merged_kernel(part, in_hbm, after_ref, a_ref, e_ref, g_ref, out_ref, done_ref, a_t):
    done_ref[...] = jnp.zeros_like(done_ref)
    rows, cols = out_ref.shape
    chunk = min(cols, 512)
    at = pl.ds(part * rows, rows)
    a_t[...] = a_ref[:, at].T

    def values(i):
        here = pl.ds(pl.multiple_of(i * chunk, chunk), chunk)
        return here, dot(a_t[...], g_ref[:, here]) + e_ref[at, here].astype(F32)

    if in_hbm:

        def body(out_tile):
            out_tile[...] = values(pl.program_id(0))[1]

        pltpu.emit_pipeline(
            body, grid=(cols // chunk,), in_specs=[], out_specs=[pl.BlockSpec((rows, chunk), lambda i: (0, i))]
        )(out_ref)
    else:

        @pl.loop(0, cols // chunk)
        def _(i):
            here, value = values(i)
            out_ref[:, here] = value


def merged_part(a, e, g, part, in_hbm, after):
    tok, half = a.shape
    cols = e.shape[1]
    rows = half // 2
    place = pltpu.HBM if in_hbm else pltpu.VMEM
    return pl.pallas_call(
        functools.partial(merged_kernel, part, in_hbm),
        in_specs=[pl.BlockSpec(memory_space=pl.ANY)] + [pl.BlockSpec(memory_space=pltpu.VMEM)] * 3,
        out_specs=[pl.BlockSpec(memory_space=place), pl.BlockSpec(memory_space=pltpu.VMEM)],
        out_shape=[place((rows, cols), F32), jax.ShapeDtypeStruct((8, RANK), F32)],
        scratch_shapes=[pltpu.VMEM((rows, tok), BF16)],
        compiler_params=params(MERGED_LIMIT),
        cost_estimate=cost(2 * tok * cols * rows, rows * cols * 2),
        name="merged",
    )(after, a, e, g)


def q_kernel(owners, nm, nz, last, ids_ref, after_ref, *refs):
    pieces, refs = refs[:4], refs[4:]
    if last:
        v_in, q_in, gram_in, a_ref, e_ref, g_ref, send_ref, keep_ref, gram_ref, p_half, pcat, q_acc = refs
    else:
        a_ref, e_ref, v_ref, q_acc, gram_ref, p_half, pcat = refs
    rows = pieces[0].shape[2]
    cols = e_ref.shape[1]
    chunk = min(cols, 512)
    for piece, (half, members) in zip(pieces, owners):
        for i, km in enumerate(members):
            for k in range(nz):
                start = ((ids_ref[1] ^ km) * nz + (ids_ref[2] ^ k)) * (2 * rows) + half * rows
                p_half[pl.ds(pl.multiple_of(start, rows), rows), :] = piece[i, k]
    pcat[...] = split_rows(p_half[...].T)
    v = fold(dot(pcat[...], a_ref[...], ROWS_BY_ROWS))
    gram = dot(pcat[...], pcat[...], ROWS_BY_ROWS)
    if last:
        vcat = split_rows(v + v_in[...])
        whole = fold(gram + gram_in[...])
        gram_ref[...] = whole[:, :RANK] + whole[:, RANK:]
    else:
        v_ref[...] = v
        gram_ref[...] = gram

    for i in range(cols // chunk):
        here = pl.ds(i * chunk, chunk)
        q = dot(pcat[...], e_ref[:, here])
        if last:
            q += dot(vcat, g_ref[:, here])
            q_acc[:, here] = fold(q) + q_in[:, here]
        else:
            q_acc[:, here] = fold(q)

    if last:
        small = send_ref.shape[1]
        for out, flip in ((send_ref, 1), (keep_ref, 0)):
            for k in range(nz):
                start = ((ids_ref[0] ^ flip) * nz + (ids_ref[2] ^ k)) * small
                out[k] = q_acc[pl.ds(pl.multiple_of(start, small), small), :]


def right_terms(ids, pieces, owners, a, e, g, nm, after, before=None):
    tok, half = a.shape
    cols = e.shape[1]
    nz = pieces[0].shape[1]
    last = before is not None
    vmem = pl.BlockSpec(memory_space=pltpu.VMEM)
    sums = [(RANK, tok), (RANK, cols), (2 * RANK, 2 * RANK)]
    scratch = [pltpu.VMEM((half, RANK), F32), pltpu.VMEM((2 * RANK, half), BF16)]
    if last:
        args = [*pieces, *before, a, e, g]
        outs = [(nz, RANK // (2 * nz), cols)] * 2 + [(RANK, RANK)]
        scratch += [pltpu.VMEM((RANK, cols), F32)]
    else:
        args = [*pieces, a, e]
        outs = sums
    return pl.pallas_call(
        functools.partial(q_kernel, owners, nm, nz, last),
        grid_spec=pltpu.PrefetchScalarGridSpec(
            num_scalar_prefetch=1,
            grid=(),
            in_specs=[pl.BlockSpec(memory_space=pl.ANY)] + [vmem] * len(args),
            out_specs=[vmem] * 3,
            scratch_shapes=scratch,
        ),
        out_shape=[jax.ShapeDtypeStruct(shape, F32) for shape in outs],
        compiler_params=params(RIGHT_LIMIT),
        cost_estimate=cost(4 * half * RANK * (tok + cols), half * (tok + cols)),
        name="right_terms",
    )(ids, after, *args)


def chol_inverse_kernel(gram_ref, out_ref):
    left = gram_ref[...]
    row = lax.broadcasted_iota(jnp.int32, (RANK, RANK), 0)
    right = (row == lax.broadcasted_iota(jnp.int32, (RANK, RANK), 1)).astype(F32)
    for j in range(RANK):
        at = j % 8
        if j and at == 0:
            left, right = left[8:], right[8:]
        pivot_row, own = left[at : at + 1], right[at : at + 1]
        pivot = pivot_row[:, j : j + 1]
        out_ref[j : j + 1, :] = own * (1.0 / jnp.sqrt(pivot))
        inverse = 1.0 / pivot
        below = row[: left.shape[0], :1] > at
        factor = jnp.where(below, left[:, j : j + 1], 0.0)
        left = left - factor * (pivot_row * inverse)
        right = right - factor * (own * inverse)


def p_hat_kernel(owners, nm, nz, ids_ref, after_ref, *refs):
    pieces, (inv_ref, out_ref, p_all) = refs[:8], refs[8:]
    rows = pieces[0].shape[2]
    for h in range(2):
        for piece, (half, members) in zip(pieces[4 * h : 4 * h + 4], owners):
            for i, km in enumerate(members):
                for k in range(nz):
                    block = (h * nm + (ids_ref[1] ^ km)) * nz + (ids_ref[2] ^ k)
                    start = block * (2 * rows) + half * rows
                    p_all[pl.ds(pl.multiple_of(start, rows), rows), :] = piece[i, k]
    inv_hi = inv_ref[...].T.astype(BF16)
    inv_lo = (inv_ref[...].T - inv_hi.astype(F32)).astype(BF16)
    inv = jnp.concatenate([inv_hi, inv_hi, inv_lo, inv_lo], axis=0)
    tile = p_all.shape[0] // 8

    @pl.loop(0, 8)
    def _(i):
        at = pl.ds(pl.multiple_of(i * tile, tile), tile)
        x = p_all[at, :]
        hi = x.astype(BF16)
        lo = (x - hi.astype(F32)).astype(BF16)
        y = dot(jnp.concatenate([hi, lo, hi, lo], axis=1), inv)
        y_hi = y.astype(BF16)
        y_lo = (y - y_hi.astype(F32)).astype(BF16)
        out_ref[at, :] = jnp.concatenate([y_hi, y_lo], axis=1)


def left_factor(ids, pieces, owners, inv, rows, nm, nz, after):
    return pl.pallas_call(
        functools.partial(p_hat_kernel, owners, nm, nz),
        grid_spec=pltpu.PrefetchScalarGridSpec(
            num_scalar_prefetch=1,
            grid=(),
            in_specs=[pl.BlockSpec(memory_space=pl.ANY)] + [pl.BlockSpec(memory_space=pltpu.VMEM)] * 9,
            out_specs=pl.BlockSpec(memory_space=pltpu.VMEM),
            scratch_shapes=[pltpu.VMEM((rows, RANK), F32)],
        ),
        out_shape=jax.ShapeDtypeStruct((rows, 2 * RANK), BF16),
        compiler_params=params(SMALL_LIMIT),
        cost_estimate=cost(8 * rows * RANK * RANK, rows * RANK * 8),
        name="left_factor",
    )(ids, after, *pieces, inv)


def final_kernel(nz, scale, ids_ref, *refs):
    pieces, refs = refs[: 2 * nz], refs[2 * nz :]
    inv_ref, phat_ref, parts = refs[0], refs[1], refs[2:6]
    err_ref, qnew_hbm, q_sum, q_cat, qnew_ref, sem = refs[6:]
    small = pieces[0].shape[0]
    for h in range(2):
        for k in range(nz):
            block = (ids_ref[0] ^ h) * nz + (ids_ref[2] ^ k)
            q_sum[pl.ds(pl.multiple_of(block * small, small), small), :] = pieces[h * nz + k][...]
    q_t = scale * lax.dot_general(
        inv_ref[...], q_sum[...], (((1,), (0,)), ((), ())), precision=HIGHEST, preferred_element_type=F32
    )
    hi = q_t.astype(BF16)
    lo = (q_t - hi.astype(F32)).astype(BF16)
    q_cat[...] = jnp.concatenate([hi, hi, lo, lo], axis=0)
    qnew_ref[...] = q_t.T
    copy = pltpu.make_async_copy(qnew_ref, qnew_hbm, sem)
    copy.start()
    part_rows, cols = parts[0].shape
    chunk = min(cols, 512)
    own = ids_ref[0]

    def body(out_tile):
        here = pl.ds(pl.multiple_of(pl.program_id(1) * chunk, chunk), chunk)
        for number, merged in enumerate(parts):

            @pl.when(pl.program_id(0) == number)
            def _():
                x = phat_ref[pl.ds(number * part_rows, part_rows), :]
                approx = dot(jnp.concatenate([x, x], axis=1), q_cat[:, here])
                out_tile[0] = (merged[:, here] - approx).astype(BF16)

    pltpu.emit_pipeline(
        body,
        grid=(len(parts), cols // chunk),
        in_specs=[],
        out_specs=[pl.BlockSpec((1, part_rows, chunk), lambda i, j: (0, i ^ (own * 2), j))],
    )(err_ref)
    copy.wait()


def finish(ids, pieces, inv, phat, parts, replicas):
    nz = len(pieces) // 2
    part_rows, cols = parts[0].shape
    rows = part_rows * len(parts)
    vmem = pl.BlockSpec(memory_space=pltpu.VMEM)
    hbm = pl.BlockSpec(memory_space=pltpu.HBM)
    return pl.pallas_call(
        functools.partial(final_kernel, nz, 1.0 / replicas),
        grid_spec=pltpu.PrefetchScalarGridSpec(
            num_scalar_prefetch=1,
            grid=(),
            in_specs=[vmem] * (2 * nz + 2 + len(parts)),
            out_specs=[hbm, hbm],
            scratch_shapes=[
                pltpu.VMEM((RANK, cols), F32),
                pltpu.VMEM((4 * RANK, cols), BF16),
                pltpu.VMEM((cols, RANK), F32),
                pltpu.SemaphoreType.DMA,
            ],
        ),
        out_shape=[jax.ShapeDtypeStruct((1, rows, cols), BF16), jax.ShapeDtypeStruct((cols, RANK), F32)],
        compiler_params=params(FINAL_LIMIT),
        cost_estimate=cost(8 * rows * cols * RANK, rows * cols * 6),
        name="new_error",
    )(ids, *pieces, inv, phat, *parts)


def q_sum_kernel(nz, *refs):
    keep, came, outs = refs[0], refs[1], refs[2:]
    for k in range(nz):
        outs[k][...] = keep[k] + came[k]


def per_device(n_dp, n_mp, activations, out_grads, error_fb, q_prev):
    a, g, e, q = [
        pltpu.with_memory_space_constraint(x, pltpu.HBM) for x in (activations[0], out_grads[0], error_fb[0], q_prev)
    ]
    rows = a.shape[1]
    nz = n_dp // 2
    dp, mp = lax.axis_index("dp"), lax.axis_index("mp")
    ids = jnp.stack([dp % 2, mp, dp // 2]).astype(jnp.int32)
    bits = list(range(n_mp.bit_length() - 1))
    orders = [bits, bits[::-1]]

    def to_core(x):
        return lax.ppermute(x, "dp", [(i, i ^ 1) for i in range(n_dp)])

    def to_z(x, k):
        return lax.ppermute(x, "dp", [(i, i ^ (2 * k)) for i in range(n_dp)])

    def to_mp(x, k):
        return lax.ppermute(x, "mp", [(i, i ^ k) for i in range(n_mp)])

    p_far, a_far, e_far, g_here, ucat, qcat = left_terms(ids, q, g, a, e, n_mp, nz)
    p_arrived = to_core(p_far)
    p_near, a_near, e_near = left_terms(ids, q, g, a, e, n_mp, nz, (ucat, qcat))
    parts = []

    def beside(sent):
        number = len(parts)
        mine = (a_near, e_near) if number < 2 else (a_far, e_far)
        part, done = merged_part(*mine, g_here, number % 2, True, sent)
        parts.append(part)
        return done

    by_z = scatter_over_mp(p_near, p_arrived, to_mp, orders, beside)
    done = [beside(by_z[0])]
    came = [to_z(by_z[k], k) for k in range(1, nz)]
    [p_own] = in_vmem(own_sum_kernel, [(by_z[0].shape, F32)], [by_z[0], *came], "p_own", after=done)
    done = [beside(p_own)]
    p_pieces = [p_own] + [to_z(p_own, k) for k in range(1, nz)]
    near, owners = gather_over_mp(p_pieces, to_mp, orders, done)
    done = beside(near[0])
    far = [to_core(x) for x in near]

    half = right_terms(ids, near, owners, a_near, e_near, g_here, n_mp, done)
    q_send, q_keep, gram = right_terms(ids, far, owners, a_far, e_far, g_here, n_mp, done, half)

    piece = (q_keep.shape[1:], F32)
    q_by_z = in_vmem(functools.partial(q_sum_kernel, nz), [piece] * nz, [q_keep, to_core(q_send)], "q_sum")
    square = ((RANK, RANK), F32)
    [inv] = in_vmem(
        chol_inverse_kernel, [square], [gram], "chol_inverse", after=[q_by_z[0]], work=cost(2 * 10**10, 10**5)
    )
    came = [to_z(q_by_z[k], k) for k in range(1, nz)]
    [q_own] = in_vmem(own_sum_kernel, [piece], [q_by_z[0], *came], "q_own", after=[inv])
    q_near = [q_own] + [to_z(q_own, k) for k in range(1, nz)]
    q_pieces = q_near + [to_core(x) for x in q_near]

    phat = left_factor(ids, near + far, owners, inv, rows, n_mp, nz, q_own)
    new_error, q_new = finish(ids, q_pieces, inv, phat, parts, n_dp)
    return new_error, q_new


def solution(mesh):
    placed = (P("dp", None, None), P("dp", None, "mp"), P("dp", None, "mp"), P("mp", None))
    return jax.shard_map(
        functools.partial(per_device, mesh.shape["dp"], mesh.shape["mp"]),
        mesh=mesh,
        in_specs=placed,
        out_specs=(P("dp", None, "mp"), P("mp", None)),
        check_vma=False,
    )
```

```python
import functools

import jax
import jax.numpy as jnp
from jax import lax
from jax.experimental import pallas as pl
from jax.experimental.pallas import tpu as pltpu
from jax.sharding import PartitionSpec as P

F32 = jnp.float32
BF16 = jnp.bfloat16
HIGHEST = lax.Precision.HIGHEST
RANK = 128
VMEM_LIMIT = 50 * 1024 * 1024
LEFT_LIMIT = 14 * 1024 * 1024
SMALL_LIMIT = 6 * 1024 * 1024
MERGED_LIMIT = 8 * 1024 * 1024
RIGHT_LIMIT = 11 * 1024 * 1024
FINAL_LIMIT = 9 * 1024 * 1024


def params(limit=VMEM_LIMIT):
    return pltpu.CompilerParams(vmem_limit_bytes=limit)


def cost(flops, nbytes):
    return pl.CostEstimate(flops=flops, bytes_accessed=nbytes, transcendentals=0)


def split_rows(x):
    hi = x.astype(BF16)
    lo = (x - hi.astype(F32)).astype(BF16)
    return jnp.concatenate([hi, lo], axis=0)


def fold(y):
    return y[:RANK] + y[RANK:]


def dot(a, b, contract=((1,), (0,))):
    return lax.dot_general(a, b, (contract, ((), ())), preferred_element_type=F32)


ROWS_BY_ROWS = ((1,), (1,))


def skipping(count, body, *refs):
    body(*refs[count:])


def in_vmem(body, outs, args, name, limit=SMALL_LIMIT, work=None, after=()):
    args = [*after, *args]
    return pl.pallas_call(
        functools.partial(skipping, len(after), body),
        in_specs=[pl.BlockSpec(memory_space=pltpu.VMEM)] * len(args),
        out_specs=[pl.BlockSpec(memory_space=pltpu.VMEM)] * len(outs),
        out_shape=[jax.ShapeDtypeStruct(*out) for out in outs],
        compiler_params=params(limit),
        cost_estimate=work,
        name=name,
    )(*args)


STEPS = 8


def copies_of_half(a_hbm, e_hbm, a_ref, e_ref, sems, half):
    rows = e_ref.shape[0]
    tile = rows // STEPS
    copies = []
    for i in range(STEPS):
        here = pl.ds(i * tile, tile)
        there = pl.ds(pl.multiple_of(half * rows + i * tile, tile), tile)
        copies.append(
            (
                pltpu.make_async_copy(e_hbm.at[there, :], e_ref.at[here, :], sems.at[2 * i]),
                pltpu.make_async_copy(a_hbm.at[:, there], a_ref.at[:, here], sems.at[2 * i + 1]),
            )
        )
    return copies


def p_of_half(ids_ref, copies, a_ref, e_ref, ucat_ref, qcat_ref, p_ref):
    nz, small = p_ref.shape[1:3]
    tile = e_ref.shape[0] // 2
    for i in range(2):
        here = pl.ds(i * tile, tile)
        pairs = copies[i * STEPS // 2 : (i + 1) * STEPS // 2]
        for e_copy, _ in pairs:
            e_copy.wait()
        acc = dot(qcat_ref[...], e_ref[here, :], ROWS_BY_ROWS)
        for _, a_copy in pairs:
            a_copy.wait()
        acc += dot(ucat_ref[...], a_ref[:, here])
        p_tile = fold(acc).T
        for k in range(tile // small):
            block = i * (tile // small) + k
            p_ref[(block // nz) ^ ids_ref[1], (block % nz) ^ ids_ref[2]] = p_tile[k * small : (k + 1) * small]


def far_kernel(
    ids_ref, q_hbm, g_hbm, a_hbm, e_hbm, p_ref, a_ref, e_ref, g_ref, ucat_ref, qcat_ref, q_ref, sems, first_sems
):
    tok = g_ref.shape[0]
    q_copy = pltpu.make_async_copy(q_hbm, q_ref, first_sems.at[0])
    q_copy.start()
    g_copies = []
    for i in range(2):
        at = pl.ds(i * (tok // 2), tok // 2)
        g_copies.append(pltpu.make_async_copy(g_hbm.at[at, :], g_ref.at[at, :], first_sems.at[1 + i]))
        g_copies[-1].start()
    copies = copies_of_half(a_hbm, e_hbm, a_ref, e_ref, sems, ids_ref[0] ^ 1)
    for pair in copies:
        for copy in pair:
            copy.start()
    q_copy.wait()
    qcat_ref[...] = split_rows(q_ref[...].T)
    for i in range(2):
        at = pl.ds(i * (tok // 2), tok // 2)
        g_copies[i].wait()
        ucat_ref[:, at] = split_rows(fold(dot(qcat_ref[...], g_ref[at, :], ROWS_BY_ROWS)))
    p_of_half(ids_ref, copies, a_ref, e_ref, ucat_ref, qcat_ref, p_ref)


def near_kernel(ids_ref, ucat_ref, qcat_ref, a_hbm, e_hbm, p_ref, a_ref, e_ref, sems):
    copies = copies_of_half(a_hbm, e_hbm, a_ref, e_ref, sems, ids_ref[0])
    for pair in copies:
        for copy in pair:
            copy.start()
    p_of_half(ids_ref, copies, a_ref, e_ref, ucat_ref, qcat_ref, p_ref)


def left_terms(ids, q, g, a, e, nm, nz, before=None):
    tok, rows = a.shape
    cols = e.shape[1]
    vmem = pl.BlockSpec(memory_space=pltpu.VMEM)
    hbm = pl.BlockSpec(memory_space=pltpu.HBM)
    outs = [
        pltpu.VMEM((nm, nz, rows // (2 * nm * nz), RANK), F32),
        pltpu.VMEM((tok, rows // 2), BF16),
        pltpu.VMEM((rows // 2, cols), BF16),
    ]
    scratch = [pltpu.SemaphoreType.DMA((2 * STEPS,))]
    if before is None:
        body, specs, args = far_kernel, [hbm] * 4, (q, g, a, e)
        outs += [
            pltpu.VMEM((tok, cols), BF16),
            pltpu.VMEM((2 * RANK, tok), BF16),
            pltpu.VMEM((2 * RANK, cols), BF16),
        ]
        scratch = [pltpu.VMEM((cols, RANK), F32)] + scratch + [pltpu.SemaphoreType.DMA((3,))]
    else:
        body, specs, args = near_kernel, [vmem] * 2 + [hbm] * 2, (*before, a, e)
    return pl.pallas_call(
        body,
        grid_spec=pltpu.PrefetchScalarGridSpec(
            num_scalar_prefetch=1,
            grid=(),
            in_specs=specs,
            out_specs=[vmem] * len(outs),
            scratch_shapes=scratch,
        ),
        out_shape=outs,
        compiler_params=params(LEFT_LIMIT),
        cost_estimate=cost(2 * rows * RANK * (tok + cols), rows * (tok + cols)),
        name="left_terms",
    )(ids, *args)


def first_sum_kernel(keeps, sends, near_ref, far_ref, *outs):
    rows = near_ref.shape[2] // 2
    for half in range(2):
        for out, members in ((outs[2 * half], sends[half]), (outs[2 * half + 1], keeps[half])):
            for i, km in enumerate(members):
                at = (km, slice(None), pl.ds(half * rows, rows))
                out[i] = near_ref[at] + far_ref[at]


def next_sum_kernel(keeps, sends, *refs):
    ins, outs = refs[:4], refs[4:]
    for half in range(2):
        kept, came = ins[2 * half : 2 * half + 2]
        for out, places in ((outs[2 * half], sends[half]), (outs[2 * half + 1], keeps[half])):
            for i, at in enumerate(places):
                out[i] = kept[at] + came[at]


def last_sum_kernel(nz, *refs):
    ins, outs = refs[:4], refs[4:]
    rows = ins[0].shape[2]
    for k in range(nz):
        for half in range(2):
            outs[k][pl.ds(half * rows, rows), :] = ins[2 * half][0, k] + ins[2 * half + 1][0, k]


def scatter_over_mp(near, far, to_mp, orders, beside):
    nm, nz, block, _ = near.shape
    rows = block // 2
    members = [list(range(nm))] * 2
    values, done = None, ()
    for step in range(len(orders[0])):
        bits = [1 << order[step] for order in orders]
        keep_lists = [[km for km in members[h] if not km & bits[h]] for h in range(2)]
        send_lists = [[km | bits[h] for km in keep_lists[h]] for h in range(2)]
        count = len(keep_lists[0])
        outs = [((count, nz, rows, RANK), F32)] * 4
        if values is None:
            parts = in_vmem(functools.partial(first_sum_kernel, keep_lists, send_lists), outs, [near, far], "first_sum")
        else:
            keep_at = [[members[h].index(km) for km in keep_lists[h]] for h in range(2)]
            send_at = [[members[h].index(km) for km in send_lists[h]] for h in range(2)]
            parts = in_vmem(functools.partial(next_sum_kernel, keep_at, send_at), outs, values, "next_sum", after=done)
        members = keep_lists
        came = [to_mp(parts[0], bits[0]), to_mp(parts[2], bits[1])]
        done = beside(parts[1])
        values = [parts[1], came[0], parts[3], came[1]]
    return in_vmem(functools.partial(last_sum_kernel, nz), [((block, RANK), F32)] * nz, values, "last_sum", after=done)


def own_sum_kernel(*refs):
    ins, out = refs[:-1], refs[-1]
    total = ins[0][...]
    for came in ins[1:]:
        total = total + came[...]
    out[...] = total


def own_kernel(nz, *refs):
    ins, outs = refs[:nz], refs[nz:]
    rows = outs[0].shape[2]
    for k in range(nz):
        for half in range(2):
            outs[half][0, k] = ins[k][pl.ds(half * rows, rows), :]


def grow_kernel(*refs):
    ins, outs = refs[:4], refs[4:]
    count = ins[0].shape[0]
    for half in range(2):
        outs[half][pl.ds(0, count)] = ins[2 * half][...]
        outs[half][pl.ds(count, count)] = ins[2 * half + 1][...]


def gather_over_mp(pieces, to_mp, orders, beside, done):
    nz = len(pieces)
    rows = pieces[0].shape[0] // 2
    held = in_vmem(functools.partial(own_kernel, nz), [((1, nz, rows, RANK), F32)] * 2, pieces, "own_rows", after=done)
    members = [[0], [0]]
    last = len(orders[0]) - 1
    for step in range(last, -1, -1):
        bits = [1 << order[step] for order in orders]
        came = [to_mp(held[h], bits[h]) for h in range(2)]
        came_members = [[km ^ bits[h] for km in members[h]] for h in range(2)]
        if step == 0:
            return [held[0], held[1], came[0], came[1]], [
                (0, members[0]), (1, members[1]), (0, came_members[0]), (1, came_members[1])
            ]
        count = len(members[0])
        held = in_vmem(
            grow_kernel,
            [((2 * count, nz, rows, RANK), F32)] * 2,
            [held[0], came[0], held[1], came[1]],
            "grow",
            after=beside(held[0], 2),
        )
        members = [members[h] + came_members[h] for h in range(2)]


def merged_kernel(part, after_ref, a_ref, e_ref, g_ref, out_ref, done_ref, a_t):
    done_ref[...] = jnp.zeros_like(done_ref)
    rows, cols = out_ref.shape
    tile = rows // 2
    a_t[...] = a_ref[:, pl.ds(part * rows, rows)].T

    def body(out_tile):
        start = pl.multiple_of(pl.program_id(0) * tile, tile)
        e_tile = e_ref[pl.ds(part * rows + start, tile), :]
        out_tile[...] = dot(a_t[pl.ds(start, tile), :], g_ref[...]) + e_tile.astype(F32)

    pltpu.emit_pipeline(body, grid=(2,), in_specs=[], out_specs=[pl.BlockSpec((tile, cols), lambda i: (i, 0))])(out_ref)


def merged_part(a, e, g, part, after):
    tok, half = a.shape
    cols = e.shape[1]
    rows = half // 4
    return pl.pallas_call(
        functools.partial(merged_kernel, part),
        in_specs=[pl.BlockSpec(memory_space=pl.ANY)] + [pl.BlockSpec(memory_space=pltpu.VMEM)] * 3,
        out_specs=[pl.BlockSpec(memory_space=pltpu.HBM), pl.BlockSpec(memory_space=pltpu.VMEM)],
        out_shape=[pltpu.HBM((rows, cols), F32), jax.ShapeDtypeStruct((8, RANK), F32)],
        scratch_shapes=[pltpu.VMEM((rows, tok), BF16)],
        compiler_params=params(MERGED_LIMIT),
        cost_estimate=cost(2 * tok * cols * rows, rows * cols * 2),
        name="merged",
    )(after, a, e, g)


def q_kernel(owners, nm, nz, last, ids_ref, after_ref, *refs):
    pieces, refs = refs[:4], refs[4:]
    if last:
        v_in, q_in, gram_in, a_ref, e_ref, g_ref, send_ref, keep_ref, gram_ref, p_half, pcat, q_acc = refs
    else:
        a_ref, e_ref, v_ref, q_acc, gram_ref, p_half, pcat = refs
    rows = pieces[0].shape[2]
    cols = e_ref.shape[1]
    chunk = min(cols, 512)
    for piece, (half, members) in zip(pieces, owners):
        for i, km in enumerate(members):
            for k in range(nz):
                start = ((ids_ref[1] ^ km) * nz + (ids_ref[2] ^ k)) * (2 * rows) + half * rows
                p_half[pl.ds(pl.multiple_of(start, rows), rows), :] = piece[i, k]
    pcat[...] = split_rows(p_half[...].T)
    v = fold(dot(pcat[...], a_ref[...], ROWS_BY_ROWS))
    gram = dot(pcat[...], pcat[...], ROWS_BY_ROWS)
    if last:
        vcat = split_rows(v + v_in[...])
        whole = fold(gram + gram_in[...])
        gram_ref[...] = whole[:, :RANK] + whole[:, RANK:]
    else:
        v_ref[...] = v
        gram_ref[...] = gram

    for i in range(cols // chunk):
        here = pl.ds(i * chunk, chunk)
        q = dot(pcat[...], e_ref[:, here])
        if last:
            q += dot(vcat, g_ref[:, here])
            q_acc[:, here] = fold(q) + q_in[:, here]
        else:
            q_acc[:, here] = fold(q)

    if last:
        small = send_ref.shape[1]
        for out, flip in ((send_ref, 1), (keep_ref, 0)):
            for k in range(nz):
                start = ((ids_ref[0] ^ flip) * nz + (ids_ref[2] ^ k)) * small
                out[k] = q_acc[pl.ds(pl.multiple_of(start, small), small), :]


def right_terms(ids, pieces, owners, a, e, g, nm, after, before=None):
    tok, half = a.shape
    cols = e.shape[1]
    nz = pieces[0].shape[1]
    last = before is not None
    vmem = pl.BlockSpec(memory_space=pltpu.VMEM)
    sums = [(RANK, tok), (RANK, cols), (2 * RANK, 2 * RANK)]
    scratch = [pltpu.VMEM((half, RANK), F32), pltpu.VMEM((2 * RANK, half), BF16)]
    if last:
        args = [*pieces, *before, a, e, g]
        outs = [(nz, RANK // (2 * nz), cols)] * 2 + [(RANK, RANK)]
        scratch += [pltpu.VMEM((RANK, cols), F32)]
    else:
        args = [*pieces, a, e]
        outs = sums
    return pl.pallas_call(
        functools.partial(q_kernel, owners, nm, nz, last),
        grid_spec=pltpu.PrefetchScalarGridSpec(
            num_scalar_prefetch=1,
            grid=(),
            in_specs=[pl.BlockSpec(memory_space=pl.ANY)] + [vmem] * len(args),
            out_specs=[vmem] * 3,
            scratch_shapes=scratch,
        ),
        out_shape=[jax.ShapeDtypeStruct(shape, F32) for shape in outs],
        compiler_params=params(RIGHT_LIMIT),
        cost_estimate=cost(4 * half * RANK * (tok + cols), half * (tok + cols)),
        name="right_terms",
    )(ids, after, *args)


def chol_inverse_kernel(gram_ref, out_ref):
    left = gram_ref[...]
    row = lax.broadcasted_iota(jnp.int32, (RANK, RANK), 0)
    right = (row == lax.broadcasted_iota(jnp.int32, (RANK, RANK), 1)).astype(F32)
    for j in range(RANK):
        at = j % 8
        if j and at == 0:
            left, right = left[8:], right[8:]
        pivot_row, own = left[at : at + 1], right[at : at + 1]
        pivot = pivot_row[:, j : j + 1]
        out_ref[j : j + 1, :] = own * (1.0 / jnp.sqrt(pivot))
        inverse = 1.0 / pivot
        below = row[: left.shape[0], :1] > at
        factor = jnp.where(below, left[:, j : j + 1], 0.0)
        left = left - factor * (pivot_row * inverse)
        right = right - factor * (own * inverse)


def p_hat_kernel(owners, nm, nz, ids_ref, q_ref, *refs):
    pieces, (inv_ref, out_ref, q_again, p_all) = refs[:8], refs[8:]
    q_again[...] = q_ref[...]
    rows = pieces[0].shape[2]
    for h in range(2):
        for piece, (half, members) in zip(pieces[4 * h : 4 * h + 4], owners):
            for i, km in enumerate(members):
                for k in range(nz):
                    block = (h * nm + (ids_ref[1] ^ km)) * nz + (ids_ref[2] ^ k)
                    start = block * (2 * rows) + half * rows
                    p_all[pl.ds(pl.multiple_of(start, rows), rows), :] = piece[i, k]
    inv_hi = inv_ref[...].T.astype(BF16)
    inv_lo = (inv_ref[...].T - inv_hi.astype(F32)).astype(BF16)
    inv = jnp.concatenate([inv_hi, inv_hi, inv_lo, inv_lo], axis=0)
    tile = p_all.shape[0] // 8

    @pl.loop(0, 8)
    def _(i):
        at = pl.ds(pl.multiple_of(i * tile, tile), tile)
        x = p_all[at, :]
        hi = x.astype(BF16)
        lo = (x - hi.astype(F32)).astype(BF16)
        y = dot(jnp.concatenate([hi, lo, hi, lo], axis=1), inv)
        y_hi = y.astype(BF16)
        y_lo = (y - y_hi.astype(F32)).astype(BF16)
        out_ref[at, :] = jnp.concatenate([y_hi, y_lo], axis=1)


def left_factor(ids, pieces, owners, inv, rows, nm, nz, q_own):
    return pl.pallas_call(
        functools.partial(p_hat_kernel, owners, nm, nz),
        grid_spec=pltpu.PrefetchScalarGridSpec(
            num_scalar_prefetch=1,
            grid=(),
            in_specs=[pl.BlockSpec(memory_space=pltpu.VMEM)] * 10,
            out_specs=[pl.BlockSpec(memory_space=pltpu.VMEM)] * 2,
            scratch_shapes=[pltpu.VMEM((rows, RANK), F32)],
        ),
        out_shape=[jax.ShapeDtypeStruct((rows, 2 * RANK), BF16), jax.ShapeDtypeStruct(q_own.shape, F32)],
        compiler_params=params(SMALL_LIMIT),
        cost_estimate=cost(8 * rows * RANK * RANK, rows * RANK * 8),
        name="left_factor",
    )(ids, q_own, *pieces, inv)


def final_kernel(nz, scale, ids_ref, *refs):
    pieces, refs = refs[: 2 * nz], refs[2 * nz :]
    inv_ref, phat_ref, parts = refs[0], refs[1], refs[2:10]
    err_ref, qnew_hbm, q_sum, q_cat, qnew_ref, sem = refs[10:]
    small = pieces[0].shape[0]
    for h in range(2):
        for k in range(nz):
            block = (ids_ref[0] ^ h) * nz + (ids_ref[2] ^ k)
            q_sum[pl.ds(pl.multiple_of(block * small, small), small), :] = pieces[h * nz + k][...]
    q_t = scale * lax.dot_general(
        inv_ref[...], q_sum[...], (((1,), (0,)), ((), ())), precision=HIGHEST, preferred_element_type=F32
    )
    hi = q_t.astype(BF16)
    lo = (q_t - hi.astype(F32)).astype(BF16)
    q_cat[...] = jnp.concatenate([hi, hi, lo, lo], axis=0)
    qnew_ref[...] = q_t.T
    copy = pltpu.make_async_copy(qnew_ref, qnew_hbm, sem)
    copy.start()
    part_rows, cols = parts[0].shape
    chunk = min(cols, 1024)
    tile = part_rows // 2
    own = ids_ref[0]

    def body(out_tile):
        here = pl.ds(pl.multiple_of(pl.program_id(1) * chunk, chunk), chunk)
        for number, merged in enumerate(parts):

            @pl.when(pl.program_id(0) == number)
            def _():
                for i in range(2):
                    at = pl.ds(i * tile, tile)
                    x = phat_ref[pl.ds(number * part_rows + i * tile, tile), :]
                    approx = dot(jnp.concatenate([x, x], axis=1), q_cat[:, here])
                    out_tile[0, at] = (merged[at, here] - approx).astype(BF16)

    pltpu.emit_pipeline(
        body,
        grid=(len(parts), cols // chunk),
        in_specs=[],
        out_specs=[pl.BlockSpec((1, part_rows, chunk), lambda i, j: (0, i ^ (own * 4), j))],
    )(err_ref)
    copy.wait()


def finish(ids, pieces, inv, phat, parts, replicas):
    nz = len(pieces) // 2
    part_rows, cols = parts[0].shape
    rows = part_rows * len(parts)
    vmem = pl.BlockSpec(memory_space=pltpu.VMEM)
    hbm = pl.BlockSpec(memory_space=pltpu.HBM)
    return pl.pallas_call(
        functools.partial(final_kernel, nz, 1.0 / replicas),
        grid_spec=pltpu.PrefetchScalarGridSpec(
            num_scalar_prefetch=1,
            grid=(),
            in_specs=[vmem] * (2 * nz + 2 + len(parts)),
            out_specs=[hbm, hbm],
            scratch_shapes=[
                pltpu.VMEM((RANK, cols), F32),
                pltpu.VMEM((4 * RANK, cols), BF16),
                pltpu.VMEM((cols, RANK), F32),
                pltpu.SemaphoreType.DMA,
            ],
        ),
        out_shape=[jax.ShapeDtypeStruct((1, rows, cols), BF16), jax.ShapeDtypeStruct((cols, RANK), F32)],
        compiler_params=params(FINAL_LIMIT),
        cost_estimate=cost(8 * rows * cols * RANK, rows * cols * 6),
        name="new_error",
    )(ids, *pieces, inv, phat, *parts)


def q_sum_kernel(nz, *refs):
    keep, came, outs = refs[0], refs[1], refs[2:]
    for k in range(nz):
        outs[k][...] = keep[k] + came[k]


def per_device(n_dp, n_mp, activations, out_grads, error_fb, q_prev):
    a, g, e, q = [
        pltpu.with_memory_space_constraint(x, pltpu.HBM) for x in (activations[0], out_grads[0], error_fb[0], q_prev)
    ]
    rows = a.shape[1]
    nz = n_dp // 2
    dp, mp = lax.axis_index("dp"), lax.axis_index("mp")
    ids = jnp.stack([dp % 2, mp, dp // 2]).astype(jnp.int32)
    bits = list(range(n_mp.bit_length() - 1))
    orders = [bits, bits[::-1]]

    def to_core(x):
        return lax.ppermute(x, "dp", [(i, i ^ 1) for i in range(n_dp)])

    def to_z(x, k):
        return lax.ppermute(x, "dp", [(i, i ^ (2 * k)) for i in range(n_dp)])

    def to_mp(x, k):
        return lax.ppermute(x, "mp", [(i, i ^ k) for i in range(n_mp)])

    p_far, a_far, e_far, g_here, ucat, qcat = left_terms(ids, q, g, a, e, n_mp, nz)
    p_arrived = to_core(p_far)
    p_near, a_near, e_near = left_terms(ids, q, g, a, e, n_mp, nz, (ucat, qcat))
    parts = []

    def beside(sent, count=1):
        done = []
        while count and len(parts) < 8:
            number = len(parts)
            mine = (a_near, e_near) if number < 4 else (a_far, e_far)
            part, sent = merged_part(*mine, g_here, number % 4, sent)
            parts.append(part)
            done = [sent]
            count -= 1
        return done

    by_z = scatter_over_mp(p_near, p_arrived, to_mp, orders, beside)
    done = beside(by_z[0])
    came = [to_z(by_z[k], k) for k in range(1, nz)]
    [p_own] = in_vmem(own_sum_kernel, [(by_z[0].shape, F32)], [by_z[0], *came], "p_own", after=done)
    done = beside(p_own)
    p_pieces = [p_own] + [to_z(p_own, k) for k in range(1, nz)]
    near, owners = gather_over_mp(p_pieces, to_mp, orders, beside, done)
    done = (beside(near[0], 8) or [near[0]])[0]
    far = [to_core(x) for x in near]

    half = right_terms(ids, near, owners, a_near, e_near, g_here, n_mp, done)
    q_send, q_keep, gram = right_terms(ids, far, owners, a_far, e_far, g_here, n_mp, done, half)

    piece = (q_keep.shape[1:], F32)
    q_by_z = in_vmem(functools.partial(q_sum_kernel, nz), [piece] * nz, [q_keep, to_core(q_send)], "q_sum")
    square = ((RANK, RANK), F32)
    [inv] = in_vmem(
        chol_inverse_kernel, [square], [gram], "chol_inverse", after=[q_by_z[0]], work=cost(2 * 10**10, 10**5)
    )
    came = [to_z(q_by_z[k], k) for k in range(1, nz)]
    [q_own] = in_vmem(own_sum_kernel, [piece], [q_by_z[0], *came], "q_own", after=[inv])
    phat, q_again = left_factor(ids, near + far, owners, inv, rows, n_mp, nz, q_own)
    q_near = [q_own] + [to_z(q_own, k) for k in range(1, nz)]
    q_pieces = q_near + [to_core(x) for x in [q_again] + q_near[1:]]

    new_error, q_new = finish(ids, q_pieces, inv, phat, parts, n_dp)
    return new_error, q_new


def solution(mesh):
    placed = (P("dp", None, None), P("dp", None, "mp"), P("dp", None, "mp"), P("mp", None))
    return jax.shard_map(
        functools.partial(per_device, mesh.shape["dp"], mesh.shape["mp"]),
        mesh=mesh,
        in_specs=placed,
        out_specs=(P("dp", None, "mp"), P("mp", None)),
        check_vma=False,
    )
```

```python
import functools

import jax
import jax.numpy as jnp
from jax import lax
from jax.experimental import pallas as pl
from jax.experimental.pallas import tpu as pltpu
from jax.sharding import PartitionSpec as P

F32 = jnp.float32
BF16 = jnp.bfloat16
HIGHEST = lax.Precision.HIGHEST
RANK = 128
VMEM_LIMIT = 50 * 1024 * 1024
LEFT_LIMIT = 14 * 1024 * 1024
SMALL_LIMIT = 6 * 1024 * 1024
MERGED_LIMIT = 8 * 1024 * 1024
RIGHT_LIMIT = 11 * 1024 * 1024
FINAL_LIMIT = 9 * 1024 * 1024


def params(limit=VMEM_LIMIT):
    return pltpu.CompilerParams(vmem_limit_bytes=limit)


def cost(flops, nbytes):
    return pl.CostEstimate(flops=flops, bytes_accessed=nbytes, transcendentals=0)


def split_rows(x):
    hi = x.astype(BF16)
    lo = (x - hi.astype(F32)).astype(BF16)
    return jnp.concatenate([hi, lo], axis=0)


def fold(y):
    return y[:RANK] + y[RANK:]


def dot(a, b, contract=((1,), (0,))):
    return lax.dot_general(a, b, (contract, ((), ())), preferred_element_type=F32)


ROWS_BY_ROWS = ((1,), (1,))


def skipping(count, body, *refs):
    body(*refs[count:])


def in_vmem(body, outs, args, name, limit=SMALL_LIMIT, work=None, after=()):
    args = [*after, *args]
    return pl.pallas_call(
        functools.partial(skipping, len(after), body),
        in_specs=[pl.BlockSpec(memory_space=pltpu.VMEM)] * len(args),
        out_specs=[pl.BlockSpec(memory_space=pltpu.VMEM)] * len(outs),
        out_shape=[jax.ShapeDtypeStruct(*out) for out in outs],
        compiler_params=params(limit),
        cost_estimate=work,
        name=name,
    )(*args)


STEPS = 8


def copies_of_half(a_hbm, e_hbm, a_ref, e_ref, sems, half):
    rows = e_ref.shape[0]
    tile = rows // STEPS
    copies = []
    for i in range(STEPS):
        here = pl.ds(i * tile, tile)
        there = pl.ds(pl.multiple_of(half * rows + i * tile, tile), tile)
        copies.append(
            (
                pltpu.make_async_copy(e_hbm.at[there, :], e_ref.at[here, :], sems.at[2 * i]),
                pltpu.make_async_copy(a_hbm.at[:, there], a_ref.at[:, here], sems.at[2 * i + 1]),
            )
        )
    return copies


def p_of_half(ids_ref, copies, a_ref, e_ref, ucat_ref, qcat_ref, p_ref):
    nz, small = p_ref.shape[1:3]
    tile = e_ref.shape[0] // 2
    for i in range(2):
        here = pl.ds(i * tile, tile)
        pairs = copies[i * STEPS // 2 : (i + 1) * STEPS // 2]
        for e_copy, _ in pairs:
            e_copy.wait()
        acc = dot(qcat_ref[...], e_ref[here, :], ROWS_BY_ROWS)
        for _, a_copy in pairs:
            a_copy.wait()
        acc += dot(ucat_ref[...], a_ref[:, here])
        p_tile = fold(acc).T
        for k in range(tile // small):
            block = i * (tile // small) + k
            p_ref[(block // nz) ^ ids_ref[1], (block % nz) ^ ids_ref[2]] = p_tile[k * small : (k + 1) * small]


def far_kernel(
    ids_ref, q_hbm, g_hbm, a_hbm, e_hbm, p_ref, a_ref, e_ref, g_ref, ucat_ref, qcat_ref, q_ref, sems, first_sems
):
    tok = g_ref.shape[0]
    q_copy = pltpu.make_async_copy(q_hbm, q_ref, first_sems.at[0])
    q_copy.start()
    g_copies = []
    for i in range(2):
        at = pl.ds(i * (tok // 2), tok // 2)
        g_copies.append(pltpu.make_async_copy(g_hbm.at[at, :], g_ref.at[at, :], first_sems.at[1 + i]))
        g_copies[-1].start()
    copies = copies_of_half(a_hbm, e_hbm, a_ref, e_ref, sems, ids_ref[0] ^ 1)
    for pair in copies:
        for copy in pair:
            copy.start()
    q_copy.wait()
    qcat_ref[...] = split_rows(q_ref[...].T)
    for i in range(2):
        at = pl.ds(i * (tok // 2), tok // 2)
        g_copies[i].wait()
        ucat_ref[:, at] = split_rows(fold(dot(qcat_ref[...], g_ref[at, :], ROWS_BY_ROWS)))
    p_of_half(ids_ref, copies, a_ref, e_ref, ucat_ref, qcat_ref, p_ref)


def near_kernel(ids_ref, ucat_ref, qcat_ref, a_hbm, e_hbm, p_ref, a_ref, e_ref, sems):
    copies = copies_of_half(a_hbm, e_hbm, a_ref, e_ref, sems, ids_ref[0])
    for pair in copies:
        for copy in pair:
            copy.start()
    p_of_half(ids_ref, copies, a_ref, e_ref, ucat_ref, qcat_ref, p_ref)


def left_terms(ids, q, g, a, e, nm, nz, before=None):
    tok, rows = a.shape
    cols = e.shape[1]
    vmem = pl.BlockSpec(memory_space=pltpu.VMEM)
    hbm = pl.BlockSpec(memory_space=pltpu.HBM)
    outs = [
        pltpu.VMEM((nm, nz, rows // (2 * nm * nz), RANK), F32),
        pltpu.VMEM((tok, rows // 2), BF16),
        pltpu.VMEM((rows // 2, cols), BF16),
    ]
    scratch = [pltpu.SemaphoreType.DMA((2 * STEPS,))]
    if before is None:
        body, specs, args = far_kernel, [hbm] * 4, (q, g, a, e)
        outs += [
            pltpu.VMEM((tok, cols), BF16),
            pltpu.VMEM((2 * RANK, tok), BF16),
            pltpu.VMEM((2 * RANK, cols), BF16),
        ]
        scratch = [pltpu.VMEM((cols, RANK), F32)] + scratch + [pltpu.SemaphoreType.DMA((3,))]
    else:
        body, specs, args = near_kernel, [vmem] * 2 + [hbm] * 2, (*before, a, e)
    return pl.pallas_call(
        body,
        grid_spec=pltpu.PrefetchScalarGridSpec(
            num_scalar_prefetch=1,
            grid=(),
            in_specs=specs,
            out_specs=[vmem] * len(outs),
            scratch_shapes=scratch,
        ),
        out_shape=outs,
        compiler_params=params(LEFT_LIMIT),
        cost_estimate=cost(2 * rows * RANK * (tok + cols), rows * (tok + cols)),
        name="left_terms",
    )(ids, *args)


def first_sum_kernel(keeps, sends, near_ref, far_ref, *outs):
    rows = near_ref.shape[2] // 2
    for half in range(2):
        for out, members in ((outs[2 * half], sends[half]), (outs[2 * half + 1], keeps[half])):
            for i, km in enumerate(members):
                at = (km, slice(None), pl.ds(half * rows, rows))
                out[i] = near_ref[at] + far_ref[at]


def next_sum_kernel(keeps, sends, *refs):
    ins, outs = refs[:4], refs[4:]
    for half in range(2):
        kept, came = ins[2 * half : 2 * half + 2]
        for out, places in ((outs[2 * half], sends[half]), (outs[2 * half + 1], keeps[half])):
            for i, at in enumerate(places):
                out[i] = kept[at] + came[at]


def last_sum_kernel(nz, *refs):
    ins, outs = refs[:4], refs[4:]
    rows = ins[0].shape[2]
    for k in range(nz):
        for half in range(2):
            outs[k][pl.ds(half * rows, rows), :] = ins[2 * half][0, k] + ins[2 * half + 1][0, k]


def scatter_over_mp(near, far, to_mp, orders, beside):
    nm, nz, block, _ = near.shape
    rows = block // 2
    members = [list(range(nm))] * 2
    values, done = None, ()
    for step in range(len(orders[0])):
        bits = [1 << order[step] for order in orders]
        keep_lists = [[km for km in members[h] if not km & bits[h]] for h in range(2)]
        send_lists = [[km | bits[h] for km in keep_lists[h]] for h in range(2)]
        count = len(keep_lists[0])
        outs = [((count, nz, rows, RANK), F32)] * 4
        if values is None:
            parts = in_vmem(functools.partial(first_sum_kernel, keep_lists, send_lists), outs, [near, far], "first_sum")
        else:
            keep_at = [[members[h].index(km) for km in keep_lists[h]] for h in range(2)]
            send_at = [[members[h].index(km) for km in send_lists[h]] for h in range(2)]
            parts = in_vmem(functools.partial(next_sum_kernel, keep_at, send_at), outs, values, "next_sum", after=done)
        members = keep_lists
        came = [to_mp(parts[0], bits[0]), to_mp(parts[2], bits[1])]
        done = beside(parts[1])
        values = [parts[1], came[0], parts[3], came[1]]
    return in_vmem(functools.partial(last_sum_kernel, nz), [((block, RANK), F32)] * nz, values, "last_sum", after=done)


def own_sum_kernel(*refs):
    ins, out = refs[:-1], refs[-1]
    total = ins[0][...]
    for came in ins[1:]:
        total = total + came[...]
    out[...] = total


def own_kernel(nz, *refs):
    ins, outs = refs[:nz], refs[nz:]
    rows = outs[0].shape[2]
    for k in range(nz):
        for half in range(2):
            outs[half][0, k] = ins[k][pl.ds(half * rows, rows), :]


def grow_kernel(*refs):
    ins, outs = refs[:4], refs[4:]
    count = ins[0].shape[0]
    for half in range(2):
        outs[half][pl.ds(0, count)] = ins[2 * half][...]
        outs[half][pl.ds(count, count)] = ins[2 * half + 1][...]


def gather_over_mp(pieces, to_mp, orders, beside, done):
    nz = len(pieces)
    rows = pieces[0].shape[0] // 2
    held = in_vmem(functools.partial(own_kernel, nz), [((1, nz, rows, RANK), F32)] * 2, pieces, "own_rows", after=done)
    members = [[0], [0]]
    last = len(orders[0]) - 1
    for step in range(last, -1, -1):
        bits = [1 << order[step] for order in orders]
        came = [to_mp(held[h], bits[h]) for h in range(2)]
        came_members = [[km ^ bits[h] for km in members[h]] for h in range(2)]
        if step == 0:
            return [held[0], held[1], came[0], came[1]], [
                (0, members[0]), (1, members[1]), (0, came_members[0]), (1, came_members[1])
            ]
        count = len(members[0])
        held = in_vmem(
            grow_kernel,
            [((2 * count, nz, rows, RANK), F32)] * 2,
            [held[0], came[0], held[1], came[1]],
            "grow",
            after=beside(held[0]),
        )
        members = [members[h] + came_members[h] for h in range(2)]


def merged_kernel(part, in_hbm, after_ref, a_ref, e_ref, g_ref, out_ref, done_ref, a_t, *scratch):
    done_ref[...] = jnp.zeros_like(done_ref)
    rows, cols = out_ref.shape
    tile, chunk = rows // 2, min(cols, 512)
    held, sems = scratch if in_hbm else (out_ref, None)
    copies = []
    for i in range(2):
        at = pl.ds(i * tile, tile)
        a_t[at, :] = a_ref[:, pl.ds(part * rows + i * tile, tile)].T
        for j in range(cols // chunk):
            here = pl.ds(j * chunk, chunk)
            e_tile = e_ref[pl.ds(part * rows + i * tile, tile), here]
            held[at, here] = dot(a_t[at, :], g_ref[:, here]) + e_tile.astype(F32)
            if in_hbm:
                copy = pltpu.make_async_copy(held.at[at, here], out_ref.at[at, here], sems.at[len(copies)])
                copy.start()
                copies.append(copy)
    for copy in copies:
        copy.wait()


def merged_part(a, e, g, part, in_hbm, after):
    tok, half = a.shape
    cols = e.shape[1]
    rows = half // 4
    place = pltpu.HBM if in_hbm else pltpu.VMEM
    scratch = [pltpu.VMEM((rows, tok), BF16)]
    if in_hbm:
        scratch += [pltpu.VMEM((rows, cols), F32), pltpu.SemaphoreType.DMA((2 * (cols // min(cols, 512)),))]
    return pl.pallas_call(
        functools.partial(merged_kernel, part, in_hbm),
        in_specs=[pl.BlockSpec(memory_space=pl.ANY)] + [pl.BlockSpec(memory_space=pltpu.VMEM)] * 3,
        out_specs=[pl.BlockSpec(memory_space=place), pl.BlockSpec(memory_space=pltpu.VMEM)],
        out_shape=[place((rows, cols), F32), jax.ShapeDtypeStruct((8, RANK), F32)],
        scratch_shapes=scratch,
        compiler_params=params(MERGED_LIMIT),
        cost_estimate=cost(2 * tok * cols * rows, rows * cols * 2),
        name="merged",
    )(after, a, e, g)


def q_kernel(owners, nm, nz, last, ids_ref, after_ref, *refs):
    pieces, refs = refs[:4], refs[4:]
    if last:
        v_in, q_in, gram_in, a_ref, e_ref, g_ref, send_ref, keep_ref, gram_ref, p_half, pcat, q_acc = refs
    else:
        a_ref, e_ref, v_ref, q_acc, gram_ref, p_half, pcat = refs
    rows = pieces[0].shape[2]
    cols = e_ref.shape[1]
    chunk = min(cols, 512)
    for piece, (half, members) in zip(pieces, owners):
        for i, km in enumerate(members):
            for k in range(nz):
                start = ((ids_ref[1] ^ km) * nz + (ids_ref[2] ^ k)) * (2 * rows) + half * rows
                p_half[pl.ds(pl.multiple_of(start, rows), rows), :] = piece[i, k]
    pcat[...] = split_rows(p_half[...].T)
    v = fold(dot(pcat[...], a_ref[...], ROWS_BY_ROWS))
    gram = dot(pcat[...], pcat[...], ROWS_BY_ROWS)
    if last:
        vcat = split_rows(v + v_in[...])
        whole = fold(gram + gram_in[...])
        gram_ref[...] = whole[:, :RANK] + whole[:, RANK:]
    else:
        v_ref[...] = v
        gram_ref[...] = gram

    for i in range(cols // chunk):
        here = pl.ds(i * chunk, chunk)
        q = dot(pcat[...], e_ref[:, here])
        if last:
            q += dot(vcat, g_ref[:, here])
            q_acc[:, here] = fold(q) + q_in[:, here]
        else:
            q_acc[:, here] = fold(q)

    if last:
        small = send_ref.shape[1]
        for out, flip in ((send_ref, 1), (keep_ref, 0)):
            for k in range(nz):
                start = ((ids_ref[0] ^ flip) * nz + (ids_ref[2] ^ k)) * small
                out[k] = q_acc[pl.ds(pl.multiple_of(start, small), small), :]


def right_terms(ids, pieces, owners, a, e, g, nm, after, before=None):
    tok, half = a.shape
    cols = e.shape[1]
    nz = pieces[0].shape[1]
    last = before is not None
    vmem = pl.BlockSpec(memory_space=pltpu.VMEM)
    sums = [(RANK, tok), (RANK, cols), (2 * RANK, 2 * RANK)]
    scratch = [pltpu.VMEM((half, RANK), F32), pltpu.VMEM((2 * RANK, half), BF16)]
    if last:
        args = [*pieces, *before, a, e, g]
        outs = [(nz, RANK // (2 * nz), cols)] * 2 + [(RANK, RANK)]
        scratch += [pltpu.VMEM((RANK, cols), F32)]
    else:
        args = [*pieces, a, e]
        outs = sums
    return pl.pallas_call(
        functools.partial(q_kernel, owners, nm, nz, last),
        grid_spec=pltpu.PrefetchScalarGridSpec(
            num_scalar_prefetch=1,
            grid=(),
            in_specs=[pl.BlockSpec(memory_space=pl.ANY)] + [vmem] * len(args),
            out_specs=[vmem] * 3,
            scratch_shapes=scratch,
        ),
        out_shape=[jax.ShapeDtypeStruct(shape, F32) for shape in outs],
        compiler_params=params(RIGHT_LIMIT),
        cost_estimate=cost(4 * half * RANK * (tok + cols), half * (tok + cols)),
        name="right_terms",
    )(ids, after, *args)


def chol_inverse_kernel(gram_ref, out_ref):
    left = gram_ref[...]
    row = lax.broadcasted_iota(jnp.int32, (RANK, RANK), 0)
    right = (row == lax.broadcasted_iota(jnp.int32, (RANK, RANK), 1)).astype(F32)
    for j in range(RANK):
        at = j % 8
        if j and at == 0:
            left, right = left[8:], right[8:]
        pivot_row, own = left[at : at + 1], right[at : at + 1]
        pivot = pivot_row[:, j : j + 1]
        out_ref[j : j + 1, :] = own * (1.0 / jnp.sqrt(pivot))
        inverse = 1.0 / pivot
        below = row[: left.shape[0], :1] > at
        factor = jnp.where(below, left[:, j : j + 1], 0.0)
        left = left - factor * (pivot_row * inverse)
        right = right - factor * (own * inverse)


def p_hat_kernel(owners, nm, nz, ids_ref, q_ref, after_ref, *refs):
    pieces, (inv_ref, out_ref, q_again, p_all) = refs[:8], refs[8:]
    q_again[...] = q_ref[...]
    rows = pieces[0].shape[2]
    for h in range(2):
        for piece, (half, members) in zip(pieces[4 * h : 4 * h + 4], owners):
            for i, km in enumerate(members):
                for k in range(nz):
                    block = (h * nm + (ids_ref[1] ^ km)) * nz + (ids_ref[2] ^ k)
                    start = block * (2 * rows) + half * rows
                    p_all[pl.ds(pl.multiple_of(start, rows), rows), :] = piece[i, k]
    inv_hi = inv_ref[...].T.astype(BF16)
    inv_lo = (inv_ref[...].T - inv_hi.astype(F32)).astype(BF16)
    inv = jnp.concatenate([inv_hi, inv_hi, inv_lo, inv_lo], axis=0)
    tile = p_all.shape[0] // 8

    @pl.loop(0, 8)
    def _(i):
        at = pl.ds(pl.multiple_of(i * tile, tile), tile)
        x = p_all[at, :]
        hi = x.astype(BF16)
        lo = (x - hi.astype(F32)).astype(BF16)
        y = dot(jnp.concatenate([hi, lo, hi, lo], axis=1), inv)
        y_hi = y.astype(BF16)
        y_lo = (y - y_hi.astype(F32)).astype(BF16)
        out_ref[at, :] = jnp.concatenate([y_hi, y_lo], axis=1)


def left_factor(ids, pieces, owners, inv, rows, nm, nz, q_own, after):
    return pl.pallas_call(
        functools.partial(p_hat_kernel, owners, nm, nz),
        grid_spec=pltpu.PrefetchScalarGridSpec(
            num_scalar_prefetch=1,
            grid=(),
            in_specs=[pl.BlockSpec(memory_space=pltpu.VMEM)] * 11,
            out_specs=[pl.BlockSpec(memory_space=pltpu.VMEM)] * 2,
            scratch_shapes=[pltpu.VMEM((rows, RANK), F32)],
        ),
        out_shape=[jax.ShapeDtypeStruct((rows, 2 * RANK), BF16), jax.ShapeDtypeStruct(q_own.shape, F32)],
        compiler_params=params(SMALL_LIMIT),
        cost_estimate=cost(8 * rows * RANK * RANK, rows * RANK * 8),
        name="left_factor",
    )(ids, q_own, after, *pieces, inv)


def final_kernel(nz, scale, ids_ref, *refs):
    pieces, refs = refs[: 2 * nz], refs[2 * nz :]
    inv_ref, phat_ref, parts = refs[0], refs[1], refs[2:10]
    err_ref, qnew_hbm, q_sum, q_cat, qnew_ref, sem = refs[10:]
    small = pieces[0].shape[0]
    for h in range(2):
        for k in range(nz):
            block = (ids_ref[0] ^ h) * nz + (ids_ref[2] ^ k)
            q_sum[pl.ds(pl.multiple_of(block * small, small), small), :] = pieces[h * nz + k][...]
    q_t = scale * lax.dot_general(
        inv_ref[...], q_sum[...], (((1,), (0,)), ((), ())), precision=HIGHEST, preferred_element_type=F32
    )
    hi = q_t.astype(BF16)
    lo = (q_t - hi.astype(F32)).astype(BF16)
    q_cat[...] = jnp.concatenate([hi, hi, lo, lo], axis=0)
    qnew_ref[...] = q_t.T
    copy = pltpu.make_async_copy(qnew_ref, qnew_hbm, sem)
    copy.start()
    part_rows, cols = parts[0].shape
    chunk = min(cols, 1024)
    width = min(cols, 512)
    own = ids_ref[0]

    def body(out_tile):
        for number, merged in enumerate(parts):

            @pl.when(pl.program_id(0) == number)
            def _():
                x = phat_ref[pl.ds(number * part_rows, part_rows), :]
                x = jnp.concatenate([x, x], axis=1)
                for i in range(chunk // width):
                    start = pl.multiple_of(pl.program_id(1) * chunk + i * width, width)
                    here = pl.ds(start, width)
                    value = merged[:, here] - dot(x, q_cat[:, here])
                    out_tile[0, :, pl.ds(i * width, width)] = value.astype(BF16)

    pltpu.emit_pipeline(
        body,
        grid=(len(parts), cols // chunk),
        in_specs=[],
        out_specs=[pl.BlockSpec((1, part_rows, chunk), lambda i, j: (0, i ^ (own * 4), j))],
    )(err_ref)
    copy.wait()


def finish(ids, pieces, inv, phat, parts, replicas):
    nz = len(pieces) // 2
    part_rows, cols = parts[0].shape
    rows = part_rows * len(parts)
    vmem = pl.BlockSpec(memory_space=pltpu.VMEM)
    hbm = pl.BlockSpec(memory_space=pltpu.HBM)
    return pl.pallas_call(
        functools.partial(final_kernel, nz, 1.0 / replicas),
        grid_spec=pltpu.PrefetchScalarGridSpec(
            num_scalar_prefetch=1,
            grid=(),
            in_specs=[vmem] * (2 * nz + 2 + len(parts)),
            out_specs=[hbm, hbm],
            scratch_shapes=[
                pltpu.VMEM((RANK, cols), F32),
                pltpu.VMEM((4 * RANK, cols), BF16),
                pltpu.VMEM((cols, RANK), F32),
                pltpu.SemaphoreType.DMA,
            ],
        ),
        out_shape=[jax.ShapeDtypeStruct((1, rows, cols), BF16), jax.ShapeDtypeStruct((cols, RANK), F32)],
        compiler_params=params(FINAL_LIMIT),
        cost_estimate=cost(8 * rows * cols * RANK, rows * cols * 6),
        name="new_error",
    )(ids, *pieces, inv, phat, *parts)


def q_sum_kernel(nz, *refs):
    keep, came, outs = refs[0], refs[1], refs[2:]
    for k in range(nz):
        outs[k][...] = keep[k] + came[k]


def per_device(n_dp, n_mp, activations, out_grads, error_fb, q_prev):
    a, g, e, q = [
        pltpu.with_memory_space_constraint(x, pltpu.HBM) for x in (activations[0], out_grads[0], error_fb[0], q_prev)
    ]
    rows = a.shape[1]
    nz = n_dp // 2
    dp, mp = lax.axis_index("dp"), lax.axis_index("mp")
    ids = jnp.stack([dp % 2, mp, dp // 2]).astype(jnp.int32)
    bits = list(range(n_mp.bit_length() - 1))
    orders = [bits, bits[::-1]]

    def to_core(x):
        return lax.ppermute(x, "dp", [(i, i ^ 1) for i in range(n_dp)])

    def to_z(x, k):
        return lax.ppermute(x, "dp", [(i, i ^ (2 * k)) for i in range(n_dp)])

    def to_mp(x, k):
        return lax.ppermute(x, "mp", [(i, i ^ k) for i in range(n_mp)])

    p_far, a_far, e_far, g_here, ucat, qcat = left_terms(ids, q, g, a, e, n_mp, nz)
    p_arrived = to_core(p_far)
    p_near, a_near, e_near = left_terms(ids, q, g, a, e, n_mp, nz, (ucat, qcat))
    parts = []

    def beside(sent, count=1):
        done = []
        while count and len(parts) < 7:
            number = len(parts)
            mine = (a_near, e_near) if number < 4 else (a_far, e_far)
            part, sent = merged_part(*mine, g_here, number % 4, True, sent)
            parts.append(part)
            done = [sent]
            count -= 1
        return done

    by_z = scatter_over_mp(p_near, p_arrived, to_mp, orders, beside)
    done = beside(by_z[0])
    came = [to_z(by_z[k], k) for k in range(1, nz)]
    [p_own] = in_vmem(own_sum_kernel, [(by_z[0].shape, F32)], [by_z[0], *came], "p_own", after=done)
    done = beside(p_own)
    p_pieces = [p_own] + [to_z(p_own, k) for k in range(1, nz)]
    near, owners = gather_over_mp(p_pieces, to_mp, orders, beside, done)
    done = (beside(near[0], 8) or [near[0]])[0]
    far = [to_core(x) for x in near]

    half = right_terms(ids, near, owners, a_near, e_near, g_here, n_mp, done)
    q_send, q_keep, gram = right_terms(ids, far, owners, a_far, e_far, g_here, n_mp, done, half)

    piece = (q_keep.shape[1:], F32)
    q_by_z = in_vmem(functools.partial(q_sum_kernel, nz), [piece] * nz, [q_keep, to_core(q_send)], "q_sum")
    square = ((RANK, RANK), F32)
    [inv] = in_vmem(
        chol_inverse_kernel, [square], [gram], "chol_inverse", after=[q_by_z[0]], work=cost(2 * 10**10, 10**5)
    )
    came = [to_z(q_by_z[k], k) for k in range(1, nz)]
    [q_own] = in_vmem(own_sum_kernel, [piece], [q_by_z[0], *came], "q_own", after=[inv])
    part, done = merged_part(a_far, e_far, g_here, 3, False, q_own)
    parts.append(part)
    phat, q_again = left_factor(ids, near + far, owners, inv, rows, n_mp, nz, q_own, done)
    q_near = [q_own] + [to_z(q_own, k) for k in range(1, nz)]
    q_pieces = q_near + [to_core(x) for x in [q_again] + q_near[1:]]

    new_error, q_new = finish(ids, q_pieces, inv, phat, parts, n_dp)
    return new_error, q_new


def solution(mesh):
    placed = (P("dp", None, None), P("dp", None, "mp"), P("dp", None, "mp"), P("mp", None))
    return jax.shard_map(
        functools.partial(per_device, mesh.shape["dp"], mesh.shape["mp"]),
        mesh=mesh,
        in_specs=placed,
        out_specs=(P("dp", None, "mp"), P("mp", None)),
        check_vma=False,
    )
```

```python
import functools

import jax
import jax.numpy as jnp
from jax import lax
from jax.experimental import pallas as pl
from jax.experimental.pallas import tpu as pltpu
from jax.sharding import PartitionSpec as P

F32 = jnp.float32
BF16 = jnp.bfloat16
HIGHEST = lax.Precision.HIGHEST
RANK = 128
VMEM_LIMIT = 50 * 1024 * 1024
LEFT_LIMIT = 14 * 1024 * 1024
SMALL_LIMIT = 6 * 1024 * 1024
MERGED_LIMIT = 8 * 1024 * 1024
RIGHT_LIMIT = 11 * 1024 * 1024
FINAL_LIMIT = 9 * 1024 * 1024


def params(limit=VMEM_LIMIT):
    return pltpu.CompilerParams(vmem_limit_bytes=limit)


def cost(flops, nbytes):
    return pl.CostEstimate(flops=flops, bytes_accessed=nbytes, transcendentals=0)


def split_rows(x):
    hi = x.astype(BF16)
    lo = (x - hi.astype(F32)).astype(BF16)
    return jnp.concatenate([hi, lo], axis=0)


def fold(y):
    return y[:RANK] + y[RANK:]


def dot(a, b, contract=((1,), (0,))):
    return lax.dot_general(a, b, (contract, ((), ())), preferred_element_type=F32)


ROWS_BY_ROWS = ((1,), (1,))


def skipping(count, body, *refs):
    body(*refs[count:])


def in_vmem(body, outs, args, name, limit=SMALL_LIMIT, work=None, after=()):
    args = [*after, *args]
    return pl.pallas_call(
        functools.partial(skipping, len(after), body),
        in_specs=[pl.BlockSpec(memory_space=pltpu.VMEM)] * len(args),
        out_specs=[pl.BlockSpec(memory_space=pltpu.VMEM)] * len(outs),
        out_shape=[jax.ShapeDtypeStruct(*out) for out in outs],
        compiler_params=params(limit),
        cost_estimate=work,
        name=name,
    )(*args)


STEPS = 4
AHEAD = 2


def copies_of_half(a_hbm, e_hbm, a_ref, e_ref, sems, half):
    rows = e_ref.shape[0]
    tile = rows // STEPS
    copies = []
    for i in range(STEPS):
        here = pl.ds(i * tile, tile)
        there = pl.ds(pl.multiple_of(half * rows + i * tile, tile), tile)
        copies.append(
            (
                pltpu.make_async_copy(e_hbm.at[there, :], e_ref.at[here, :], sems.at[2 * i]),
                pltpu.make_async_copy(a_hbm.at[:, there], a_ref.at[:, here], sems.at[2 * i + 1]),
            )
        )
    return copies


def start(pair):
    for copy in pair:
        copy.start()


def p_of_half(ids_ref, copies, a_ref, e_ref, ucat_ref, qcat_ref, p_ref):
    nz, small = p_ref.shape[1:3]
    tile = e_ref.shape[0] // STEPS
    for i, (e_copy, a_copy) in enumerate(copies):
        here = pl.ds(i * tile, tile)
        e_copy.wait()
        a_copy.wait()
        if i + AHEAD < STEPS:
            start(copies[i + AHEAD])
        acc = dot(qcat_ref[...], e_ref[here, :], ROWS_BY_ROWS) + dot(ucat_ref[...], a_ref[:, here])
        p_tile = fold(acc).T
        for k in range(tile // small):
            block = i * (tile // small) + k
            p_ref[(block // nz) ^ ids_ref[1], (block % nz) ^ ids_ref[2]] = p_tile[k * small : (k + 1) * small]


def far_kernel(
    ids_ref, q_hbm, g_hbm, a_hbm, e_hbm, p_ref, a_ref, e_ref, g_ref, ucat_ref, qcat_ref, q_ref, sems, first_sems
):
    tok = g_ref.shape[0]
    q_copy = pltpu.make_async_copy(q_hbm, q_ref, first_sems.at[0])
    q_copy.start()
    g_copies = []
    for i in range(2):
        at = pl.ds(i * (tok // 2), tok // 2)
        g_copies.append(pltpu.make_async_copy(g_hbm.at[at, :], g_ref.at[at, :], first_sems.at[1 + i]))
        g_copies[-1].start()
    copies = copies_of_half(a_hbm, e_hbm, a_ref, e_ref, sems, ids_ref[0] ^ 1)
    q_copy.wait()
    qcat_ref[...] = split_rows(q_ref[...].T)
    for i in range(2):
        at = pl.ds(i * (tok // 2), tok // 2)
        g_copies[i].wait()
        start(copies[i])
        ucat_ref[:, at] = split_rows(fold(dot(qcat_ref[...], g_ref[at, :], ROWS_BY_ROWS)))
    p_of_half(ids_ref, copies, a_ref, e_ref, ucat_ref, qcat_ref, p_ref)


def near_kernel(ids_ref, ucat_ref, qcat_ref, a_hbm, e_hbm, p_ref, a_ref, e_ref, sems):
    copies = copies_of_half(a_hbm, e_hbm, a_ref, e_ref, sems, ids_ref[0])
    for pair in copies[:AHEAD]:
        start(pair)
    p_of_half(ids_ref, copies, a_ref, e_ref, ucat_ref, qcat_ref, p_ref)


def left_terms(ids, q, g, a, e, nm, nz, before=None):
    tok, rows = a.shape
    cols = e.shape[1]
    vmem = pl.BlockSpec(memory_space=pltpu.VMEM)
    hbm = pl.BlockSpec(memory_space=pltpu.HBM)
    outs = [
        pltpu.VMEM((nm, nz, rows // (2 * nm * nz), RANK), F32),
        pltpu.VMEM((tok, rows // 2), BF16),
        pltpu.VMEM((rows // 2, cols), BF16),
    ]
    scratch = [pltpu.SemaphoreType.DMA((2 * STEPS,))]
    if before is None:
        body, specs, args = far_kernel, [hbm] * 4, (q, g, a, e)
        outs += [
            pltpu.VMEM((tok, cols), BF16),
            pltpu.VMEM((2 * RANK, tok), BF16),
            pltpu.VMEM((2 * RANK, cols), BF16),
        ]
        scratch = [pltpu.VMEM((cols, RANK), F32)] + scratch + [pltpu.SemaphoreType.DMA((3,))]
    else:
        body, specs, args = near_kernel, [vmem] * 2 + [hbm] * 2, (*before, a, e)
    return pl.pallas_call(
        body,
        grid_spec=pltpu.PrefetchScalarGridSpec(
            num_scalar_prefetch=1,
            grid=(),
            in_specs=specs,
            out_specs=[vmem] * len(outs),
            scratch_shapes=scratch,
        ),
        out_shape=outs,
        compiler_params=params(LEFT_LIMIT),
        cost_estimate=cost(2 * rows * RANK * (tok + cols), rows * (tok + cols)),
        name="left_terms",
    )(ids, *args)


def first_sum_kernel(keeps, sends, near_ref, far_ref, *outs):
    rows = near_ref.shape[2] // 2
    for half in range(2):
        for out, members in ((outs[2 * half], sends[half]), (outs[2 * half + 1], keeps[half])):
            for i, km in enumerate(members):
                at = (km, slice(None), pl.ds(half * rows, rows))
                out[i] = near_ref[at] + far_ref[at]


def next_sum_kernel(keeps, sends, *refs):
    ins, outs = refs[:4], refs[4:]
    for half in range(2):
        kept, came = ins[2 * half : 2 * half + 2]
        for out, places in ((outs[2 * half], sends[half]), (outs[2 * half + 1], keeps[half])):
            for i, at in enumerate(places):
                out[i] = kept[at] + came[at]


def last_sum_kernel(nz, *refs):
    ins, outs = refs[:4], refs[4:]
    rows = ins[0].shape[2]
    for k in range(nz):
        for half in range(2):
            outs[k][pl.ds(half * rows, rows), :] = ins[2 * half][0, k] + ins[2 * half + 1][0, k]


def scatter_over_mp(near, far, to_mp, orders, beside):
    nm, nz, block, _ = near.shape
    rows = block // 2
    members = [list(range(nm))] * 2
    values, done = None, ()
    for step in range(len(orders[0])):
        bits = [1 << order[step] for order in orders]
        keep_lists = [[km for km in members[h] if not km & bits[h]] for h in range(2)]
        send_lists = [[km | bits[h] for km in keep_lists[h]] for h in range(2)]
        count = len(keep_lists[0])
        outs = [((count, nz, rows, RANK), F32)] * 4
        if values is None:
            parts = in_vmem(functools.partial(first_sum_kernel, keep_lists, send_lists), outs, [near, far], "first_sum")
        else:
            keep_at = [[members[h].index(km) for km in keep_lists[h]] for h in range(2)]
            send_at = [[members[h].index(km) for km in send_lists[h]] for h in range(2)]
            parts = in_vmem(functools.partial(next_sum_kernel, keep_at, send_at), outs, values, "next_sum", after=done)
        members = keep_lists
        came = [to_mp(parts[0], bits[0]), to_mp(parts[2], bits[1])]
        done = beside(parts[1], 1 if step else 2)
        values = [parts[1], came[0], parts[3], came[1]]
    return in_vmem(functools.partial(last_sum_kernel, nz), [((block, RANK), F32)] * nz, values, "last_sum", after=done)


def own_sum_kernel(*refs):
    ins, out = refs[:-1], refs[-1]
    total = ins[0][...]
    for came in ins[1:]:
        total = total + came[...]
    out[...] = total


def own_kernel(nz, *refs):
    ins, outs = refs[:nz], refs[nz:]
    rows = outs[0].shape[2]
    for k in range(nz):
        for half in range(2):
            outs[half][0, k] = ins[k][pl.ds(half * rows, rows), :]


def grow_kernel(*refs):
    ins, outs = refs[:4], refs[4:]
    count = ins[0].shape[0]
    for half in range(2):
        outs[half][pl.ds(0, count)] = ins[2 * half][...]
        outs[half][pl.ds(count, count)] = ins[2 * half + 1][...]


def gather_over_mp(pieces, to_mp, orders, beside, done):
    nz = len(pieces)
    rows = pieces[0].shape[0] // 2
    held = in_vmem(functools.partial(own_kernel, nz), [((1, nz, rows, RANK), F32)] * 2, pieces, "own_rows", after=done)
    members = [[0], [0]]
    last = len(orders[0]) - 1
    for step in range(last, -1, -1):
        bits = [1 << order[step] for order in orders]
        came = [to_mp(held[h], bits[h]) for h in range(2)]
        came_members = [[km ^ bits[h] for km in members[h]] for h in range(2)]
        if step == 0:
            return [held[0], held[1], came[0], came[1]], [
                (0, members[0]), (1, members[1]), (0, came_members[0]), (1, came_members[1])
            ]
        count = len(members[0])
        held = in_vmem(
            grow_kernel,
            [((2 * count, nz, rows, RANK), F32)] * 2,
            [held[0], came[0], held[1], came[1]],
            "grow",
            after=beside(held[0]),
        )
        members = [members[h] + came_members[h] for h in range(2)]


def merged_kernel(part, in_hbm, after_ref, a_ref, e_ref, g_ref, out_ref, done_ref, a_t, *scratch):
    done_ref[...] = jnp.zeros_like(done_ref)
    rows, cols = out_ref.shape
    tile, chunk = rows // 2, min(cols, 512)
    held, sems = scratch if in_hbm else (out_ref, None)
    copies = []
    for i in range(2):
        at = pl.ds(i * tile, tile)
        a_t[at, :] = a_ref[:, pl.ds(part * rows + i * tile, tile)].T
        for j in range(cols // chunk):
            here = pl.ds(j * chunk, chunk)
            e_tile = e_ref[pl.ds(part * rows + i * tile, tile), here]
            held[at, here] = dot(a_t[at, :], g_ref[:, here]) + e_tile.astype(F32)
            if in_hbm:
                copy = pltpu.make_async_copy(held.at[at, here], out_ref.at[at, here], sems.at[len(copies)])
                copy.start()
                copies.append(copy)
    for copy in copies:
        copy.wait()


def merged_part(a, e, g, part, in_hbm, after):
    tok, half = a.shape
    cols = e.shape[1]
    rows = half // 4
    place = pltpu.HBM if in_hbm else pltpu.VMEM
    scratch = [pltpu.VMEM((rows, tok), BF16)]
    if in_hbm:
        scratch += [pltpu.VMEM((rows, cols), F32), pltpu.SemaphoreType.DMA((2 * (cols // min(cols, 512)),))]
    return pl.pallas_call(
        functools.partial(merged_kernel, part, in_hbm),
        in_specs=[pl.BlockSpec(memory_space=pl.ANY)] + [pl.BlockSpec(memory_space=pltpu.VMEM)] * 3,
        out_specs=[pl.BlockSpec(memory_space=place), pl.BlockSpec(memory_space=pltpu.VMEM)],
        out_shape=[place((rows, cols), F32), jax.ShapeDtypeStruct((8, RANK), F32)],
        scratch_shapes=scratch,
        compiler_params=params(MERGED_LIMIT if in_hbm else MERGED_LIMIT // 2),
        cost_estimate=cost(2 * tok * cols * rows, rows * cols * 2),
        name="merged",
    )(after, a, e, g)


def q_kernel(owners, nm, nz, last, ids_ref, after_ref, *refs):
    pieces, refs = refs[:4], refs[4:]
    if last:
        v_in, q_in, gram_in, a_ref, e_ref, g_ref, send_ref, keep_ref, gram_ref, p_half, pcat, q_acc = refs
    else:
        a_ref, e_ref, v_ref, q_acc, gram_ref, p_half, pcat = refs
    rows = pieces[0].shape[2]
    cols = e_ref.shape[1]
    chunk = min(cols, 512)
    for piece, (half, members) in zip(pieces, owners):
        for i, km in enumerate(members):
            for k in range(nz):
                start = ((ids_ref[1] ^ km) * nz + (ids_ref[2] ^ k)) * (2 * rows) + half * rows
                p_half[pl.ds(pl.multiple_of(start, rows), rows), :] = piece[i, k]
    pcat[...] = split_rows(p_half[...].T)
    v = fold(dot(pcat[...], a_ref[...], ROWS_BY_ROWS))
    gram = dot(pcat[...], pcat[...], ROWS_BY_ROWS)
    if last:
        vcat = split_rows(v + v_in[...])
        whole = fold(gram + gram_in[...])
        gram_ref[...] = whole[:, :RANK] + whole[:, RANK:]
    else:
        v_ref[...] = v
        gram_ref[...] = gram

    for i in range(cols // chunk):
        here = pl.ds(i * chunk, chunk)
        q = dot(pcat[...], e_ref[:, here])
        if last:
            q += dot(vcat, g_ref[:, here])
            q_acc[:, here] = fold(q) + q_in[:, here]
        else:
            q_acc[:, here] = fold(q)

    if last:
        small = send_ref.shape[1]
        for out, flip in ((send_ref, 1), (keep_ref, 0)):
            for k in range(nz):
                start = ((ids_ref[0] ^ flip) * nz + (ids_ref[2] ^ k)) * small
                out[k] = q_acc[pl.ds(pl.multiple_of(start, small), small), :]


def right_terms(ids, pieces, owners, a, e, g, nm, after, before=None):
    tok, half = a.shape
    cols = e.shape[1]
    nz = pieces[0].shape[1]
    last = before is not None
    vmem = pl.BlockSpec(memory_space=pltpu.VMEM)
    sums = [(RANK, tok), (RANK, cols), (2 * RANK, 2 * RANK)]
    scratch = [pltpu.VMEM((half, RANK), F32), pltpu.VMEM((2 * RANK, half), BF16)]
    if last:
        args = [*pieces, *before, a, e, g]
        outs = [(nz, RANK // (2 * nz), cols)] * 2 + [(RANK, RANK)]
        scratch += [pltpu.VMEM((RANK, cols), F32)]
    else:
        args = [*pieces, a, e]
        outs = sums
    return pl.pallas_call(
        functools.partial(q_kernel, owners, nm, nz, last),
        grid_spec=pltpu.PrefetchScalarGridSpec(
            num_scalar_prefetch=1,
            grid=(),
            in_specs=[pl.BlockSpec(memory_space=pl.ANY)] + [vmem] * len(args),
            out_specs=[vmem] * 3,
            scratch_shapes=scratch,
        ),
        out_shape=[jax.ShapeDtypeStruct(shape, F32) for shape in outs],
        compiler_params=params(RIGHT_LIMIT),
        cost_estimate=cost(4 * half * RANK * (tok + cols), half * (tok + cols)),
        name="right_terms",
    )(ids, after, *args)


def chol_inverse_kernel(gram_ref, out_ref):
    left = gram_ref[...]
    row = lax.broadcasted_iota(jnp.int32, (RANK, RANK), 0)
    right = (row == lax.broadcasted_iota(jnp.int32, (RANK, RANK), 1)).astype(F32)
    for j in range(RANK):
        at = j % 8
        if j and at == 0:
            left, right = left[8:], right[8:]
        pivot_row, own = left[at : at + 1], right[at : at + 1]
        pivot = pivot_row[:, j : j + 1]
        out_ref[j : j + 1, :] = own * (1.0 / jnp.sqrt(pivot))
        inverse = 1.0 / pivot
        below = row[: left.shape[0], :1] > at
        factor = jnp.where(below, left[:, j : j + 1], 0.0)
        left = left - factor * (pivot_row * inverse)
        right = right - factor * (own * inverse)


def p_hat_kernel(owners, nm, nz, ids_ref, q_ref, after_ref, *refs):
    pieces, (inv_ref, out_ref, q_again, p_all) = refs[:8], refs[8:]
    q_again[...] = q_ref[...]
    rows = pieces[0].shape[2]
    for h in range(2):
        for piece, (half, members) in zip(pieces[4 * h : 4 * h + 4], owners):
            for i, km in enumerate(members):
                for k in range(nz):
                    block = (h * nm + (ids_ref[1] ^ km)) * nz + (ids_ref[2] ^ k)
                    start = block * (2 * rows) + half * rows
                    p_all[pl.ds(pl.multiple_of(start, rows), rows), :] = piece[i, k]
    inv_hi = inv_ref[...].T.astype(BF16)
    inv_lo = (inv_ref[...].T - inv_hi.astype(F32)).astype(BF16)
    inv = jnp.concatenate([inv_hi, inv_hi, inv_lo, inv_lo], axis=0)
    tile = p_all.shape[0] // 8

    @pl.loop(0, 8)
    def _(i):
        at = pl.ds(pl.multiple_of(i * tile, tile), tile)
        x = p_all[at, :]
        hi = x.astype(BF16)
        lo = (x - hi.astype(F32)).astype(BF16)
        y = dot(jnp.concatenate([hi, lo, hi, lo], axis=1), inv)
        y_hi = y.astype(BF16)
        y_lo = (y - y_hi.astype(F32)).astype(BF16)
        out_ref[at, :] = jnp.concatenate([y_hi, y_lo], axis=1)


def left_factor(ids, pieces, owners, inv, rows, nm, nz, q_own, after):
    return pl.pallas_call(
        functools.partial(p_hat_kernel, owners, nm, nz),
        grid_spec=pltpu.PrefetchScalarGridSpec(
            num_scalar_prefetch=1,
            grid=(),
            in_specs=[pl.BlockSpec(memory_space=pltpu.VMEM)] * 11,
            out_specs=[pl.BlockSpec(memory_space=pltpu.VMEM)] * 2,
            scratch_shapes=[pltpu.VMEM((rows, RANK), F32)],
        ),
        out_shape=[jax.ShapeDtypeStruct((rows, 2 * RANK), BF16), jax.ShapeDtypeStruct(q_own.shape, F32)],
        compiler_params=params(SMALL_LIMIT),
        cost_estimate=cost(8 * rows * RANK * RANK, rows * RANK * 8),
        name="left_factor",
    )(ids, q_own, after, *pieces, inv)


def final_kernel(nz, scale, ids_ref, *refs):
    pieces, refs = refs[: 2 * nz], refs[2 * nz :]
    inv_ref, phat_ref, parts = refs[0], refs[1], refs[2:10]
    err_ref, qnew_hbm, q_sum, q_cat, qnew_ref, sem, held, sems = refs[10:]
    small = pieces[0].shape[0]
    for h in range(2):
        for k in range(nz):
            block = (ids_ref[0] ^ h) * nz + (ids_ref[2] ^ k)
            q_sum[pl.ds(pl.multiple_of(block * small, small), small), :] = pieces[h * nz + k][...]
    q_t = scale * lax.dot_general(
        inv_ref[...], q_sum[...], (((1,), (0,)), ((), ())), precision=HIGHEST, preferred_element_type=F32
    )
    hi = q_t.astype(BF16)
    lo = (q_t - hi.astype(F32)).astype(BF16)
    q_cat[...] = jnp.concatenate([hi, hi, lo, lo], axis=0)
    part_rows, cols = parts[0].shape
    chunk = min(cols, 512)
    tile = part_rows // 2
    slots = held.shape[0]
    copies = []
    for number, merged in enumerate(parts):
        for i in range(2):
            at = pl.ds(i * tile, tile)
            slot = len(copies) % slots
            if len(copies) >= slots:
                copies[-slots].wait()
            x = phat_ref[pl.ds(number * part_rows + i * tile, tile), :]
            x = jnp.concatenate([x, x], axis=1)
            for j in range(cols // chunk):
                here = pl.ds(j * chunk, chunk)
                held[slot, :, here] = (merged[at, here] - dot(x, q_cat[:, here])).astype(BF16)
            row = pl.multiple_of((number ^ (ids_ref[0] * 4)) * part_rows + i * tile, tile)
            copies.append(
                pltpu.make_async_copy(held.at[slot], err_ref.at[0, pl.ds(row, tile), :], sems.at[slot])
            )
            copies[-1].start()
        if number == 0:
            qnew_ref[...] = q_t.T
            copy = pltpu.make_async_copy(qnew_ref, qnew_hbm, sem)
            copy.start()
    for last in copies[-slots:]:
        last.wait()
    copy.wait()


def finish(ids, pieces, inv, phat, parts, replicas):
    nz = len(pieces) // 2
    part_rows, cols = parts[0].shape
    rows = part_rows * len(parts)
    vmem = pl.BlockSpec(memory_space=pltpu.VMEM)
    hbm = pl.BlockSpec(memory_space=pltpu.HBM)
    return pl.pallas_call(
        functools.partial(final_kernel, nz, 1.0 / replicas),
        grid_spec=pltpu.PrefetchScalarGridSpec(
            num_scalar_prefetch=1,
            grid=(),
            in_specs=[vmem] * (2 * nz + 2 + len(parts)),
            out_specs=[hbm, hbm],
            scratch_shapes=[
                pltpu.VMEM((RANK, cols), F32),
                pltpu.VMEM((4 * RANK, cols), BF16),
                pltpu.VMEM((cols, RANK), F32),
                pltpu.SemaphoreType.DMA,
                pltpu.VMEM((4, part_rows // 2, cols), BF16),
                pltpu.SemaphoreType.DMA((4,)),
            ],
        ),
        out_shape=[jax.ShapeDtypeStruct((1, rows, cols), BF16), jax.ShapeDtypeStruct((cols, RANK), F32)],
        compiler_params=params(FINAL_LIMIT),
        cost_estimate=cost(8 * rows * cols * RANK, rows * cols * 6),
        name="new_error",
    )(ids, *pieces, inv, phat, *parts)


def q_sum_kernel(nz, *refs):
    keep, came, outs = refs[0], refs[1], refs[2:]
    for k in range(nz):
        outs[k][...] = keep[k] + came[k]


def per_device(n_dp, n_mp, activations, out_grads, error_fb, q_prev):
    a, g, e, q = [
        pltpu.with_memory_space_constraint(x, pltpu.HBM) for x in (activations[0], out_grads[0], error_fb[0], q_prev)
    ]
    rows = a.shape[1]
    nz = n_dp // 2
    dp, mp = lax.axis_index("dp"), lax.axis_index("mp")
    ids = jnp.stack([dp % 2, mp, dp // 2]).astype(jnp.int32)
    bits = list(range(n_mp.bit_length() - 1))
    orders = [bits, bits[::-1]]

    def to_core(x):
        return lax.ppermute(x, "dp", [(i, i ^ 1) for i in range(n_dp)])

    def to_z(x, k):
        return lax.ppermute(x, "dp", [(i, i ^ (2 * k)) for i in range(n_dp)])

    def to_mp(x, k):
        return lax.ppermute(x, "mp", [(i, i ^ k) for i in range(n_mp)])

    p_far, a_far, e_far, g_here, ucat, qcat = left_terms(ids, q, g, a, e, n_mp, nz)
    p_arrived = to_core(p_far)
    p_near, a_near, e_near = left_terms(ids, q, g, a, e, n_mp, nz, (ucat, qcat))
    parts = []

    def beside(sent, count=1):
        done = []
        while count and len(parts) < 7:
            number = len(parts)
            mine = (a_near, e_near) if number < 4 else (a_far, e_far)
            part, sent = merged_part(*mine, g_here, number % 4, True, sent)
            parts.append(part)
            done = [sent]
            count -= 1
        return done

    by_z = scatter_over_mp(p_near, p_arrived, to_mp, orders, beside)
    done = beside(by_z[0])
    came = [to_z(by_z[k], k) for k in range(1, nz)]
    [p_own] = in_vmem(own_sum_kernel, [(by_z[0].shape, F32)], [by_z[0], *came], "p_own", after=done)
    done = beside(p_own)
    p_pieces = [p_own] + [to_z(p_own, k) for k in range(1, nz)]
    near, owners = gather_over_mp(p_pieces, to_mp, orders, beside, done)
    done = (beside(near[0], 8) or [near[0]])[0]
    far = [to_core(x) for x in near]

    half = right_terms(ids, near, owners, a_near, e_near, g_here, n_mp, done)
    q_send, q_keep, gram = right_terms(ids, far, owners, a_far, e_far, g_here, n_mp, done, half)

    piece = (q_keep.shape[1:], F32)
    q_by_z = in_vmem(functools.partial(q_sum_kernel, nz), [piece] * nz, [q_keep, to_core(q_send)], "q_sum")
    square = ((RANK, RANK), F32)
    [inv] = in_vmem(
        chol_inverse_kernel, [square], [gram], "chol_inverse", after=[q_by_z[0]], work=cost(2 * 10**10, 10**5)
    )
    came = [to_z(q_by_z[k], k) for k in range(1, nz)]
    [q_own] = in_vmem(own_sum_kernel, [piece], [q_by_z[0], *came], "q_own", after=[inv])
    part, done = merged_part(a_far, e_far, g_here, 3, False, q_own)
    parts.append(part)
    phat, q_again = left_factor(ids, near + far, owners, inv, rows, n_mp, nz, q_own, done)
    q_near = [q_own] + [to_z(q_own, k) for k in range(1, nz)]
    q_pieces = q_near + [to_core(x) for x in [q_again] + q_near[1:]]

    new_error, q_new = finish(ids, q_pieces, inv, phat, parts, n_dp)
    return new_error, q_new


def solution(mesh):
    placed = (P("dp", None, None), P("dp", None, "mp"), P("dp", None, "mp"), P("mp", None))
    return jax.shard_map(
        functools.partial(per_device, mesh.shape["dp"], mesh.shape["mp"]),
        mesh=mesh,
        in_specs=placed,
        out_specs=(P("dp", None, "mp"), P("mp", None)),
        check_vma=False,
    )
```

```python
import functools

import jax
import jax.numpy as jnp
from jax import lax
from jax.experimental import pallas as pl
from jax.experimental.pallas import tpu as pltpu
from jax.sharding import PartitionSpec as P

F32 = jnp.float32
BF16 = jnp.bfloat16
HIGHEST = lax.Precision.HIGHEST
RANK = 128
VMEM_LIMIT = 50 * 1024 * 1024
LEFT_LIMIT = 14 * 1024 * 1024
SMALL_LIMIT = 6 * 1024 * 1024
MERGED_LIMIT = 8 * 1024 * 1024
RIGHT_LIMIT = 11 * 1024 * 1024
FINAL_LIMIT = 9 * 1024 * 1024


def params(limit=VMEM_LIMIT):
    return pltpu.CompilerParams(vmem_limit_bytes=limit)


def cost(flops, nbytes):
    return pl.CostEstimate(flops=flops, bytes_accessed=nbytes, transcendentals=0)


def split_rows(x):
    hi = x.astype(BF16)
    lo = (x - hi.astype(F32)).astype(BF16)
    return jnp.concatenate([hi, lo], axis=0)


def fold(y):
    return y[:RANK] + y[RANK:]


def dot(a, b, contract=((1,), (0,))):
    return lax.dot_general(a, b, (contract, ((), ())), preferred_element_type=F32)


ROWS_BY_ROWS = ((1,), (1,))


def skipping(count, body, *refs):
    body(*refs[count:])


def in_vmem(body, outs, args, name, limit=SMALL_LIMIT, work=None, after=()):
    args = [*after, *args]
    return pl.pallas_call(
        functools.partial(skipping, len(after), body),
        in_specs=[pl.BlockSpec(memory_space=pltpu.VMEM)] * len(args),
        out_specs=[pl.BlockSpec(memory_space=pltpu.VMEM)] * len(outs),
        out_shape=[jax.ShapeDtypeStruct(*out) for out in outs],
        compiler_params=params(limit),
        cost_estimate=work,
        name=name,
    )(*args)


STEPS = 4
AHEAD = 2


def copies_of_half(a_hbm, e_hbm, a_ref, e_ref, sems, half):
    rows = e_ref.shape[0]
    tile = rows // STEPS
    copies = []
    for i in range(STEPS):
        here = pl.ds(i * tile, tile)
        there = pl.ds(pl.multiple_of(half * rows + i * tile, tile), tile)
        copies.append(
            (
                pltpu.make_async_copy(e_hbm.at[there, :], e_ref.at[here, :], sems.at[2 * i]),
                pltpu.make_async_copy(a_hbm.at[:, there], a_ref.at[:, here], sems.at[2 * i + 1]),
            )
        )
    return copies


def start(pair):
    for copy in pair:
        copy.start()


def p_of_half(ids_ref, copies, a_ref, e_ref, ucat_ref, qcat_ref, p_ref):
    nz, small = p_ref.shape[1:3]
    tile = e_ref.shape[0] // STEPS
    for i, (e_copy, a_copy) in enumerate(copies):
        here = pl.ds(i * tile, tile)
        e_copy.wait()
        a_copy.wait()
        if i + AHEAD < STEPS:
            start(copies[i + AHEAD])
        acc = dot(qcat_ref[...], e_ref[here, :], ROWS_BY_ROWS) + dot(ucat_ref[...], a_ref[:, here])
        p_tile = fold(acc).T
        for k in range(tile // small):
            block = i * (tile // small) + k
            p_ref[(block // nz) ^ ids_ref[1], (block % nz) ^ ids_ref[2]] = p_tile[k * small : (k + 1) * small]


def far_kernel(
    ids_ref, q_hbm, g_hbm, a_hbm, e_hbm, p_ref, a_ref, e_ref, g_ref, ucat_ref, qcat_ref, q_ref, sems, first_sems
):
    tok = g_ref.shape[0]
    q_copy = pltpu.make_async_copy(q_hbm, q_ref, first_sems.at[0])
    q_copy.start()
    g_copies = []
    for i in range(2):
        at = pl.ds(i * (tok // 2), tok // 2)
        g_copies.append(pltpu.make_async_copy(g_hbm.at[at, :], g_ref.at[at, :], first_sems.at[1 + i]))
        g_copies[-1].start()
    copies = copies_of_half(a_hbm, e_hbm, a_ref, e_ref, sems, ids_ref[0] ^ 1)
    q_copy.wait()
    qcat_ref[...] = split_rows(q_ref[...].T)
    for i in range(2):
        at = pl.ds(i * (tok // 2), tok // 2)
        g_copies[i].wait()
        start(copies[i])
        ucat_ref[:, at] = split_rows(fold(dot(qcat_ref[...], g_ref[at, :], ROWS_BY_ROWS)))
    p_of_half(ids_ref, copies, a_ref, e_ref, ucat_ref, qcat_ref, p_ref)


def near_kernel(ids_ref, ucat_ref, qcat_ref, a_hbm, e_hbm, p_ref, a_ref, e_ref, sems):
    copies = copies_of_half(a_hbm, e_hbm, a_ref, e_ref, sems, ids_ref[0])
    for pair in copies[:AHEAD]:
        start(pair)
    p_of_half(ids_ref, copies, a_ref, e_ref, ucat_ref, qcat_ref, p_ref)


def left_terms(ids, q, g, a, e, nm, nz, before=None):
    tok, rows = a.shape
    cols = e.shape[1]
    vmem = pl.BlockSpec(memory_space=pltpu.VMEM)
    hbm = pl.BlockSpec(memory_space=pltpu.HBM)
    outs = [
        pltpu.VMEM((nm, nz, rows // (2 * nm * nz), RANK), F32),
        pltpu.VMEM((tok, rows // 2), BF16),
        pltpu.VMEM((rows // 2, cols), BF16),
    ]
    scratch = [pltpu.SemaphoreType.DMA((2 * STEPS,))]
    if before is None:
        body, specs, args = far_kernel, [hbm] * 4, (q, g, a, e)
        outs += [
            pltpu.VMEM((tok, cols), BF16),
            pltpu.VMEM((2 * RANK, tok), BF16),
            pltpu.VMEM((2 * RANK, cols), BF16),
        ]
        scratch = [pltpu.VMEM((cols, RANK), F32)] + scratch + [pltpu.SemaphoreType.DMA((3,))]
    else:
        body, specs, args = near_kernel, [vmem] * 2 + [hbm] * 2, (*before, a, e)
    return pl.pallas_call(
        body,
        grid_spec=pltpu.PrefetchScalarGridSpec(
            num_scalar_prefetch=1,
            grid=(),
            in_specs=specs,
            out_specs=[vmem] * len(outs),
            scratch_shapes=scratch,
        ),
        out_shape=outs,
        compiler_params=params(LEFT_LIMIT),
        cost_estimate=cost(2 * rows * RANK * (tok + cols), rows * (tok + cols)),
        name="left_terms",
    )(ids, *args)


def first_sum_kernel(keeps, sends, near_ref, far_ref, *outs):
    rows = near_ref.shape[2] // 2
    for half in range(2):
        for out, members in ((outs[2 * half], sends[half]), (outs[2 * half + 1], keeps[half])):
            for i, km in enumerate(members):
                at = (km, slice(None), pl.ds(half * rows, rows))
                out[i] = near_ref[at] + far_ref[at]


def next_sum_kernel(keeps, sends, *refs):
    ins, outs = refs[:4], refs[4:]
    for half in range(2):
        kept, came = ins[2 * half : 2 * half + 2]
        for out, places in ((outs[2 * half], sends[half]), (outs[2 * half + 1], keeps[half])):
            for i, at in enumerate(places):
                out[i] = kept[at] + came[at]


def last_sum_kernel(nz, *refs):
    ins, outs = refs[:4], refs[4:]
    rows = ins[0].shape[2]
    for k in range(nz):
        for half in range(2):
            outs[k][pl.ds(half * rows, rows), :] = ins[2 * half][0, k] + ins[2 * half + 1][0, k]


def scatter_over_mp(near, far, to_mp, orders, beside):
    nm, nz, block, _ = near.shape
    rows = block // 2
    members = [list(range(nm))] * 2
    values, done = None, ()
    for step in range(len(orders[0])):
        bits = [1 << order[step] for order in orders]
        keep_lists = [[km for km in members[h] if not km & bits[h]] for h in range(2)]
        send_lists = [[km | bits[h] for km in keep_lists[h]] for h in range(2)]
        count = len(keep_lists[0])
        outs = [((count, nz, rows, RANK), F32)] * 4
        if values is None:
            parts = in_vmem(functools.partial(first_sum_kernel, keep_lists, send_lists), outs, [near, far], "first_sum")
        else:
            keep_at = [[members[h].index(km) for km in keep_lists[h]] for h in range(2)]
            send_at = [[members[h].index(km) for km in send_lists[h]] for h in range(2)]
            parts = in_vmem(functools.partial(next_sum_kernel, keep_at, send_at), outs, values, "next_sum", after=done)
        members = keep_lists
        came = [to_mp(parts[0], bits[0]), to_mp(parts[2], bits[1])]
        done = beside(parts[1], 1 if step else 2)
        values = [parts[1], came[0], parts[3], came[1]]
    return in_vmem(functools.partial(last_sum_kernel, nz), [((block, RANK), F32)] * nz, values, "last_sum", after=done)


def own_sum_kernel(*refs):
    ins, out = refs[:-1], refs[-1]
    total = ins[0][...]
    for came in ins[1:]:
        total = total + came[...]
    out[...] = total


def own_kernel(nz, *refs):
    ins, outs = refs[:nz], refs[nz:]
    rows = outs[0].shape[2]
    for k in range(nz):
        for half in range(2):
            outs[half][0, k] = ins[k][pl.ds(half * rows, rows), :]


def grow_kernel(*refs):
    ins, outs = refs[:4], refs[4:]
    count = ins[0].shape[0]
    for half in range(2):
        outs[half][pl.ds(0, count)] = ins[2 * half][...]
        outs[half][pl.ds(count, count)] = ins[2 * half + 1][...]


def gather_over_mp(pieces, to_mp, orders, beside, done):
    nz = len(pieces)
    rows = pieces[0].shape[0] // 2
    held = in_vmem(functools.partial(own_kernel, nz), [((1, nz, rows, RANK), F32)] * 2, pieces, "own_rows", after=done)
    members = [[0], [0]]
    last = len(orders[0]) - 1
    for step in range(last, -1, -1):
        bits = [1 << order[step] for order in orders]
        came = [to_mp(held[h], bits[h]) for h in range(2)]
        came_members = [[km ^ bits[h] for km in members[h]] for h in range(2)]
        if step == 0:
            return [held[0], held[1], came[0], came[1]], [
                (0, members[0]), (1, members[1]), (0, came_members[0]), (1, came_members[1])
            ]
        count = len(members[0])
        held = in_vmem(
            grow_kernel,
            [((2 * count, nz, rows, RANK), F32)] * 2,
            [held[0], came[0], held[1], came[1]],
            "grow",
            after=beside(held[0]),
        )
        members = [members[h] + came_members[h] for h in range(2)]


def merged_kernel(part, in_hbm, after_ref, a_ref, e_ref, g_ref, out_ref, done_ref, a_t, *scratch):
    done_ref[...] = jnp.zeros_like(done_ref)
    rows, cols = out_ref.shape
    tile, chunk = rows // 2, min(cols, 512)
    held, sems = scratch if in_hbm else (out_ref, None)
    copies = []
    for i in range(2):
        at = pl.ds(i * tile, tile)
        a_t[at, :] = a_ref[:, pl.ds(part * rows + i * tile, tile)].T
        for j in range(cols // chunk):
            here = pl.ds(j * chunk, chunk)
            e_tile = e_ref[pl.ds(part * rows + i * tile, tile), here]
            held[at, here] = dot(a_t[at, :], g_ref[:, here]) + e_tile.astype(F32)
            if in_hbm:
                copy = pltpu.make_async_copy(held.at[at, here], out_ref.at[at, here], sems.at[len(copies)])
                copy.start()
                copies.append(copy)
    for copy in copies:
        copy.wait()


def merged_part(a, e, g, part, in_hbm, after):
    tok, half = a.shape
    cols = e.shape[1]
    rows = half // 4
    place = pltpu.HBM if in_hbm else pltpu.VMEM
    scratch = [pltpu.VMEM((rows, tok), BF16)]
    if in_hbm:
        scratch += [pltpu.VMEM((rows, cols), F32), pltpu.SemaphoreType.DMA((2 * (cols // min(cols, 512)),))]
    return pl.pallas_call(
        functools.partial(merged_kernel, part, in_hbm),
        in_specs=[pl.BlockSpec(memory_space=pl.ANY)] + [pl.BlockSpec(memory_space=pltpu.VMEM)] * 3,
        out_specs=[pl.BlockSpec(memory_space=place), pl.BlockSpec(memory_space=pltpu.VMEM)],
        out_shape=[place((rows, cols), F32), jax.ShapeDtypeStruct((8, RANK), F32)],
        scratch_shapes=scratch,
        compiler_params=params(MERGED_LIMIT if in_hbm else MERGED_LIMIT // 2),
        cost_estimate=cost(2 * tok * cols * rows, rows * cols * 2),
        name="merged",
    )(after, a, e, g)


def q_kernel(owners, nm, nz, last, ids_ref, after_ref, *refs):
    pieces, refs = refs[:4], refs[4:]
    if last:
        v_in, q_in, gram_in, a_ref, e_ref, g_ref, send_ref, keep_ref, gram_ref, p_half, pcat, q_acc = refs
    else:
        a_ref, e_ref, v_ref, q_acc, gram_ref, p_half, pcat = refs
    rows = pieces[0].shape[2]
    cols = e_ref.shape[1]
    chunk = min(cols, 512)
    for piece, (half, members) in zip(pieces, owners):
        for i, km in enumerate(members):
            for k in range(nz):
                start = ((ids_ref[1] ^ km) * nz + (ids_ref[2] ^ k)) * (2 * rows) + half * rows
                p_half[pl.ds(pl.multiple_of(start, rows), rows), :] = piece[i, k]
    pcat[...] = split_rows(p_half[...].T)
    v = fold(dot(pcat[...], a_ref[...], ROWS_BY_ROWS))
    gram = dot(pcat[...], pcat[...], ROWS_BY_ROWS)
    if last:
        vcat = split_rows(v + v_in[...])
        whole = fold(gram + gram_in[...])
        gram_ref[...] = whole[:, :RANK] + whole[:, RANK:]
    else:
        v_ref[...] = v
        gram_ref[...] = gram

    for i in range(cols // chunk):
        here = pl.ds(i * chunk, chunk)
        q = dot(pcat[...], e_ref[:, here])
        if last:
            q += dot(vcat, g_ref[:, here])
            q_acc[:, here] = fold(q) + q_in[:, here]
        else:
            q_acc[:, here] = fold(q)

    if last:
        small = send_ref.shape[1]
        for out, flip in ((send_ref, 1), (keep_ref, 0)):
            for k in range(nz):
                start = ((ids_ref[0] ^ flip) * nz + (ids_ref[2] ^ k)) * small
                out[k] = q_acc[pl.ds(pl.multiple_of(start, small), small), :]


def right_terms(ids, pieces, owners, a, e, g, nm, after, before=None):
    tok, half = a.shape
    cols = e.shape[1]
    nz = pieces[0].shape[1]
    last = before is not None
    vmem = pl.BlockSpec(memory_space=pltpu.VMEM)
    sums = [(RANK, tok), (RANK, cols), (2 * RANK, 2 * RANK)]
    scratch = [pltpu.VMEM((half, RANK), F32), pltpu.VMEM((2 * RANK, half), BF16)]
    if last:
        args = [*pieces, *before, a, e, g]
        outs = [(nz, RANK // (2 * nz), cols)] * 2 + [(RANK, RANK)]
        scratch += [pltpu.VMEM((RANK, cols), F32)]
    else:
        args = [*pieces, a, e]
        outs = sums
    return pl.pallas_call(
        functools.partial(q_kernel, owners, nm, nz, last),
        grid_spec=pltpu.PrefetchScalarGridSpec(
            num_scalar_prefetch=1,
            grid=(),
            in_specs=[pl.BlockSpec(memory_space=pl.ANY)] + [vmem] * len(args),
            out_specs=[vmem] * 3,
            scratch_shapes=scratch,
        ),
        out_shape=[jax.ShapeDtypeStruct(shape, F32) for shape in outs],
        compiler_params=params(RIGHT_LIMIT),
        cost_estimate=cost(4 * half * RANK * (tok + cols), half * (tok + cols)),
        name="right_terms",
    )(ids, after, *args)


def chol_inverse_kernel(gram_ref, out_ref):
    left = gram_ref[...]
    row = lax.broadcasted_iota(jnp.int32, (RANK, RANK), 0)
    right = (row == lax.broadcasted_iota(jnp.int32, (RANK, RANK), 1)).astype(F32)
    for j in range(0, RANK, 2):
        at = j % 8
        if j and at == 0:
            left, right = left[8:], right[8:]
        first, second = left[at : at + 1], left[at + 1 : at + 2]
        own, other = right[at : at + 1], right[at + 1 : at + 2]
        pivot = first[:, j : j + 1]
        inverse = 1.0 / pivot
        ratio = second[:, j : j + 1] * inverse
        second = second - ratio * first
        other = other - ratio * own
        pivot2 = second[:, j + 1 : j + 2]
        inverse2 = 1.0 / pivot2
        out_ref[j : j + 1, :] = own * (1.0 / jnp.sqrt(pivot))
        out_ref[j + 1 : j + 2, :] = other * (1.0 / jnp.sqrt(pivot2))
        below = row[: left.shape[0], :1] > at + 1
        factor = jnp.where(below, left[:, j : j + 1] * inverse, 0.0)
        factor2 = jnp.where(below, left[:, j + 1 : j + 2], 0.0) - factor * first[:, j + 1 : j + 2]
        factor2 = factor2 * inverse2
        left = left - factor * first - factor2 * second
        right = right - factor * own - factor2 * other


def p_hat_kernel(owners, nm, nz, ids_ref, q_ref, after_ref, *refs):
    pieces, (inv_ref, out_ref, q_again, p_all) = refs[:8], refs[8:]
    q_again[...] = q_ref[...]
    rows = pieces[0].shape[2]
    for h in range(2):
        for piece, (half, members) in zip(pieces[4 * h : 4 * h + 4], owners):
            for i, km in enumerate(members):
                for k in range(nz):
                    block = (h * nm + (ids_ref[1] ^ km)) * nz + (ids_ref[2] ^ k)
                    start = block * (2 * rows) + half * rows
                    p_all[pl.ds(pl.multiple_of(start, rows), rows), :] = piece[i, k]
    inv_hi = inv_ref[...].T.astype(BF16)
    inv_lo = (inv_ref[...].T - inv_hi.astype(F32)).astype(BF16)
    inv = jnp.concatenate([inv_hi, inv_hi, inv_lo, inv_lo], axis=0)
    tile = p_all.shape[0] // 8

    @pl.loop(0, 8)
    def _(i):
        at = pl.ds(pl.multiple_of(i * tile, tile), tile)
        x = p_all[at, :]
        hi = x.astype(BF16)
        lo = (x - hi.astype(F32)).astype(BF16)
        y = dot(jnp.concatenate([hi, lo, hi, lo], axis=1), inv)
        y_hi = y.astype(BF16)
        y_lo = (y - y_hi.astype(F32)).astype(BF16)
        out_ref[at, :] = jnp.concatenate([y_hi, y_lo], axis=1)


def left_factor(ids, pieces, owners, inv, rows, nm, nz, q_own, after):
    return pl.pallas_call(
        functools.partial(p_hat_kernel, owners, nm, nz),
        grid_spec=pltpu.PrefetchScalarGridSpec(
            num_scalar_prefetch=1,
            grid=(),
            in_specs=[pl.BlockSpec(memory_space=pltpu.VMEM)] * 11,
            out_specs=[pl.BlockSpec(memory_space=pltpu.VMEM)] * 2,
            scratch_shapes=[pltpu.VMEM((rows, RANK), F32)],
        ),
        out_shape=[jax.ShapeDtypeStruct((rows, 2 * RANK), BF16), jax.ShapeDtypeStruct(q_own.shape, F32)],
        compiler_params=params(SMALL_LIMIT),
        cost_estimate=cost(8 * rows * RANK * RANK, rows * RANK * 8),
        name="left_factor",
    )(ids, q_own, after, *pieces, inv)


def final_kernel(nz, scale, ids_ref, *refs):
    pieces, refs = refs[: 2 * nz], refs[2 * nz :]
    inv_ref, phat_ref, parts = refs[0], refs[1], refs[2:10]
    err_ref, qnew_hbm, q_sum, q_cat, qnew_ref, sem, held, sems = refs[10:]
    small = pieces[0].shape[0]
    for h in range(2):
        for k in range(nz):
            block = (ids_ref[0] ^ h) * nz + (ids_ref[2] ^ k)
            q_sum[pl.ds(pl.multiple_of(block * small, small), small), :] = pieces[h * nz + k][...]
    q_t = scale * lax.dot_general(
        inv_ref[...], q_sum[...], (((1,), (0,)), ((), ())), precision=HIGHEST, preferred_element_type=F32
    )
    hi = q_t.astype(BF16)
    lo = (q_t - hi.astype(F32)).astype(BF16)
    q_cat[...] = jnp.concatenate([hi, hi, lo, lo], axis=0)
    part_rows, cols = parts[0].shape
    chunk = min(cols, 512)
    tile = part_rows // 2
    slots = held.shape[0]
    copies = []
    for number, merged in enumerate(parts):
        for i in range(2):
            at = pl.ds(i * tile, tile)
            slot = len(copies) % slots
            if len(copies) >= slots:
                copies[-slots].wait()
            x = phat_ref[pl.ds(number * part_rows + i * tile, tile), :]
            x = jnp.concatenate([x, x], axis=1)
            for j in range(cols // chunk):
                here = pl.ds(j * chunk, chunk)
                held[slot, :, here] = (merged[at, here] - dot(x, q_cat[:, here])).astype(BF16)
            row = pl.multiple_of((number ^ (ids_ref[0] * 4)) * part_rows + i * tile, tile)
            copies.append(
                pltpu.make_async_copy(held.at[slot], err_ref.at[0, pl.ds(row, tile), :], sems.at[slot])
            )
            copies[-1].start()
        if number == 0:
            qnew_ref[...] = q_t.T
            copy = pltpu.make_async_copy(qnew_ref, qnew_hbm, sem)
            copy.start()
    for last in copies[-slots:]:
        last.wait()
    copy.wait()


def finish(ids, pieces, inv, phat, parts, replicas):
    nz = len(pieces) // 2
    part_rows, cols = parts[0].shape
    rows = part_rows * len(parts)
    vmem = pl.BlockSpec(memory_space=pltpu.VMEM)
    hbm = pl.BlockSpec(memory_space=pltpu.HBM)
    return pl.pallas_call(
        functools.partial(final_kernel, nz, 1.0 / replicas),
        grid_spec=pltpu.PrefetchScalarGridSpec(
            num_scalar_prefetch=1,
            grid=(),
            in_specs=[vmem] * (2 * nz + 2 + len(parts)),
            out_specs=[hbm, hbm],
            scratch_shapes=[
                pltpu.VMEM((RANK, cols), F32),
                pltpu.VMEM((4 * RANK, cols), BF16),
                pltpu.VMEM((cols, RANK), F32),
                pltpu.SemaphoreType.DMA,
                pltpu.VMEM((4, part_rows // 2, cols), BF16),
                pltpu.SemaphoreType.DMA((4,)),
            ],
        ),
        out_shape=[jax.ShapeDtypeStruct((1, rows, cols), BF16), jax.ShapeDtypeStruct((cols, RANK), F32)],
        compiler_params=params(FINAL_LIMIT),
        cost_estimate=cost(8 * rows * cols * RANK, rows * cols * 6),
        name="new_error",
    )(ids, *pieces, inv, phat, *parts)


def q_sum_kernel(nz, *refs):
    keep, came, outs = refs[0], refs[1], refs[2:]
    for k in range(nz):
        outs[k][...] = keep[k] + came[k]


def per_device(n_dp, n_mp, activations, out_grads, error_fb, q_prev):
    a, g, e, q = [
        pltpu.with_memory_space_constraint(x, pltpu.HBM) for x in (activations[0], out_grads[0], error_fb[0], q_prev)
    ]
    rows = a.shape[1]
    nz = n_dp // 2
    dp, mp = lax.axis_index("dp"), lax.axis_index("mp")
    ids = jnp.stack([dp % 2, mp, dp // 2]).astype(jnp.int32)
    bits = list(range(n_mp.bit_length() - 1))
    orders = [bits, bits[::-1]]

    def to_core(x):
        return lax.ppermute(x, "dp", [(i, i ^ 1) for i in range(n_dp)])

    def to_z(x, k):
        return lax.ppermute(x, "dp", [(i, i ^ (2 * k)) for i in range(n_dp)])

    def to_mp(x, k):
        return lax.ppermute(x, "mp", [(i, i ^ k) for i in range(n_mp)])

    p_far, a_far, e_far, g_here, ucat, qcat = left_terms(ids, q, g, a, e, n_mp, nz)
    p_arrived = to_core(p_far)
    p_near, a_near, e_near = left_terms(ids, q, g, a, e, n_mp, nz, (ucat, qcat))
    parts = []

    def beside(sent, count=1):
        done = []
        while count and len(parts) < 7:
            number = len(parts)
            mine = (a_near, e_near) if number < 4 else (a_far, e_far)
            part, sent = merged_part(*mine, g_here, number % 4, True, sent)
            parts.append(part)
            done = [sent]
            count -= 1
        return done

    by_z = scatter_over_mp(p_near, p_arrived, to_mp, orders, beside)
    done = beside(by_z[0])
    came = [to_z(by_z[k], k) for k in range(1, nz)]
    [p_own] = in_vmem(own_sum_kernel, [(by_z[0].shape, F32)], [by_z[0], *came], "p_own", after=done)
    done = beside(p_own)
    p_pieces = [p_own] + [to_z(p_own, k) for k in range(1, nz)]
    near, owners = gather_over_mp(p_pieces, to_mp, orders, beside, done)
    done = (beside(near[0], 8) or [near[0]])[0]
    far = [to_core(x) for x in near]

    half = right_terms(ids, near, owners, a_near, e_near, g_here, n_mp, done)
    q_send, q_keep, gram = right_terms(ids, far, owners, a_far, e_far, g_here, n_mp, done, half)

    piece = (q_keep.shape[1:], F32)
    q_by_z = in_vmem(functools.partial(q_sum_kernel, nz), [piece] * nz, [q_keep, to_core(q_send)], "q_sum")
    square = ((RANK, RANK), F32)
    [inv] = in_vmem(
        chol_inverse_kernel, [square], [gram], "chol_inverse", after=[q_by_z[0]], work=cost(2 * 10**10, 10**5)
    )
    came = [to_z(q_by_z[k], k) for k in range(1, nz)]
    [q_own] = in_vmem(own_sum_kernel, [piece], [q_by_z[0], *came], "q_own", after=[inv])
    part, done = merged_part(a_far, e_far, g_here, 3, False, q_own)
    parts.append(part)
    phat, q_again = left_factor(ids, near + far, owners, inv, rows, n_mp, nz, q_own, done)
    q_near = [q_own] + [to_z(q_own, k) for k in range(1, nz)]
    q_pieces = q_near + [to_core(x) for x in [q_again] + q_near[1:]]

    new_error, q_new = finish(ids, q_pieces, inv, phat, parts, n_dp)
    return new_error, q_new


def solution(mesh):
    placed = (P("dp", None, None), P("dp", None, "mp"), P("dp", None, "mp"), P("mp", None))
    return jax.shard_map(
        functools.partial(per_device, mesh.shape["dp"], mesh.shape["mp"]),
        mesh=mesh,
        in_specs=placed,
        out_specs=(P("dp", None, "mp"), P("mp", None)),
        check_vma=False,
    )
```

```python
import functools

import jax
import jax.numpy as jnp
from jax import lax
from jax.experimental import pallas as pl
from jax.experimental.pallas import tpu as pltpu
from jax.sharding import PartitionSpec as P

F32 = jnp.float32
BF16 = jnp.bfloat16
HIGHEST = lax.Precision.HIGHEST
RANK = 128
VMEM_LIMIT = 50 * 1024 * 1024
LEFT_LIMIT = 14 * 1024 * 1024
SMALL_LIMIT = 6 * 1024 * 1024
MERGED_LIMIT = 8 * 1024 * 1024
RIGHT_LIMIT = 11 * 1024 * 1024
FINAL_LIMIT = 9 * 1024 * 1024


def params(limit=VMEM_LIMIT):
    return pltpu.CompilerParams(vmem_limit_bytes=limit)


def cost(flops, nbytes):
    return pl.CostEstimate(flops=flops, bytes_accessed=nbytes, transcendentals=0)


def split_rows(x):
    hi = x.astype(BF16)
    lo = (x - hi.astype(F32)).astype(BF16)
    return jnp.concatenate([hi, lo], axis=0)


def fold(y):
    return y[:RANK] + y[RANK:]


def dot(a, b, contract=((1,), (0,))):
    return lax.dot_general(a, b, (contract, ((), ())), preferred_element_type=F32)


ROWS_BY_ROWS = ((1,), (1,))


def skipping(count, body, *refs):
    body(*refs[count:])


def in_vmem(body, outs, args, name, limit=SMALL_LIMIT, work=None, after=()):
    args = [*after, *args]
    return pl.pallas_call(
        functools.partial(skipping, len(after), body),
        in_specs=[pl.BlockSpec(memory_space=pltpu.VMEM)] * len(args),
        out_specs=[pl.BlockSpec(memory_space=pltpu.VMEM)] * len(outs),
        out_shape=[jax.ShapeDtypeStruct(*out) for out in outs],
        compiler_params=params(limit),
        cost_estimate=work,
        name=name,
    )(*args)


STEPS = 4
AHEAD = 2


def copies_of_half(a_hbm, e_hbm, a_ref, e_ref, sems, half):
    rows = e_ref.shape[0]
    tile = rows // STEPS
    copies = []
    for i in range(STEPS):
        here = pl.ds(i * tile, tile)
        there = pl.ds(pl.multiple_of(half * rows + i * tile, tile), tile)
        copies.append(
            (
                pltpu.make_async_copy(e_hbm.at[there, :], e_ref.at[here, :], sems.at[2 * i]),
                pltpu.make_async_copy(a_hbm.at[:, there], a_ref.at[:, here], sems.at[2 * i + 1]),
            )
        )
    return copies


def start(pair):
    for copy in pair:
        copy.start()


def p_of_half(ids_ref, copies, a_ref, e_ref, ucat_ref, qcat_ref, p_ref):
    nz, small = p_ref.shape[1:3]
    tile = e_ref.shape[0] // STEPS
    for i, (e_copy, a_copy) in enumerate(copies):
        here = pl.ds(i * tile, tile)
        e_copy.wait()
        a_copy.wait()
        if i + AHEAD < STEPS:
            start(copies[i + AHEAD])
        acc = dot(qcat_ref[...], e_ref[here, :], ROWS_BY_ROWS) + dot(ucat_ref[...], a_ref[:, here])
        p_tile = fold(acc).T
        for k in range(tile // small):
            block = i * (tile // small) + k
            p_ref[(block // nz) ^ ids_ref[1], (block % nz) ^ ids_ref[2]] = p_tile[k * small : (k + 1) * small]


def far_kernel(
    ids_ref, q_hbm, g_hbm, a_hbm, e_hbm, p_ref, a_ref, e_ref, g_ref, ucat_ref, qcat_ref, q_ref, sems, first_sems
):
    tok = g_ref.shape[0]
    q_copy = pltpu.make_async_copy(q_hbm, q_ref, first_sems.at[0])
    q_copy.start()
    g_copies = []
    for i in range(2):
        at = pl.ds(i * (tok // 2), tok // 2)
        g_copies.append(pltpu.make_async_copy(g_hbm.at[at, :], g_ref.at[at, :], first_sems.at[1 + i]))
        g_copies[-1].start()
    copies = copies_of_half(a_hbm, e_hbm, a_ref, e_ref, sems, ids_ref[0] ^ 1)
    q_copy.wait()
    qcat_ref[...] = split_rows(q_ref[...].T)
    for i in range(2):
        at = pl.ds(i * (tok // 2), tok // 2)
        g_copies[i].wait()
        start(copies[i])
        ucat_ref[:, at] = split_rows(fold(dot(qcat_ref[...], g_ref[at, :], ROWS_BY_ROWS)))
    p_of_half(ids_ref, copies, a_ref, e_ref, ucat_ref, qcat_ref, p_ref)


def near_kernel(ids_ref, ucat_ref, qcat_ref, a_hbm, e_hbm, p_ref, a_ref, e_ref, sems):
    copies = copies_of_half(a_hbm, e_hbm, a_ref, e_ref, sems, ids_ref[0])
    for pair in copies[:AHEAD]:
        start(pair)
    p_of_half(ids_ref, copies, a_ref, e_ref, ucat_ref, qcat_ref, p_ref)


def left_terms(ids, q, g, a, e, nm, nz, before=None):
    tok, rows = a.shape
    cols = e.shape[1]
    vmem = pl.BlockSpec(memory_space=pltpu.VMEM)
    hbm = pl.BlockSpec(memory_space=pltpu.HBM)
    outs = [
        pltpu.VMEM((nm, nz, rows // (2 * nm * nz), RANK), F32),
        pltpu.VMEM((tok, rows // 2), BF16),
        pltpu.VMEM((rows // 2, cols), BF16),
    ]
    scratch = [pltpu.SemaphoreType.DMA((2 * STEPS,))]
    if before is None:
        body, specs, args = far_kernel, [hbm] * 4, (q, g, a, e)
        outs += [
            pltpu.VMEM((tok, cols), BF16),
            pltpu.VMEM((2 * RANK, tok), BF16),
            pltpu.VMEM((2 * RANK, cols), BF16),
        ]
        scratch = [pltpu.VMEM((cols, RANK), F32)] + scratch + [pltpu.SemaphoreType.DMA((3,))]
    else:
        body, specs, args = near_kernel, [vmem] * 2 + [hbm] * 2, (*before, a, e)
    return pl.pallas_call(
        body,
        grid_spec=pltpu.PrefetchScalarGridSpec(
            num_scalar_prefetch=1,
            grid=(),
            in_specs=specs,
            out_specs=[vmem] * len(outs),
            scratch_shapes=scratch,
        ),
        out_shape=outs,
        compiler_params=params(LEFT_LIMIT),
        cost_estimate=cost(2 * rows * RANK * (tok + cols), rows * (tok + cols)),
        name="left_terms",
    )(ids, *args)


def first_sum_kernel(keeps, sends, near_ref, far_ref, *outs):
    rows = near_ref.shape[2] // 2
    for half in range(2):
        for out, members in ((outs[2 * half], sends[half]), (outs[2 * half + 1], keeps[half])):
            for i, km in enumerate(members):
                at = (km, slice(None), pl.ds(half * rows, rows))
                out[i] = near_ref[at] + far_ref[at]


def next_sum_kernel(keeps, sends, *refs):
    ins, outs = refs[:4], refs[4:]
    for half in range(2):
        kept, came = ins[2 * half : 2 * half + 2]
        for out, places in ((outs[2 * half], sends[half]), (outs[2 * half + 1], keeps[half])):
            for i, at in enumerate(places):
                out[i] = kept[at] + came[at]


def last_sum_kernel(nz, *refs):
    ins, outs = refs[:4], refs[4:]
    rows = ins[0].shape[2]
    for k in range(nz):
        for half in range(2):
            outs[k][pl.ds(half * rows, rows), :] = ins[2 * half][0, k] + ins[2 * half + 1][0, k]


def scatter_over_mp(near, far, to_mp, orders, beside):
    nm, nz, block, _ = near.shape
    rows = block // 2
    members = [list(range(nm))] * 2
    values, done = None, ()
    for step in range(len(orders[0])):
        bits = [1 << order[step] for order in orders]
        keep_lists = [[km for km in members[h] if not km & bits[h]] for h in range(2)]
        send_lists = [[km | bits[h] for km in keep_lists[h]] for h in range(2)]
        count = len(keep_lists[0])
        outs = [((count, nz, rows, RANK), F32)] * 4
        if values is None:
            parts = in_vmem(functools.partial(first_sum_kernel, keep_lists, send_lists), outs, [near, far], "first_sum")
        else:
            keep_at = [[members[h].index(km) for km in keep_lists[h]] for h in range(2)]
            send_at = [[members[h].index(km) for km in send_lists[h]] for h in range(2)]
            parts = in_vmem(functools.partial(next_sum_kernel, keep_at, send_at), outs, values, "next_sum", after=done)
        members = keep_lists
        came = [to_mp(parts[0], bits[0]), to_mp(parts[2], bits[1])]
        done = beside(parts[1], 1 if step else 2)
        values = [parts[1], came[0], parts[3], came[1]]
    return in_vmem(functools.partial(last_sum_kernel, nz), [((block, RANK), F32)] * nz, values, "last_sum", after=done)


def own_sum_kernel(*refs):
    ins, out = refs[:-1], refs[-1]
    total = ins[0][...]
    for came in ins[1:]:
        total = total + came[...]
    out[...] = total


def own_kernel(nz, *refs):
    ins, outs = refs[:nz], refs[nz:]
    rows = outs[0].shape[2]
    for k in range(nz):
        for half in range(2):
            outs[half][0, k] = ins[k][pl.ds(half * rows, rows), :]


def grow_kernel(*refs):
    ins, outs = refs[:4], refs[4:]
    count = ins[0].shape[0]
    for half in range(2):
        outs[half][pl.ds(0, count)] = ins[2 * half][...]
        outs[half][pl.ds(count, count)] = ins[2 * half + 1][...]


def gather_over_mp(pieces, to_mp, orders, beside, done):
    nz = len(pieces)
    rows = pieces[0].shape[0] // 2
    held = in_vmem(functools.partial(own_kernel, nz), [((1, nz, rows, RANK), F32)] * 2, pieces, "own_rows", after=done)
    members = [[0], [0]]
    last = len(orders[0]) - 1
    for step in range(last, -1, -1):
        bits = [1 << order[step] for order in orders]
        came = [to_mp(held[h], bits[h]) for h in range(2)]
        came_members = [[km ^ bits[h] for km in members[h]] for h in range(2)]
        if step == 0:
            return [held[0], held[1], came[0], came[1]], [
                (0, members[0]), (1, members[1]), (0, came_members[0]), (1, came_members[1])
            ]
        count = len(members[0])
        held = in_vmem(
            grow_kernel,
            [((2 * count, nz, rows, RANK), F32)] * 2,
            [held[0], came[0], held[1], came[1]],
            "grow",
            after=beside(held[0]),
        )
        members = [members[h] + came_members[h] for h in range(2)]


def merged_kernel(part, in_hbm, after_ref, a_ref, e_ref, g_ref, out_ref, done_ref, a_t, *scratch):
    done_ref[...] = jnp.zeros_like(done_ref)
    rows, cols = out_ref.shape
    tile, chunk = rows // 2, min(cols, 512)
    held, sems = scratch if in_hbm else (out_ref, None)
    copies = []
    for i in range(2):
        at = pl.ds(i * tile, tile)
        a_t[at, :] = a_ref[:, pl.ds(part * rows + i * tile, tile)].T
        for j in range(cols // chunk):
            here = pl.ds(j * chunk, chunk)
            e_tile = e_ref[pl.ds(part * rows + i * tile, tile), here]
            held[at, here] = dot(a_t[at, :], g_ref[:, here]) + e_tile.astype(F32)
            if in_hbm:
                copy = pltpu.make_async_copy(held.at[at, here], out_ref.at[at, here], sems.at[len(copies)])
                copy.start()
                copies.append(copy)
    for copy in copies:
        copy.wait()


def merged_part(a, e, g, part, in_hbm, after):
    tok, half = a.shape
    cols = e.shape[1]
    rows = half // 4
    place = pltpu.HBM if in_hbm else pltpu.VMEM
    scratch = [pltpu.VMEM((rows, tok), BF16)]
    if in_hbm:
        scratch += [pltpu.VMEM((rows, cols), F32), pltpu.SemaphoreType.DMA((2 * (cols // min(cols, 512)),))]
    return pl.pallas_call(
        functools.partial(merged_kernel, part, in_hbm),
        in_specs=[pl.BlockSpec(memory_space=pl.ANY)] + [pl.BlockSpec(memory_space=pltpu.VMEM)] * 3,
        out_specs=[pl.BlockSpec(memory_space=place), pl.BlockSpec(memory_space=pltpu.VMEM)],
        out_shape=[place((rows, cols), F32), jax.ShapeDtypeStruct((8, RANK), F32)],
        scratch_shapes=scratch,
        compiler_params=params(MERGED_LIMIT if in_hbm else MERGED_LIMIT // 2),
        cost_estimate=cost(2 * tok * cols * rows, rows * cols * 2),
        name="merged",
    )(after, a, e, g)


def q_kernel(owners, nm, nz, last, ids_ref, after_ref, *refs):
    pieces, refs = refs[:4], refs[4:]
    if last:
        v_in, q_in, gram_in, a_ref, e_ref, g_ref, send_ref, keep_ref, gram_ref, p_half, pcat, q_acc = refs
    else:
        a_ref, e_ref, v_ref, q_acc, gram_ref, p_half, pcat = refs
    rows = pieces[0].shape[2]
    cols = e_ref.shape[1]
    chunk = min(cols, 512)
    for piece, (half, members) in zip(pieces, owners):
        for i, km in enumerate(members):
            for k in range(nz):
                start = ((ids_ref[1] ^ km) * nz + (ids_ref[2] ^ k)) * (2 * rows) + half * rows
                p_half[pl.ds(pl.multiple_of(start, rows), rows), :] = piece[i, k]
    pcat[...] = split_rows(p_half[...].T)
    v = fold(dot(pcat[...], a_ref[...], ROWS_BY_ROWS))
    gram = dot(pcat[...], pcat[...], ROWS_BY_ROWS)
    if last:
        vcat = split_rows(v + v_in[...])
        whole = fold(gram + gram_in[...])
        gram_ref[...] = whole[:, :RANK] + whole[:, RANK:]
    else:
        v_ref[...] = v
        gram_ref[...] = gram

    for i in range(cols // chunk):
        here = pl.ds(i * chunk, chunk)
        q = dot(pcat[...], e_ref[:, here])
        if last:
            q += dot(vcat, g_ref[:, here])
            q_acc[:, here] = fold(q) + q_in[:, here]
        else:
            q_acc[:, here] = fold(q)

    if last:
        small = send_ref.shape[1]
        for out, flip in ((send_ref, 1), (keep_ref, 0)):
            for k in range(nz):
                start = ((ids_ref[0] ^ flip) * nz + (ids_ref[2] ^ k)) * small
                out[k] = q_acc[pl.ds(pl.multiple_of(start, small), small), :]


def right_terms(ids, pieces, owners, a, e, g, nm, after, before=None):
    tok, half = a.shape
    cols = e.shape[1]
    nz = pieces[0].shape[1]
    last = before is not None
    vmem = pl.BlockSpec(memory_space=pltpu.VMEM)
    sums = [(RANK, tok), (RANK, cols), (2 * RANK, 2 * RANK)]
    scratch = [pltpu.VMEM((half, RANK), F32), pltpu.VMEM((2 * RANK, half), BF16)]
    if last:
        args = [*pieces, *before, a, e, g]
        outs = [(nz, RANK // (2 * nz), cols)] * 2 + [(RANK, RANK)]
        scratch += [pltpu.VMEM((RANK, cols), F32)]
    else:
        args = [*pieces, a, e]
        outs = sums
    return pl.pallas_call(
        functools.partial(q_kernel, owners, nm, nz, last),
        grid_spec=pltpu.PrefetchScalarGridSpec(
            num_scalar_prefetch=1,
            grid=(),
            in_specs=[pl.BlockSpec(memory_space=pl.ANY)] + [vmem] * len(args),
            out_specs=[vmem] * 3,
            scratch_shapes=scratch,
        ),
        out_shape=[jax.ShapeDtypeStruct(shape, F32) for shape in outs],
        compiler_params=params(RIGHT_LIMIT),
        cost_estimate=cost(4 * half * RANK * (tok + cols), half * (tok + cols)),
        name="right_terms",
    )(ids, after, *args)


def chol_inverse_kernel(gram_ref, out_ref):
    left = gram_ref[...]
    row = lax.broadcasted_iota(jnp.int32, (RANK, RANK), 0)
    right = (row == lax.broadcasted_iota(jnp.int32, (RANK, RANK), 1)).astype(F32)
    for j in range(0, RANK, 2):
        at = j % 8
        if j and at == 0:
            left, right = left[8:], right[8:]
        column = jnp.broadcast_to(left[:, j : j + 1], left.shape)
        column2 = jnp.broadcast_to(left[:, j + 1 : j + 2], left.shape)
        first, own = left[at : at + 1], right[at : at + 1]
        pivot, cross = column[at : at + 1], column2[at : at + 1]
        inverse = 1.0 / pivot
        ratio = column[at + 1 : at + 2] * inverse
        second = left[at + 1 : at + 2] - ratio * first
        other = right[at + 1 : at + 2] - ratio * own
        pivot2 = column2[at + 1 : at + 2] - ratio * cross
        inverse2 = 1.0 / pivot2
        out_ref[j : j + 1, :] = own * (1.0 / jnp.sqrt(pivot))
        out_ref[j + 1 : j + 2, :] = other * (1.0 / jnp.sqrt(pivot2))
        column2 = column2 - column * (cross * inverse)
        below = row[: left.shape[0]] > at + 1
        column = jnp.where(below, column, 0.0)
        column2 = jnp.where(below, column2, 0.0)
        left = left - column * (first * inverse) - column2 * (second * inverse2)
        right = right - column * (own * inverse) - column2 * (other * inverse2)


def p_hat_kernel(owners, nm, nz, ids_ref, q_ref, after_ref, *refs):
    pieces, (inv_ref, out_ref, q_again, p_all) = refs[:8], refs[8:]
    q_again[...] = q_ref[...]
    rows = pieces[0].shape[2]
    for h in range(2):
        for piece, (half, members) in zip(pieces[4 * h : 4 * h + 4], owners):
            for i, km in enumerate(members):
                for k in range(nz):
                    block = (h * nm + (ids_ref[1] ^ km)) * nz + (ids_ref[2] ^ k)
                    start = block * (2 * rows) + half * rows
                    p_all[pl.ds(pl.multiple_of(start, rows), rows), :] = piece[i, k]
    inv_hi = inv_ref[...].T.astype(BF16)
    inv_lo = (inv_ref[...].T - inv_hi.astype(F32)).astype(BF16)
    inv = jnp.concatenate([inv_hi, inv_hi, inv_lo, inv_lo], axis=0)
    tile = p_all.shape[0] // 8

    @pl.loop(0, 8)
    def _(i):
        at = pl.ds(pl.multiple_of(i * tile, tile), tile)
        x = p_all[at, :]
        hi = x.astype(BF16)
        lo = (x - hi.astype(F32)).astype(BF16)
        y = dot(jnp.concatenate([hi, lo, hi, lo], axis=1), inv)
        y_hi = y.astype(BF16)
        y_lo = (y - y_hi.astype(F32)).astype(BF16)
        out_ref[at, :] = jnp.concatenate([y_hi, y_lo], axis=1)


def left_factor(ids, pieces, owners, inv, rows, nm, nz, q_own, after):
    return pl.pallas_call(
        functools.partial(p_hat_kernel, owners, nm, nz),
        grid_spec=pltpu.PrefetchScalarGridSpec(
            num_scalar_prefetch=1,
            grid=(),
            in_specs=[pl.BlockSpec(memory_space=pltpu.VMEM)] * 11,
            out_specs=[pl.BlockSpec(memory_space=pltpu.VMEM)] * 2,
            scratch_shapes=[pltpu.VMEM((rows, RANK), F32)],
        ),
        out_shape=[jax.ShapeDtypeStruct((rows, 2 * RANK), BF16), jax.ShapeDtypeStruct(q_own.shape, F32)],
        compiler_params=params(SMALL_LIMIT),
        cost_estimate=cost(8 * rows * RANK * RANK, rows * RANK * 8),
        name="left_factor",
    )(ids, q_own, after, *pieces, inv)


def final_kernel(nz, scale, ids_ref, *refs):
    pieces, refs = refs[: 2 * nz], refs[2 * nz :]
    inv_ref, phat_ref, parts = refs[0], refs[1], refs[2:10]
    err_ref, qnew_hbm, q_sum, q_cat, qnew_ref, sem, held, sems = refs[10:]
    small = pieces[0].shape[0]
    for h in range(2):
        for k in range(nz):
            block = (ids_ref[0] ^ h) * nz + (ids_ref[2] ^ k)
            q_sum[pl.ds(pl.multiple_of(block * small, small), small), :] = pieces[h * nz + k][...]

    def right_factor(here):
        q_t = scale * lax.dot_general(
            inv_ref[...], q_sum[:, here], (((1,), (0,)), ((), ())), precision=HIGHEST, preferred_element_type=F32
        )
        hi = q_t.astype(BF16)
        lo = (q_t - hi.astype(F32)).astype(BF16)
        q_cat[:, here] = jnp.concatenate([hi, hi, lo, lo], axis=0)
        qnew_ref[here, :] = q_t.T

    part_rows, cols = parts[0].shape
    chunk = min(cols, 512)
    tile = part_rows // 2
    slots = held.shape[0]
    copies = []
    for number, merged in enumerate(parts):
        for i in range(2):
            at = pl.ds(i * tile, tile)
            slot = len(copies) % slots
            if len(copies) >= slots:
                copies[-slots].wait()
            x = phat_ref[pl.ds(number * part_rows + i * tile, tile), :]
            x = jnp.concatenate([x, x], axis=1)
            for j in range(cols // chunk):
                here = pl.ds(j * chunk, chunk)
                if not copies:
                    right_factor(here)
                held[slot, :, here] = (merged[at, here] - dot(x, q_cat[:, here])).astype(BF16)
            row = pl.multiple_of((number ^ (ids_ref[0] * 4)) * part_rows + i * tile, tile)
            copies.append(
                pltpu.make_async_copy(held.at[slot], err_ref.at[0, pl.ds(row, tile), :], sems.at[slot])
            )
            copies[-1].start()
        if number == 0:
            copy = pltpu.make_async_copy(qnew_ref, qnew_hbm, sem)
            copy.start()
    for last in copies[-slots:]:
        last.wait()
    copy.wait()


def finish(ids, pieces, inv, phat, parts, replicas):
    nz = len(pieces) // 2
    part_rows, cols = parts[0].shape
    rows = part_rows * len(parts)
    vmem = pl.BlockSpec(memory_space=pltpu.VMEM)
    hbm = pl.BlockSpec(memory_space=pltpu.HBM)
    return pl.pallas_call(
        functools.partial(final_kernel, nz, 1.0 / replicas),
        grid_spec=pltpu.PrefetchScalarGridSpec(
            num_scalar_prefetch=1,
            grid=(),
            in_specs=[vmem] * (2 * nz + 2 + len(parts)),
            out_specs=[hbm, hbm],
            scratch_shapes=[
                pltpu.VMEM((RANK, cols), F32),
                pltpu.VMEM((4 * RANK, cols), BF16),
                pltpu.VMEM((cols, RANK), F32),
                pltpu.SemaphoreType.DMA,
                pltpu.VMEM((4, part_rows // 2, cols), BF16),
                pltpu.SemaphoreType.DMA((4,)),
            ],
        ),
        out_shape=[jax.ShapeDtypeStruct((1, rows, cols), BF16), jax.ShapeDtypeStruct((cols, RANK), F32)],
        compiler_params=params(FINAL_LIMIT),
        cost_estimate=cost(8 * rows * cols * RANK, rows * cols * 6),
        name="new_error",
    )(ids, *pieces, inv, phat, *parts)


def q_sum_kernel(nz, *refs):
    keep, came, outs = refs[0], refs[1], refs[2:]
    for k in range(nz):
        outs[k][...] = keep[k] + came[k]


def per_device(n_dp, n_mp, activations, out_grads, error_fb, q_prev):
    a, g, e, q = [
        pltpu.with_memory_space_constraint(x, pltpu.HBM) for x in (activations[0], out_grads[0], error_fb[0], q_prev)
    ]
    rows = a.shape[1]
    nz = n_dp // 2
    dp, mp = lax.axis_index("dp"), lax.axis_index("mp")
    ids = jnp.stack([dp % 2, mp, dp // 2]).astype(jnp.int32)
    bits = list(range(n_mp.bit_length() - 1))
    orders = [bits, bits[::-1]]

    def to_core(x):
        return lax.ppermute(x, "dp", [(i, i ^ 1) for i in range(n_dp)])

    def to_z(x, k):
        return lax.ppermute(x, "dp", [(i, i ^ (2 * k)) for i in range(n_dp)])

    def to_mp(x, k):
        return lax.ppermute(x, "mp", [(i, i ^ k) for i in range(n_mp)])

    p_far, a_far, e_far, g_here, ucat, qcat = left_terms(ids, q, g, a, e, n_mp, nz)
    p_arrived = to_core(p_far)
    p_near, a_near, e_near = left_terms(ids, q, g, a, e, n_mp, nz, (ucat, qcat))
    parts = []

    def beside(sent, count=1):
        done = []
        while count and len(parts) < 7:
            number = len(parts)
            mine = (a_near, e_near) if number < 4 else (a_far, e_far)
            part, sent = merged_part(*mine, g_here, number % 4, True, sent)
            parts.append(part)
            done = [sent]
            count -= 1
        return done

    by_z = scatter_over_mp(p_near, p_arrived, to_mp, orders, beside)
    done = beside(by_z[0])
    came = [to_z(by_z[k], k) for k in range(1, nz)]
    [p_own] = in_vmem(own_sum_kernel, [(by_z[0].shape, F32)], [by_z[0], *came], "p_own", after=done)
    done = beside(p_own)
    p_pieces = [p_own] + [to_z(p_own, k) for k in range(1, nz)]
    near, owners = gather_over_mp(p_pieces, to_mp, orders, beside, done)
    done = (beside(near[0], 8) or [near[0]])[0]
    far = [to_core(x) for x in near]

    half = right_terms(ids, near, owners, a_near, e_near, g_here, n_mp, done)
    q_send, q_keep, gram = right_terms(ids, far, owners, a_far, e_far, g_here, n_mp, done, half)

    piece = (q_keep.shape[1:], F32)
    q_by_z = in_vmem(functools.partial(q_sum_kernel, nz), [piece] * nz, [q_keep, to_core(q_send)], "q_sum")
    square = ((RANK, RANK), F32)
    [inv] = in_vmem(
        chol_inverse_kernel, [square], [gram], "chol_inverse", after=[q_by_z[0]], work=cost(2 * 10**10, 10**5)
    )
    came = [to_z(q_by_z[k], k) for k in range(1, nz)]
    [q_own] = in_vmem(own_sum_kernel, [piece], [q_by_z[0], *came], "q_own", after=[inv])
    part, done = merged_part(a_far, e_far, g_here, 3, False, q_own)
    parts.append(part)
    phat, q_again = left_factor(ids, near + far, owners, inv, rows, n_mp, nz, q_own, done)
    q_near = [q_own] + [to_z(q_own, k) for k in range(1, nz)]
    q_pieces = q_near + [to_core(x) for x in [q_again] + q_near[1:]]

    new_error, q_new = finish(ids, q_pieces, inv, phat, parts, n_dp)
    return new_error, q_new


def solution(mesh):
    placed = (P("dp", None, None), P("dp", None, "mp"), P("dp", None, "mp"), P("mp", None))
    return jax.shard_map(
        functools.partial(per_device, mesh.shape["dp"], mesh.shape["mp"]),
        mesh=mesh,
        in_specs=placed,
        out_specs=(P("dp", None, "mp"), P("mp", None)),
        check_vma=False,
    )
```

```python
import functools

import jax
import jax.numpy as jnp
from jax import lax
from jax.experimental import pallas as pl
from jax.experimental.pallas import tpu as pltpu
from jax.sharding import PartitionSpec as P

F32 = jnp.float32
BF16 = jnp.bfloat16
HIGHEST = lax.Precision.HIGHEST
RANK = 128
VMEM_LIMIT = 50 * 1024 * 1024
LEFT_LIMIT = 14 * 1024 * 1024
SMALL_LIMIT = 6 * 1024 * 1024
MERGED_LIMIT = 8 * 1024 * 1024
RIGHT_LIMIT = 11 * 1024 * 1024
FINAL_LIMIT = 9 * 1024 * 1024


def params(limit=VMEM_LIMIT):
    return pltpu.CompilerParams(vmem_limit_bytes=limit)


def cost(flops, nbytes):
    return pl.CostEstimate(flops=flops, bytes_accessed=nbytes, transcendentals=0)


def split_rows(x):
    hi = x.astype(BF16)
    lo = (x - hi.astype(F32)).astype(BF16)
    return jnp.concatenate([hi, lo], axis=0)


def fold(y):
    return y[:RANK] + y[RANK:]


def dot(a, b, contract=((1,), (0,))):
    return lax.dot_general(a, b, (contract, ((), ())), preferred_element_type=F32)


ROWS_BY_ROWS = ((1,), (1,))


def skipping(count, body, *refs):
    body(*refs[count:])


def in_vmem(body, outs, args, name, limit=SMALL_LIMIT, work=None, after=()):
    args = [*after, *args]
    return pl.pallas_call(
        functools.partial(skipping, len(after), body),
        in_specs=[pl.BlockSpec(memory_space=pltpu.VMEM)] * len(args),
        out_specs=[pl.BlockSpec(memory_space=pltpu.VMEM)] * len(outs),
        out_shape=[jax.ShapeDtypeStruct(*out) for out in outs],
        compiler_params=params(limit),
        cost_estimate=work,
        name=name,
    )(*args)


STEPS = 4
AHEAD = 2


def copies_of_half(a_hbm, e_hbm, a_ref, e_ref, sems, half):
    rows = e_ref.shape[0]
    tile = rows // STEPS
    copies = []
    for i in range(STEPS):
        here = pl.ds(i * tile, tile)
        there = pl.ds(pl.multiple_of(half * rows + i * tile, tile), tile)
        copies.append(
            (
                pltpu.make_async_copy(e_hbm.at[there, :], e_ref.at[here, :], sems.at[2 * i]),
                pltpu.make_async_copy(a_hbm.at[:, there], a_ref.at[:, here], sems.at[2 * i + 1]),
            )
        )
    return copies


def start(pair):
    for copy in pair:
        copy.start()


def p_of_half(ids_ref, copies, a_ref, e_ref, ucat_ref, qcat_ref, p_ref):
    nz, small = p_ref.shape[1:3]
    tile = e_ref.shape[0] // STEPS
    for i, (e_copy, a_copy) in enumerate(copies):
        here = pl.ds(i * tile, tile)
        e_copy.wait()
        a_copy.wait()
        if i + AHEAD < STEPS:
            start(copies[i + AHEAD])
        acc = dot(qcat_ref[...], e_ref[here, :], ROWS_BY_ROWS) + dot(ucat_ref[...], a_ref[:, here])
        p_tile = fold(acc).T
        for k in range(tile // small):
            block = i * (tile // small) + k
            p_ref[(block // nz) ^ ids_ref[1], (block % nz) ^ ids_ref[2]] = p_tile[k * small : (k + 1) * small]


def far_kernel(
    ids_ref, q_hbm, g_hbm, a_hbm, e_hbm, p_ref, a_ref, e_ref, g_ref, ucat_ref, qcat_ref, q_ref, sems, first_sems
):
    tok = g_ref.shape[0]
    q_copy = pltpu.make_async_copy(q_hbm, q_ref, first_sems.at[0])
    q_copy.start()
    g_copies = []
    for i in range(2):
        at = pl.ds(i * (tok // 2), tok // 2)
        g_copies.append(pltpu.make_async_copy(g_hbm.at[at, :], g_ref.at[at, :], first_sems.at[1 + i]))
        g_copies[-1].start()
    copies = copies_of_half(a_hbm, e_hbm, a_ref, e_ref, sems, ids_ref[0] ^ 1)
    q_copy.wait()
    qcat_ref[...] = split_rows(q_ref[...].T)
    for i in range(2):
        at = pl.ds(i * (tok // 2), tok // 2)
        g_copies[i].wait()
        start(copies[i])
        ucat_ref[:, at] = split_rows(fold(dot(qcat_ref[...], g_ref[at, :], ROWS_BY_ROWS)))
    p_of_half(ids_ref, copies, a_ref, e_ref, ucat_ref, qcat_ref, p_ref)


def near_kernel(ids_ref, ucat_ref, qcat_ref, a_hbm, e_hbm, p_ref, a_ref, e_ref, sems):
    copies = copies_of_half(a_hbm, e_hbm, a_ref, e_ref, sems, ids_ref[0])
    for pair in copies[:AHEAD]:
        start(pair)
    p_of_half(ids_ref, copies, a_ref, e_ref, ucat_ref, qcat_ref, p_ref)


def left_terms(ids, q, g, a, e, nm, nz, before=None):
    tok, rows = a.shape
    cols = e.shape[1]
    vmem = pl.BlockSpec(memory_space=pltpu.VMEM)
    hbm = pl.BlockSpec(memory_space=pltpu.HBM)
    outs = [
        pltpu.VMEM((nm, nz, rows // (2 * nm * nz), RANK), F32),
        pltpu.VMEM((tok, rows // 2), BF16),
        pltpu.VMEM((rows // 2, cols), BF16),
    ]
    scratch = [pltpu.SemaphoreType.DMA((2 * STEPS,))]
    if before is None:
        body, specs, args = far_kernel, [hbm] * 4, (q, g, a, e)
        outs += [
            pltpu.VMEM((tok, cols), BF16),
            pltpu.VMEM((2 * RANK, tok), BF16),
            pltpu.VMEM((2 * RANK, cols), BF16),
        ]
        scratch = [pltpu.VMEM((cols, RANK), F32)] + scratch + [pltpu.SemaphoreType.DMA((3,))]
    else:
        body, specs, args = near_kernel, [vmem] * 2 + [hbm] * 2, (*before, a, e)
    return pl.pallas_call(
        body,
        grid_spec=pltpu.PrefetchScalarGridSpec(
            num_scalar_prefetch=1,
            grid=(),
            in_specs=specs,
            out_specs=[vmem] * len(outs),
            scratch_shapes=scratch,
        ),
        out_shape=outs,
        compiler_params=params(LEFT_LIMIT),
        cost_estimate=cost(2 * rows * RANK * (tok + cols), rows * (tok + cols)),
        name="left_terms",
    )(ids, *args)


def first_sum_kernel(keeps, sends, near_ref, far_ref, *outs):
    rows = near_ref.shape[2] // 2
    for half in range(2):
        for out, members in ((outs[2 * half], sends[half]), (outs[2 * half + 1], keeps[half])):
            for i, km in enumerate(members):
                at = (km, slice(None), pl.ds(half * rows, rows))
                out[i] = near_ref[at] + far_ref[at]


def next_sum_kernel(keeps, sends, *refs):
    ins, outs = refs[:4], refs[4:]
    for half in range(2):
        kept, came = ins[2 * half : 2 * half + 2]
        for out, places in ((outs[2 * half], sends[half]), (outs[2 * half + 1], keeps[half])):
            for i, at in enumerate(places):
                out[i] = kept[at] + came[at]


def last_sum_kernel(nz, *refs):
    ins, outs = refs[:4], refs[4:]
    rows = ins[0].shape[2]
    for k in range(nz):
        for half in range(2):
            outs[k][pl.ds(half * rows, rows), :] = ins[2 * half][0, k] + ins[2 * half + 1][0, k]


def scatter_over_mp(near, far, to_mp, orders, beside):
    nm, nz, block, _ = near.shape
    rows = block // 2
    members = [list(range(nm))] * 2
    values, done = None, ()
    for step in range(len(orders[0])):
        bits = [1 << order[step] for order in orders]
        keep_lists = [[km for km in members[h] if not km & bits[h]] for h in range(2)]
        send_lists = [[km | bits[h] for km in keep_lists[h]] for h in range(2)]
        count = len(keep_lists[0])
        outs = [((count, nz, rows, RANK), F32)] * 4
        if values is None:
            parts = in_vmem(functools.partial(first_sum_kernel, keep_lists, send_lists), outs, [near, far], "first_sum")
        else:
            keep_at = [[members[h].index(km) for km in keep_lists[h]] for h in range(2)]
            send_at = [[members[h].index(km) for km in send_lists[h]] for h in range(2)]
            parts = in_vmem(functools.partial(next_sum_kernel, keep_at, send_at), outs, values, "next_sum", after=done)
        members = keep_lists
        came = [to_mp(parts[0], bits[0]), to_mp(parts[2], bits[1])]
        done = beside(parts[1])
        values = [parts[1], came[0], parts[3], came[1]]
    return in_vmem(functools.partial(last_sum_kernel, nz), [((block, RANK), F32)] * nz, values, "last_sum", after=done)


def own_sum_kernel(*refs):
    ins, out = refs[:-1], refs[-1]
    total = ins[0][...]
    for came in ins[1:]:
        total = total + came[...]
    out[...] = total


def own_kernel(nz, *refs):
    ins, outs = refs[:nz], refs[nz:]
    rows = outs[0].shape[2]
    for k in range(nz):
        for half in range(2):
            outs[half][0, k] = ins[k][pl.ds(half * rows, rows), :]


def grow_kernel(*refs):
    ins, outs = refs[:4], refs[4:]
    count = ins[0].shape[0]
    for half in range(2):
        outs[half][pl.ds(0, count)] = ins[2 * half][...]
        outs[half][pl.ds(count, count)] = ins[2 * half + 1][...]


def gather_over_mp(pieces, to_mp, orders, beside, done):
    nz = len(pieces)
    rows = pieces[0].shape[0] // 2
    held = in_vmem(functools.partial(own_kernel, nz), [((1, nz, rows, RANK), F32)] * 2, pieces, "own_rows", after=done)
    members = [[0], [0]]
    last = len(orders[0]) - 1
    for step in range(last, -1, -1):
        bits = [1 << order[step] for order in orders]
        came = [to_mp(held[h], bits[h]) for h in range(2)]
        came_members = [[km ^ bits[h] for km in members[h]] for h in range(2)]
        if step == 0:
            return [held[0], held[1], came[0], came[1]], [
                (0, members[0]), (1, members[1]), (0, came_members[0]), (1, came_members[1])
            ]
        count = len(members[0])
        held = in_vmem(
            grow_kernel,
            [((2 * count, nz, rows, RANK), F32)] * 2,
            [held[0], came[0], held[1], came[1]],
            "grow",
            after=beside(held[0]),
        )
        members = [members[h] + came_members[h] for h in range(2)]


def merged_kernel(part, in_hbm, after_ref, a_ref, e_ref, g_ref, out_ref, done_ref, a_t, *scratch):
    done_ref[...] = jnp.zeros_like(done_ref)
    rows, cols = out_ref.shape
    tile, chunk = rows // 2, min(cols, 512)
    held, sems = scratch if in_hbm else (out_ref, None)
    copies = []
    for i in range(2):
        at = pl.ds(i * tile, tile)
        a_t[at, :] = a_ref[:, pl.ds(part * rows + i * tile, tile)].T
        for j in range(cols // chunk):
            here = pl.ds(j * chunk, chunk)
            e_tile = e_ref[pl.ds(part * rows + i * tile, tile), here]
            held[at, here] = dot(a_t[at, :], g_ref[:, here]) + e_tile.astype(F32)
            if in_hbm:
                copy = pltpu.make_async_copy(held.at[at, here], out_ref.at[at, here], sems.at[len(copies)])
                copy.start()
                copies.append(copy)
    for copy in copies:
        copy.wait()


def merged_part(a, e, g, part, in_hbm, after):
    tok, half = a.shape
    cols = e.shape[1]
    rows = half // 4
    place = pltpu.HBM if in_hbm else pltpu.VMEM
    scratch = [pltpu.VMEM((rows, tok), BF16)]
    if in_hbm:
        scratch += [pltpu.VMEM((rows, cols), F32), pltpu.SemaphoreType.DMA((2 * (cols // min(cols, 512)),))]
    return pl.pallas_call(
        functools.partial(merged_kernel, part, in_hbm),
        in_specs=[pl.BlockSpec(memory_space=pl.ANY)] + [pl.BlockSpec(memory_space=pltpu.VMEM)] * 3,
        out_specs=[pl.BlockSpec(memory_space=place), pl.BlockSpec(memory_space=pltpu.VMEM)],
        out_shape=[place((rows, cols), F32), jax.ShapeDtypeStruct((8, RANK), F32)],
        scratch_shapes=scratch,
        compiler_params=params(MERGED_LIMIT if in_hbm else MERGED_LIMIT // 2),
        cost_estimate=cost(2 * tok * cols * rows, rows * cols * 2),
        name="merged",
    )(after, a, e, g)


def q_kernel(owners, nm, nz, last, ids_ref, after_ref, *refs):
    pieces, refs = refs[:4], refs[4:]
    if last:
        v_in, q_in, gram_in, a_ref, e_ref, g_ref, send_ref, keep_ref, gram_ref, p_half, pcat, q_acc = refs
    else:
        a_ref, e_ref, v_ref, q_acc, gram_ref, p_half, pcat = refs
    rows = pieces[0].shape[2]
    cols = e_ref.shape[1]
    chunk = min(cols, 512)
    for piece, (half, members) in zip(pieces, owners):
        for i, km in enumerate(members):
            for k in range(nz):
                start = ((ids_ref[1] ^ km) * nz + (ids_ref[2] ^ k)) * (2 * rows) + half * rows
                p_half[pl.ds(pl.multiple_of(start, rows), rows), :] = piece[i, k]
    pcat[...] = split_rows(p_half[...].T)
    v = fold(dot(pcat[...], a_ref[...], ROWS_BY_ROWS))
    gram = dot(pcat[...], pcat[...], ROWS_BY_ROWS)
    if last:
        vcat = split_rows(v + v_in[...])
        whole = fold(gram + gram_in[...])
        gram_ref[...] = whole[:, :RANK] + whole[:, RANK:]
    else:
        v_ref[...] = v
        gram_ref[...] = gram

    for i in range(cols // chunk):
        here = pl.ds(i * chunk, chunk)
        q = dot(pcat[...], e_ref[:, here])
        if last:
            q += dot(vcat, g_ref[:, here])
            q_acc[:, here] = fold(q) + q_in[:, here]
        else:
            q_acc[:, here] = fold(q)

    if last:
        small = send_ref.shape[1]
        for out, flip in ((send_ref, 1), (keep_ref, 0)):
            for k in range(nz):
                start = ((ids_ref[0] ^ flip) * nz + (ids_ref[2] ^ k)) * small
                out[k] = q_acc[pl.ds(pl.multiple_of(start, small), small), :]


def right_terms(ids, pieces, owners, a, e, g, nm, after, before=None):
    tok, half = a.shape
    cols = e.shape[1]
    nz = pieces[0].shape[1]
    last = before is not None
    vmem = pl.BlockSpec(memory_space=pltpu.VMEM)
    sums = [(RANK, tok), (RANK, cols), (2 * RANK, 2 * RANK)]
    scratch = [pltpu.VMEM((half, RANK), F32), pltpu.VMEM((2 * RANK, half), BF16)]
    if last:
        args = [*pieces, *before, a, e, g]
        outs = [(nz, RANK // (2 * nz), cols)] * 2 + [(RANK, RANK)]
        scratch += [pltpu.VMEM((RANK, cols), F32)]
    else:
        args = [*pieces, a, e]
        outs = sums
    return pl.pallas_call(
        functools.partial(q_kernel, owners, nm, nz, last),
        grid_spec=pltpu.PrefetchScalarGridSpec(
            num_scalar_prefetch=1,
            grid=(),
            in_specs=[pl.BlockSpec(memory_space=pl.ANY)] + [vmem] * len(args),
            out_specs=[vmem] * 3,
            scratch_shapes=scratch,
        ),
        out_shape=[jax.ShapeDtypeStruct(shape, F32) for shape in outs],
        compiler_params=params(RIGHT_LIMIT),
        cost_estimate=cost(4 * half * RANK * (tok + cols), half * (tok + cols)),
        name="right_terms",
    )(ids, after, *args)


def chol_inverse_kernel(gram_ref, out_ref):
    left = gram_ref[...]
    row = lax.broadcasted_iota(jnp.int32, (RANK, RANK), 0)
    right = (row == lax.broadcasted_iota(jnp.int32, (RANK, RANK), 1)).astype(F32)
    for j in range(0, RANK, 2):
        at = j % 8
        if j and at == 0:
            left, right = left[8:], right[8:]
        column = jnp.broadcast_to(left[:, j : j + 1], left.shape)
        column2 = jnp.broadcast_to(left[:, j + 1 : j + 2], left.shape)
        first, own = left[at : at + 1], right[at : at + 1]
        pivot, cross = column[at : at + 1], column2[at : at + 1]
        inverse = 1.0 / pivot
        ratio = column[at + 1 : at + 2] * inverse
        second = left[at + 1 : at + 2] - ratio * first
        other = right[at + 1 : at + 2] - ratio * own
        pivot2 = column2[at + 1 : at + 2] - ratio * cross
        inverse2 = 1.0 / pivot2
        out_ref[j : j + 1, :] = own * (1.0 / jnp.sqrt(pivot))
        out_ref[j + 1 : j + 2, :] = other * (1.0 / jnp.sqrt(pivot2))
        column2 = column2 - column * (cross * inverse)
        below = row[: left.shape[0]] > at + 1
        column = jnp.where(below, column, 0.0)
        column2 = jnp.where(below, column2, 0.0)
        left = left - column * (first * inverse) - column2 * (second * inverse2)
        right = right - column * (own * inverse) - column2 * (other * inverse2)


def p_hat_kernel(owners, nm, nz, skip, ids_ref, q_ref, *refs):
    pieces, (inv_ref, out_ref, q_again, p_all) = refs[skip : skip + 8], refs[skip + 8 :]
    q_again[...] = q_ref[...]
    rows = pieces[0].shape[2]
    for h in range(2):
        for piece, (half, members) in zip(pieces[4 * h : 4 * h + 4], owners):
            for i, km in enumerate(members):
                for k in range(nz):
                    block = (h * nm + (ids_ref[1] ^ km)) * nz + (ids_ref[2] ^ k)
                    start = block * (2 * rows) + half * rows
                    p_all[pl.ds(pl.multiple_of(start, rows), rows), :] = piece[i, k]
    inv_hi = inv_ref[...].T.astype(BF16)
    inv_lo = (inv_ref[...].T - inv_hi.astype(F32)).astype(BF16)
    inv = jnp.concatenate([inv_hi, inv_hi, inv_lo, inv_lo], axis=0)
    tile = p_all.shape[0] // 8

    @pl.loop(0, 8)
    def _(i):
        at = pl.ds(pl.multiple_of(i * tile, tile), tile)
        x = p_all[at, :]
        hi = x.astype(BF16)
        lo = (x - hi.astype(F32)).astype(BF16)
        y = dot(jnp.concatenate([hi, lo, hi, lo], axis=1), inv)
        y_hi = y.astype(BF16)
        y_lo = (y - y_hi.astype(F32)).astype(BF16)
        out_ref[at, :] = jnp.concatenate([y_hi, y_lo], axis=1)


def left_factor(ids, pieces, owners, inv, rows, nm, nz, q_own, after):
    return pl.pallas_call(
        functools.partial(p_hat_kernel, owners, nm, nz, len(after)),
        grid_spec=pltpu.PrefetchScalarGridSpec(
            num_scalar_prefetch=1,
            grid=(),
            in_specs=[pl.BlockSpec(memory_space=pltpu.VMEM)] * (10 + len(after)),
            out_specs=[pl.BlockSpec(memory_space=pltpu.VMEM)] * 2,
            scratch_shapes=[pltpu.VMEM((rows, RANK), F32)],
        ),
        out_shape=[jax.ShapeDtypeStruct((rows, 2 * RANK), BF16), jax.ShapeDtypeStruct(q_own.shape, F32)],
        compiler_params=params(SMALL_LIMIT),
        cost_estimate=cost(8 * rows * RANK * RANK, rows * RANK * 8),
        name="left_factor",
    )(ids, q_own, *after, *pieces, inv)


def final_kernel(nz, scale, ids_ref, *refs):
    pieces, refs = refs[: 2 * nz], refs[2 * nz :]
    inv_ref, phat_ref, parts = refs[0], refs[1], refs[2:10]
    err_ref, qnew_hbm, q_sum, q_cat, qnew_ref, sem, held, sems = refs[10:]
    small = pieces[0].shape[0]
    for h in range(2):
        for k in range(nz):
            block = (ids_ref[0] ^ h) * nz + (ids_ref[2] ^ k)
            q_sum[pl.ds(pl.multiple_of(block * small, small), small), :] = pieces[h * nz + k][...]
    q_t = scale * lax.dot_general(
        inv_ref[...], q_sum[...], (((1,), (0,)), ((), ())), precision=HIGHEST, preferred_element_type=F32
    )
    hi = q_t.astype(BF16)
    lo = (q_t - hi.astype(F32)).astype(BF16)
    q_cat[...] = jnp.concatenate([hi, hi, lo, lo], axis=0)
    part_rows, cols = parts[0].shape
    chunk = min(cols, 512)
    tile = part_rows // 2
    slots = held.shape[0]
    copies = []
    for number, merged in enumerate(parts):
        for i in range(2):
            at = pl.ds(i * tile, tile)
            slot = len(copies) % slots
            if len(copies) >= slots:
                copies[-slots].wait()
            x = phat_ref[pl.ds(number * part_rows + i * tile, tile), :]
            x = jnp.concatenate([x, x], axis=1)
            for j in range(cols // chunk):
                here = pl.ds(j * chunk, chunk)
                held[slot, :, here] = (merged[at, here] - dot(x, q_cat[:, here])).astype(BF16)
            row = pl.multiple_of((number ^ (ids_ref[0] * 4)) * part_rows + i * tile, tile)
            copies.append(
                pltpu.make_async_copy(held.at[slot], err_ref.at[0, pl.ds(row, tile), :], sems.at[slot])
            )
            copies[-1].start()
        if number == 0:
            qnew_ref[...] = q_t.T
            copy = pltpu.make_async_copy(qnew_ref, qnew_hbm, sem)
            copy.start()
    for last in copies[-slots:]:
        last.wait()
    copy.wait()


def finish(ids, pieces, inv, phat, parts, replicas):
    nz = len(pieces) // 2
    part_rows, cols = parts[0].shape
    rows = part_rows * len(parts)
    vmem = pl.BlockSpec(memory_space=pltpu.VMEM)
    hbm = pl.BlockSpec(memory_space=pltpu.HBM)
    return pl.pallas_call(
        functools.partial(final_kernel, nz, 1.0 / replicas),
        grid_spec=pltpu.PrefetchScalarGridSpec(
            num_scalar_prefetch=1,
            grid=(),
            in_specs=[vmem] * (2 * nz + 2 + len(parts)),
            out_specs=[hbm, hbm],
            scratch_shapes=[
                pltpu.VMEM((RANK, cols), F32),
                pltpu.VMEM((4 * RANK, cols), BF16),
                pltpu.VMEM((cols, RANK), F32),
                pltpu.SemaphoreType.DMA,
                pltpu.VMEM((4, part_rows // 2, cols), BF16),
                pltpu.SemaphoreType.DMA((4,)),
            ],
        ),
        out_shape=[jax.ShapeDtypeStruct((1, rows, cols), BF16), jax.ShapeDtypeStruct((cols, RANK), F32)],
        compiler_params=params(FINAL_LIMIT),
        cost_estimate=cost(8 * rows * cols * RANK, rows * cols * 6),
        name="new_error",
    )(ids, *pieces, inv, phat, *parts)


def q_sum_kernel(nz, *refs):
    keep, came, outs = refs[0], refs[1], refs[2:]
    for k in range(nz):
        outs[k][...] = keep[k] + came[k]


def per_device(n_dp, n_mp, activations, out_grads, error_fb, q_prev):
    a, g, e, q = [
        pltpu.with_memory_space_constraint(x, pltpu.HBM) for x in (activations[0], out_grads[0], error_fb[0], q_prev)
    ]
    rows = a.shape[1]
    nz = n_dp // 2
    dp, mp = lax.axis_index("dp"), lax.axis_index("mp")
    ids = jnp.stack([dp % 2, mp, dp // 2]).astype(jnp.int32)
    bits = list(range(n_mp.bit_length() - 1))
    orders = [bits, bits[::-1]]

    def to_core(x):
        return lax.ppermute(x, "dp", [(i, i ^ 1) for i in range(n_dp)])

    def to_z(x, k):
        return lax.ppermute(x, "dp", [(i, i ^ (2 * k)) for i in range(n_dp)])

    def to_mp(x, k):
        return lax.ppermute(x, "mp", [(i, i ^ k) for i in range(n_mp)])

    p_far, a_far, e_far, g_here, ucat, qcat = left_terms(ids, q, g, a, e, n_mp, nz)
    p_arrived = to_core(p_far)
    p_near, a_near, e_near = left_terms(ids, q, g, a, e, n_mp, nz, (ucat, qcat))
    parts = []

    def beside(sent, count=1):
        done = []
        while count and len(parts) < 6:
            number = len(parts)
            mine = (a_near, e_near) if number < 4 else (a_far, e_far)
            part, sent = merged_part(*mine, g_here, number % 4, True, sent)
            parts.append(part)
            done = [sent]
            count -= 1
        return done

    by_z = scatter_over_mp(p_near, p_arrived, to_mp, orders, beside)
    done = beside(by_z[0])
    came = [to_z(by_z[k], k) for k in range(1, nz)]
    [p_own] = in_vmem(own_sum_kernel, [(by_z[0].shape, F32)], [by_z[0], *came], "p_own", after=done)
    done = beside(p_own)
    p_pieces = [p_own] + [to_z(p_own, k) for k in range(1, nz)]
    near, owners = gather_over_mp(p_pieces, to_mp, orders, beside, done)
    done = (beside(near[0], 8) or [near[0]])[0]
    far = [to_core(x) for x in near]

    half = right_terms(ids, near, owners, a_near, e_near, g_here, n_mp, done)
    q_send, q_keep, gram = right_terms(ids, far, owners, a_far, e_far, g_here, n_mp, done, half)

    piece = (q_keep.shape[1:], F32)
    q_by_z = in_vmem(functools.partial(q_sum_kernel, nz), [piece] * nz, [q_keep, to_core(q_send)], "q_sum")
    square = ((RANK, RANK), F32)
    [inv] = in_vmem(
        chol_inverse_kernel, [square], [gram], "chol_inverse", after=[q_by_z[0]], work=cost(2 * 10**10, 10**5)
    )
    came = [to_z(q_by_z[k], k) for k in range(1, nz)]
    part, done = merged_part(a_far, e_far, g_here, 2, True, inv)
    parts.append(part)
    [q_own] = in_vmem(own_sum_kernel, [piece], [q_by_z[0], *came], "q_own", after=[done])
    part, done = merged_part(a_far, e_far, g_here, 3, False, q_own)
    parts.append(part)
    phat, q_again = left_factor(ids, near + far, owners, inv, rows, n_mp, nz, q_own, [done, parts[6]])
    q_near = [q_own] + [to_z(q_own, k) for k in range(1, nz)]
    q_pieces = q_near + [to_core(x) for x in [q_again] + q_near[1:]]

    new_error, q_new = finish(ids, q_pieces, inv, phat, parts, n_dp)
    return new_error, q_new


def solution(mesh):
    placed = (P("dp", None, None), P("dp", None, "mp"), P("dp", None, "mp"), P("mp", None))
    return jax.shard_map(
        functools.partial(per_device, mesh.shape["dp"], mesh.shape["mp"]),
        mesh=mesh,
        in_specs=placed,
        out_specs=(P("dp", None, "mp"), P("mp", None)),
        check_vma=False,
    )
```

```python
import functools

import jax
import jax.numpy as jnp
from jax import lax
from jax.experimental import pallas as pl
from jax.experimental.pallas import tpu as pltpu
from jax.sharding import PartitionSpec as P

F32 = jnp.float32
BF16 = jnp.bfloat16
HIGHEST = lax.Precision.HIGHEST
RANK = 128
VMEM_LIMIT = 50 * 1024 * 1024
LEFT_LIMIT = 14 * 1024 * 1024
SMALL_LIMIT = 6 * 1024 * 1024
MERGED_LIMIT = 8 * 1024 * 1024
RIGHT_LIMIT = 11 * 1024 * 1024
FINAL_LIMIT = 9 * 1024 * 1024


def params(limit=VMEM_LIMIT):
    return pltpu.CompilerParams(vmem_limit_bytes=limit)


def cost(flops, nbytes):
    return pl.CostEstimate(flops=flops, bytes_accessed=nbytes, transcendentals=0)


def split_rows(x):
    hi = x.astype(BF16)
    lo = (x - hi.astype(F32)).astype(BF16)
    return jnp.concatenate([hi, lo], axis=0)


def fold(y):
    return y[:RANK] + y[RANK:]


def dot(a, b, contract=((1,), (0,))):
    return lax.dot_general(a, b, (contract, ((), ())), preferred_element_type=F32)


ROWS_BY_ROWS = ((1,), (1,))


def skipping(count, body, *refs):
    body(*refs[count:])


def in_vmem(body, outs, args, name, limit=SMALL_LIMIT, work=None, after=()):
    args = [*after, *args]
    return pl.pallas_call(
        functools.partial(skipping, len(after), body),
        in_specs=[pl.BlockSpec(memory_space=pltpu.VMEM)] * len(args),
        out_specs=[pl.BlockSpec(memory_space=pltpu.VMEM)] * len(outs),
        out_shape=[jax.ShapeDtypeStruct(*out) for out in outs],
        compiler_params=params(limit),
        cost_estimate=work,
        name=name,
    )(*args)


STEPS = 4
AHEAD = 2


def copies_of_half(a_hbm, e_hbm, a_ref, e_ref, sems, half):
    rows = e_ref.shape[0]
    tile = rows // STEPS
    copies = []
    for i in range(STEPS):
        here = pl.ds(i * tile, tile)
        there = pl.ds(pl.multiple_of(half * rows + i * tile, tile), tile)
        copies.append(
            (
                pltpu.make_async_copy(e_hbm.at[there, :], e_ref.at[here, :], sems.at[2 * i]),
                pltpu.make_async_copy(a_hbm.at[:, there], a_ref.at[:, here], sems.at[2 * i + 1]),
            )
        )
    return copies


def start(pair):
    for copy in pair:
        copy.start()


def p_of_half(ids_ref, copies, a_ref, e_ref, ucat_ref, qcat_ref, p_ref):
    nz, small = p_ref.shape[1:3]
    tile = e_ref.shape[0] // STEPS
    for i, (e_copy, a_copy) in enumerate(copies):
        here = pl.ds(i * tile, tile)
        e_copy.wait()
        a_copy.wait()
        if i + AHEAD < STEPS:
            start(copies[i + AHEAD])
        acc = dot(qcat_ref[...], e_ref[here, :], ROWS_BY_ROWS) + dot(ucat_ref[...], a_ref[:, here])
        p_tile = fold(acc).T
        for k in range(tile // small):
            block = i * (tile // small) + k
            p_ref[(block // nz) ^ ids_ref[1], (block % nz) ^ ids_ref[2]] = p_tile[k * small : (k + 1) * small]


def far_kernel(
    ids_ref, q_hbm, g_hbm, a_hbm, e_hbm, p_ref, a_ref, e_ref, g_ref, ucat_ref, qcat_ref, q_ref, sems, first_sems
):
    tok = g_ref.shape[0]
    q_copy = pltpu.make_async_copy(q_hbm, q_ref, first_sems.at[0])
    q_copy.start()
    g_copies = []
    for i in range(2):
        at = pl.ds(i * (tok // 2), tok // 2)
        g_copies.append(pltpu.make_async_copy(g_hbm.at[at, :], g_ref.at[at, :], first_sems.at[1 + i]))
        g_copies[-1].start()
    copies = copies_of_half(a_hbm, e_hbm, a_ref, e_ref, sems, ids_ref[0] ^ 1)
    q_copy.wait()
    start(copies[0])
    qcat_ref[...] = split_rows(q_ref[...].T)
    for i in range(2):
        at = pl.ds(i * (tok // 2), tok // 2)
        g_copies[i].wait()
        if i == 0:
            start(copies[1])
        ucat_ref[:, at] = split_rows(fold(dot(qcat_ref[...], g_ref[at, :], ROWS_BY_ROWS)))
    p_of_half(ids_ref, copies, a_ref, e_ref, ucat_ref, qcat_ref, p_ref)


def near_kernel(ids_ref, ucat_ref, qcat_ref, a_hbm, e_hbm, p_ref, a_ref, e_ref, sems):
    copies = copies_of_half(a_hbm, e_hbm, a_ref, e_ref, sems, ids_ref[0])
    for pair in copies[:AHEAD]:
        start(pair)
    p_of_half(ids_ref, copies, a_ref, e_ref, ucat_ref, qcat_ref, p_ref)


def left_terms(ids, q, g, a, e, nm, nz, before=None):
    tok, rows = a.shape
    cols = e.shape[1]
    vmem = pl.BlockSpec(memory_space=pltpu.VMEM)
    hbm = pl.BlockSpec(memory_space=pltpu.HBM)
    outs = [
        pltpu.VMEM((nm, nz, rows // (2 * nm * nz), RANK), F32),
        pltpu.VMEM((tok, rows // 2), BF16),
        pltpu.VMEM((rows // 2, cols), BF16),
    ]
    scratch = [pltpu.SemaphoreType.DMA((2 * STEPS,))]
    if before is None:
        body, specs, args = far_kernel, [hbm] * 4, (q, g, a, e)
        outs += [
            pltpu.VMEM((tok, cols), BF16),
            pltpu.VMEM((2 * RANK, tok), BF16),
            pltpu.VMEM((2 * RANK, cols), BF16),
        ]
        scratch = [pltpu.VMEM((cols, RANK), F32)] + scratch + [pltpu.SemaphoreType.DMA((3,))]
    else:
        body, specs, args = near_kernel, [vmem] * 2 + [hbm] * 2, (*before, a, e)
    return pl.pallas_call(
        body,
        grid_spec=pltpu.PrefetchScalarGridSpec(
            num_scalar_prefetch=1,
            grid=(),
            in_specs=specs,
            out_specs=[vmem] * len(outs),
            scratch_shapes=scratch,
        ),
        out_shape=outs,
        compiler_params=params(LEFT_LIMIT),
        cost_estimate=cost(2 * rows * RANK * (tok + cols), rows * (tok + cols)),
        name="left_terms",
    )(ids, *args)


def first_sum_kernel(keeps, sends, near_ref, far_ref, *outs):
    rows = near_ref.shape[2] // 2
    for half in range(2):
        for out, members in ((outs[2 * half], sends[half]), (outs[2 * half + 1], keeps[half])):
            for i, km in enumerate(members):
                at = (km, slice(None), pl.ds(half * rows, rows))
                out[i] = near_ref[at] + far_ref[at]


def next_sum_kernel(keeps, sends, *refs):
    ins, outs = refs[:4], refs[4:]
    for half in range(2):
        kept, came = ins[2 * half : 2 * half + 2]
        for out, places in ((outs[2 * half], sends[half]), (outs[2 * half + 1], keeps[half])):
            for i, at in enumerate(places):
                out[i] = kept[at] + came[at]


def last_sum_kernel(nz, *refs):
    ins, outs = refs[:4], refs[4:]
    rows = ins[0].shape[2]
    for k in range(nz):
        for half in range(2):
            outs[k][pl.ds(half * rows, rows), :] = ins[2 * half][0, k] + ins[2 * half + 1][0, k]


def scatter_over_mp(near, far, to_mp, orders, beside):
    nm, nz, block, _ = near.shape
    rows = block // 2
    members = [list(range(nm))] * 2
    values, done = None, ()
    for step in range(len(orders[0])):
        bits = [1 << order[step] for order in orders]
        keep_lists = [[km for km in members[h] if not km & bits[h]] for h in range(2)]
        send_lists = [[km | bits[h] for km in keep_lists[h]] for h in range(2)]
        count = len(keep_lists[0])
        outs = [((count, nz, rows, RANK), F32)] * 4
        if values is None:
            parts = in_vmem(functools.partial(first_sum_kernel, keep_lists, send_lists), outs, [near, far], "first_sum")
        else:
            keep_at = [[members[h].index(km) for km in keep_lists[h]] for h in range(2)]
            send_at = [[members[h].index(km) for km in send_lists[h]] for h in range(2)]
            parts = in_vmem(functools.partial(next_sum_kernel, keep_at, send_at), outs, values, "next_sum", after=done)
        members = keep_lists
        came = [to_mp(parts[0], bits[0]), to_mp(parts[2], bits[1])]
        done = beside(parts[1])
        values = [parts[1], came[0], parts[3], came[1]]
    return in_vmem(functools.partial(last_sum_kernel, nz), [((block, RANK), F32)] * nz, values, "last_sum", after=done)


def own_sum_kernel(*refs):
    ins, out = refs[:-1], refs[-1]
    total = ins[0][...]
    for came in ins[1:]:
        total = total + came[...]
    out[...] = total


def own_kernel(nz, *refs):
    ins, outs = refs[:nz], refs[nz:]
    rows = outs[0].shape[2]
    for k in range(nz):
        for half in range(2):
            outs[half][0, k] = ins[k][pl.ds(half * rows, rows), :]


def grow_kernel(*refs):
    ins, outs = refs[:4], refs[4:]
    count = ins[0].shape[0]
    for half in range(2):
        outs[half][pl.ds(0, count)] = ins[2 * half][...]
        outs[half][pl.ds(count, count)] = ins[2 * half + 1][...]


def gather_over_mp(pieces, to_mp, orders, beside, done):
    nz = len(pieces)
    rows = pieces[0].shape[0] // 2
    held = in_vmem(functools.partial(own_kernel, nz), [((1, nz, rows, RANK), F32)] * 2, pieces, "own_rows", after=done)
    members = [[0], [0]]
    last = len(orders[0]) - 1
    for step in range(last, -1, -1):
        bits = [1 << order[step] for order in orders]
        came = [to_mp(held[h], bits[h]) for h in range(2)]
        came_members = [[km ^ bits[h] for km in members[h]] for h in range(2)]
        if step == 0:
            return [held[0], held[1], came[0], came[1]], [
                (0, members[0]), (1, members[1]), (0, came_members[0]), (1, came_members[1])
            ]
        count = len(members[0])
        held = in_vmem(
            grow_kernel,
            [((2 * count, nz, rows, RANK), F32)] * 2,
            [held[0], came[0], held[1], came[1]],
            "grow",
            after=beside(held[0]),
        )
        members = [members[h] + came_members[h] for h in range(2)]


def merged_kernel(part, in_hbm, after_ref, a_ref, e_ref, g_ref, out_ref, done_ref, a_t, *scratch):
    done_ref[...] = jnp.zeros_like(done_ref)
    rows, cols = out_ref.shape
    tile, chunk = rows // 2, min(cols, 512)
    held, sems = scratch if in_hbm else (out_ref, None)
    copies = []
    for i in range(2):
        at = pl.ds(i * tile, tile)
        a_t[at, :] = a_ref[:, pl.ds(part * rows + i * tile, tile)].T
        for j in range(cols // chunk):
            here = pl.ds(j * chunk, chunk)
            e_tile = e_ref[pl.ds(part * rows + i * tile, tile), here]
            held[at, here] = dot(a_t[at, :], g_ref[:, here]) + e_tile.astype(F32)
            if in_hbm:
                copy = pltpu.make_async_copy(held.at[at, here], out_ref.at[at, here], sems.at[len(copies)])
                copy.start()
                copies.append(copy)
    for copy in copies:
        copy.wait()


def merged_part(a, e, g, part, in_hbm, after):
    tok, half = a.shape
    cols = e.shape[1]
    rows = half // 4
    place = pltpu.HBM if in_hbm else pltpu.VMEM
    scratch = [pltpu.VMEM((rows, tok), BF16)]
    if in_hbm:
        scratch += [pltpu.VMEM((rows, cols), F32), pltpu.SemaphoreType.DMA((2 * (cols // min(cols, 512)),))]
    return pl.pallas_call(
        functools.partial(merged_kernel, part, in_hbm),
        in_specs=[pl.BlockSpec(memory_space=pl.ANY)] + [pl.BlockSpec(memory_space=pltpu.VMEM)] * 3,
        out_specs=[pl.BlockSpec(memory_space=place), pl.BlockSpec(memory_space=pltpu.VMEM)],
        out_shape=[place((rows, cols), F32), jax.ShapeDtypeStruct((8, RANK), F32)],
        scratch_shapes=scratch,
        compiler_params=params(MERGED_LIMIT if in_hbm else MERGED_LIMIT // 2),
        cost_estimate=cost(2 * tok * cols * rows, rows * cols * 2),
        name="merged",
    )(after, a, e, g)


def q_kernel(owners, nm, nz, last, ids_ref, after_ref, *refs):
    pieces, refs = refs[:4], refs[4:]
    if last:
        v_in, q_in, gram_in, a_ref, e_ref, g_ref, send_ref, keep_ref, gram_ref, p_half, pcat, q_acc = refs
    else:
        a_ref, e_ref, v_ref, q_acc, gram_ref, p_half, pcat = refs
    rows = pieces[0].shape[2]
    cols = e_ref.shape[1]
    chunk = min(cols, 512)
    for piece, (half, members) in zip(pieces, owners):
        for i, km in enumerate(members):
            for k in range(nz):
                start = ((ids_ref[1] ^ km) * nz + (ids_ref[2] ^ k)) * (2 * rows) + half * rows
                p_half[pl.ds(pl.multiple_of(start, rows), rows), :] = piece[i, k]
    pcat[...] = split_rows(p_half[...].T)
    v = fold(dot(pcat[...], a_ref[...], ROWS_BY_ROWS))
    gram = dot(pcat[...], pcat[...], ROWS_BY_ROWS)
    if last:
        vcat = split_rows(v + v_in[...])
        whole = fold(gram + gram_in[...])
        gram_ref[...] = whole[:, :RANK] + whole[:, RANK:]
    else:
        v_ref[...] = v
        gram_ref[...] = gram

    for i in range(cols // chunk):
        here = pl.ds(i * chunk, chunk)
        q = dot(pcat[...], e_ref[:, here])
        if last:
            q += dot(vcat, g_ref[:, here])
            q_acc[:, here] = fold(q) + q_in[:, here]
        else:
            q_acc[:, here] = fold(q)

    if last:
        small = send_ref.shape[1]
        for out, flip in ((send_ref, 1), (keep_ref, 0)):
            for k in range(nz):
                start = ((ids_ref[0] ^ flip) * nz + (ids_ref[2] ^ k)) * small
                out[k] = q_acc[pl.ds(pl.multiple_of(start, small), small), :]


def right_terms(ids, pieces, owners, a, e, g, nm, after, before=None):
    tok, half = a.shape
    cols = e.shape[1]
    nz = pieces[0].shape[1]
    last = before is not None
    vmem = pl.BlockSpec(memory_space=pltpu.VMEM)
    sums = [(RANK, tok), (RANK, cols), (2 * RANK, 2 * RANK)]
    scratch = [pltpu.VMEM((half, RANK), F32), pltpu.VMEM((2 * RANK, half), BF16)]
    if last:
        args = [*pieces, *before, a, e, g]
        outs = [(nz, RANK // (2 * nz), cols)] * 2 + [(RANK, RANK)]
        scratch += [pltpu.VMEM((RANK, cols), F32)]
    else:
        args = [*pieces, a, e]
        outs = sums
    return pl.pallas_call(
        functools.partial(q_kernel, owners, nm, nz, last),
        grid_spec=pltpu.PrefetchScalarGridSpec(
            num_scalar_prefetch=1,
            grid=(),
            in_specs=[pl.BlockSpec(memory_space=pl.ANY)] + [vmem] * len(args),
            out_specs=[vmem] * 3,
            scratch_shapes=scratch,
        ),
        out_shape=[jax.ShapeDtypeStruct(shape, F32) for shape in outs],
        compiler_params=params(RIGHT_LIMIT),
        cost_estimate=cost(4 * half * RANK * (tok + cols), half * (tok + cols)),
        name="right_terms",
    )(ids, after, *args)


def chol_inverse_kernel(gram_ref, out_ref):
    left = gram_ref[...]
    row = lax.broadcasted_iota(jnp.int32, (RANK, RANK), 0)
    right = (row == lax.broadcasted_iota(jnp.int32, (RANK, RANK), 1)).astype(F32)
    for j in range(0, RANK, 2):
        at = j % 8
        if j and at == 0:
            left, right = left[8:], right[8:]
        column = jnp.broadcast_to(left[:, j : j + 1], left.shape)
        column2 = jnp.broadcast_to(left[:, j + 1 : j + 2], left.shape)
        first, own = left[at : at + 1], right[at : at + 1]
        pivot, cross = column[at : at + 1], column2[at : at + 1]
        inverse = 1.0 / pivot
        ratio = column[at + 1 : at + 2] * inverse
        second = left[at + 1 : at + 2] - ratio * first
        other = right[at + 1 : at + 2] - ratio * own
        pivot2 = column2[at + 1 : at + 2] - ratio * cross
        inverse2 = 1.0 / pivot2
        out_ref[j : j + 1, :] = own * (1.0 / jnp.sqrt(pivot))
        out_ref[j + 1 : j + 2, :] = other * (1.0 / jnp.sqrt(pivot2))
        column2 = column2 - column * (cross * inverse)
        below = row[: left.shape[0]] > at + 1
        column = jnp.where(below, column, 0.0)
        column2 = jnp.where(below, column2, 0.0)
        left = left - column * (first * inverse) - column2 * (second * inverse2)
        right = right - column * (own * inverse) - column2 * (other * inverse2)


def p_hat_kernel(owners, nm, nz, skip, ids_ref, q_ref, *refs):
    pieces, (inv_ref, out_ref, q_again, p_all) = refs[skip : skip + 8], refs[skip + 8 :]
    q_again[...] = q_ref[...]
    rows = pieces[0].shape[2]
    for h in range(2):
        for piece, (half, members) in zip(pieces[4 * h : 4 * h + 4], owners):
            for i, km in enumerate(members):
                for k in range(nz):
                    block = (h * nm + (ids_ref[1] ^ km)) * nz + (ids_ref[2] ^ k)
                    start = block * (2 * rows) + half * rows
                    p_all[pl.ds(pl.multiple_of(start, rows), rows), :] = piece[i, k]
    inv_hi = inv_ref[...].T.astype(BF16)
    inv_lo = (inv_ref[...].T - inv_hi.astype(F32)).astype(BF16)
    inv = jnp.concatenate([inv_hi, inv_hi, inv_lo, inv_lo], axis=0)
    tile = p_all.shape[0] // 8

    @pl.loop(0, 8)
    def _(i):
        at = pl.ds(pl.multiple_of(i * tile, tile), tile)
        x = p_all[at, :]
        hi = x.astype(BF16)
        lo = (x - hi.astype(F32)).astype(BF16)
        y = dot(jnp.concatenate([hi, lo, hi, lo], axis=1), inv)
        y_hi = y.astype(BF16)
        y_lo = (y - y_hi.astype(F32)).astype(BF16)
        out_ref[at, :] = jnp.concatenate([y_hi, y_lo], axis=1)


def left_factor(ids, pieces, owners, inv, rows, nm, nz, q_own, after):
    return pl.pallas_call(
        functools.partial(p_hat_kernel, owners, nm, nz, len(after)),
        grid_spec=pltpu.PrefetchScalarGridSpec(
            num_scalar_prefetch=1,
            grid=(),
            in_specs=[pl.BlockSpec(memory_space=pltpu.VMEM)] * (10 + len(after)),
            out_specs=[pl.BlockSpec(memory_space=pltpu.VMEM)] * 2,
            scratch_shapes=[pltpu.VMEM((rows, RANK), F32)],
        ),
        out_shape=[jax.ShapeDtypeStruct((rows, 2 * RANK), BF16), jax.ShapeDtypeStruct(q_own.shape, F32)],
        compiler_params=params(SMALL_LIMIT),
        cost_estimate=cost(8 * rows * RANK * RANK, rows * RANK * 8),
        name="left_factor",
    )(ids, q_own, *after, *pieces, inv)


def final_kernel(nz, scale, ids_ref, *refs):
    pieces, refs = refs[: 2 * nz], refs[2 * nz :]
    inv_ref, phat_ref, parts = refs[0], refs[1], refs[2:10]
    err_ref, qnew_hbm, q_sum, q_cat, qnew_ref, sem, held, sems = refs[10:]
    small = pieces[0].shape[0]
    for h in range(2):
        for k in range(nz):
            block = (ids_ref[0] ^ h) * nz + (ids_ref[2] ^ k)
            q_sum[pl.ds(pl.multiple_of(block * small, small), small), :] = pieces[h * nz + k][...]
    q_t = scale * lax.dot_general(
        inv_ref[...], q_sum[...], (((1,), (0,)), ((), ())), precision=HIGHEST, preferred_element_type=F32
    )
    hi = q_t.astype(BF16)
    lo = (q_t - hi.astype(F32)).astype(BF16)
    q_cat[...] = jnp.concatenate([hi, hi, lo, lo], axis=0)
    part_rows, cols = parts[0].shape
    chunk = min(cols, 512)
    tile = part_rows // 2
    slots = held.shape[0]
    copies = []
    for number, merged in enumerate(parts):
        for i in range(2):
            at = pl.ds(i * tile, tile)
            slot = len(copies) % slots
            if len(copies) >= slots:
                copies[-slots].wait()
            x = phat_ref[pl.ds(number * part_rows + i * tile, tile), :]
            x = jnp.concatenate([x, x], axis=1)
            for j in range(cols // chunk):
                here = pl.ds(j * chunk, chunk)
                held[slot, :, here] = (merged[at, here] - dot(x, q_cat[:, here])).astype(BF16)
            row = pl.multiple_of((number ^ (ids_ref[0] * 4)) * part_rows + i * tile, tile)
            copies.append(
                pltpu.make_async_copy(held.at[slot], err_ref.at[0, pl.ds(row, tile), :], sems.at[slot])
            )
            copies[-1].start()
        if number == 0:
            qnew_ref[...] = q_t.T
            copy = pltpu.make_async_copy(qnew_ref, qnew_hbm, sem)
            copy.start()
    for last in copies[-slots:]:
        last.wait()
    copy.wait()


def finish(ids, pieces, inv, phat, parts, replicas):
    nz = len(pieces) // 2
    part_rows, cols = parts[0].shape
    rows = part_rows * len(parts)
    vmem = pl.BlockSpec(memory_space=pltpu.VMEM)
    hbm = pl.BlockSpec(memory_space=pltpu.HBM)
    return pl.pallas_call(
        functools.partial(final_kernel, nz, 1.0 / replicas),
        grid_spec=pltpu.PrefetchScalarGridSpec(
            num_scalar_prefetch=1,
            grid=(),
            in_specs=[vmem] * (2 * nz + 2 + len(parts)),
            out_specs=[hbm, hbm],
            scratch_shapes=[
                pltpu.VMEM((RANK, cols), F32),
                pltpu.VMEM((4 * RANK, cols), BF16),
                pltpu.VMEM((cols, RANK), F32),
                pltpu.SemaphoreType.DMA,
                pltpu.VMEM((4, part_rows // 2, cols), BF16),
                pltpu.SemaphoreType.DMA((4,)),
            ],
        ),
        out_shape=[jax.ShapeDtypeStruct((1, rows, cols), BF16), jax.ShapeDtypeStruct((cols, RANK), F32)],
        compiler_params=params(FINAL_LIMIT),
        cost_estimate=cost(8 * rows * cols * RANK, rows * cols * 6),
        name="new_error",
    )(ids, *pieces, inv, phat, *parts)


def q_sum_kernel(nz, *refs):
    keep, came, outs = refs[0], refs[1], refs[2:]
    for k in range(nz):
        outs[k][...] = keep[k] + came[k]


def per_device(n_dp, n_mp, activations, out_grads, error_fb, q_prev):
    a, g, e, q = [
        pltpu.with_memory_space_constraint(x, pltpu.HBM) for x in (activations[0], out_grads[0], error_fb[0], q_prev)
    ]
    rows = a.shape[1]
    nz = n_dp // 2
    dp, mp = lax.axis_index("dp"), lax.axis_index("mp")
    ids = jnp.stack([dp % 2, mp, dp // 2]).astype(jnp.int32)
    bits = list(range(n_mp.bit_length() - 1))
    orders = [bits, bits[::-1]]

    def to_core(x):
        return lax.ppermute(x, "dp", [(i, i ^ 1) for i in range(n_dp)])

    def to_z(x, k):
        return lax.ppermute(x, "dp", [(i, i ^ (2 * k)) for i in range(n_dp)])

    def to_mp(x, k):
        return lax.ppermute(x, "mp", [(i, i ^ k) for i in range(n_mp)])

    p_far, a_far, e_far, g_here, ucat, qcat = left_terms(ids, q, g, a, e, n_mp, nz)
    p_arrived = to_core(p_far)
    p_near, a_near, e_near = left_terms(ids, q, g, a, e, n_mp, nz, (ucat, qcat))
    parts = []

    def beside(sent, count=1):
        done = []
        while count and len(parts) < 6:
            number = len(parts)
            mine = (a_near, e_near) if number < 4 else (a_far, e_far)
            part, sent = merged_part(*mine, g_here, number % 4, True, sent)
            parts.append(part)
            done = [sent]
            count -= 1
        return done

    by_z = scatter_over_mp(p_near, p_arrived, to_mp, orders, beside)
    done = beside(by_z[0])
    came = [to_z(by_z[k], k) for k in range(1, nz)]
    [p_own] = in_vmem(own_sum_kernel, [(by_z[0].shape, F32)], [by_z[0], *came], "p_own", after=done)
    done = beside(p_own)
    p_pieces = [p_own] + [to_z(p_own, k) for k in range(1, nz)]
    near, owners = gather_over_mp(p_pieces, to_mp, orders, beside, done)
    done = (beside(near[0], 8) or [near[0]])[0]
    far = [to_core(x) for x in near]

    half = right_terms(ids, near, owners, a_near, e_near, g_here, n_mp, done)
    q_send, q_keep, gram = right_terms(ids, far, owners, a_far, e_far, g_here, n_mp, done, half)

    piece = (q_keep.shape[1:], F32)
    q_by_z = in_vmem(functools.partial(q_sum_kernel, nz), [piece] * nz, [q_keep, to_core(q_send)], "q_sum")
    square = ((RANK, RANK), F32)
    [inv] = in_vmem(
        chol_inverse_kernel, [square], [gram], "chol_inverse", after=[q_by_z[0]], work=cost(2 * 10**10, 10**5)
    )
    came = [to_z(q_by_z[k], k) for k in range(1, nz)]
    part, done = merged_part(a_far, e_far, g_here, 2, True, inv)
    parts.append(part)
    [q_own] = in_vmem(own_sum_kernel, [piece], [q_by_z[0], *came], "q_own", after=[done])
    part, done = merged_part(a_far, e_far, g_here, 3, False, q_own)
    parts.append(part)
    phat, q_again = left_factor(ids, near + far, owners, inv, rows, n_mp, nz, q_own, [done, parts[6]])
    q_near = [q_own] + [to_z(q_own, k) for k in range(1, nz)]
    q_pieces = q_near + [to_core(x) for x in [q_again] + q_near[1:]]

    new_error, q_new = finish(ids, q_pieces, inv, phat, parts, n_dp)
    return new_error, q_new


def solution(mesh):
    placed = (P("dp", None, None), P("dp", None, "mp"), P("dp", None, "mp"), P("mp", None))
    return jax.shard_map(
        functools.partial(per_device, mesh.shape["dp"], mesh.shape["mp"]),
        mesh=mesh,
        in_specs=placed,
        out_specs=(P("dp", None, "mp"), P("mp", None)),
        check_vma=False,
    )
```
